512 devices in a mesh: batch: 16 (over z), hist: 32 (over y, x, core).
Axes of the slice: x: 4, y: 4, z: 16, core: 2. Of those that a mesh axis runs over, the one named last changes fastest.
Arguments:
- feats: bfloat16 [512, 128, 768], P(('batch', 'hist')), may hold values from -6 to 6
- history: bfloat16 [8192, 1536], P('hist'), may hold values from -6 to 6
- weight: bfloat16 [768, 768], replicated, may hold values from -0.21875 to 0.21875
- edge_coef: bfloat16 [512, 128, 256], P(('batch', 'hist')), may hold values from -0.375 to 0.375
- tile_map: int32 [512, 2], P(('batch', 'hist')), may hold values from 0 to 1, each once within a row
- nbr_owner: int32 [512, 256, 1], P(('batch', 'hist')), may hold values from 0 to 31; in each aligned block of 256 rows (0 to 255, 256 to 511, ..., all dimensions but the last counted through in order) at most 16 rows name the same one
- nbr_row: int32 [512, 256], P(('batch', 'hist')), may hold values from 0 to 383
- grad_out: bfloat16 [512, 128, 768], P(('batch', 'hist')), may hold values from -6 to 6
Outputs:
- out: bfloat16 [512, 128, 768], P(('batch', 'hist'))
- grad_feats: bfloat16 [512, 128, 768], P(('batch', 'hist'))
- grad_weight: float32 [768, 768], P('hist')
The draws below stay inside these ranges and needn't reach their ends.
Inputs may be any that keep to these rules, and one draw needn't show every extreme that they name: `nbr_owner`: in each group's 256 slots no hist index is named by more than 16 slots; some index is named exactly 16 times. `tile_map`: each group's row is a permutation of 0 to 1.
All inputs are finite; a program needn't handle non-finite values.
Results may differ from the reference program's by a relative error of at most 0.0055.
Values may be sent and summed in bfloat16 or wider, within the bound.
No kernel may reach another device: no remote copies, remote signals or barrier semaphores. Data moves between devices by JAX's collectives and lax.ppermute only.
A program may use at most 64 MiB of HBM per device.

```python
import math
import jax
import jax.numpy as jnp
import numpy as np
from jax import lax

D = 768
NODE_DEV = 128
HIST_DEV = 256
TILE = 128
TPB = 2
DST_BLK = 1
SLOT_BLK = 2
SLOTS = 256
CAP = 16
GROUPS = 512
HROWS = 8192
N_HIST = 32


def with_ends(entries, stream_key, least, largest):
    dims = entries.shape
    index_at = [jax.random.randint(jax.random.fold_in(stream_key, axis), (), 0, dims[axis]) for axis in range(len(dims))]
    entries = entries.at[tuple(index_at)].set(least)
    longest = dims.index(max(dims))
    index_at[longest] = (index_at[longest] + 1) % dims[longest]
    return entries.at[tuple(index_at)].set(largest)


def shard_levels(own_key, dims, shards, least, top_value):
    gain, own = 1.0, jax.random.fold_in(own_key, 6)
    for axis_at, blocks in shards:
        heights = jnp.exp(jax.random.uniform(jax.random.fold_in(own, axis_at), (blocks,), jnp.float32, least / len(shards), top_value / len(shards)))
        gain = gain * jnp.repeat(heights, dims[axis_at] // blocks).reshape([-1 if axis == axis_at else 1 for axis in range(len(dims))])
    return gain


def shared_out(own_key, own, number, rows, amount, top, limit, lean):
    ranking = jax.random.permutation(own_key, amount)
    heavy_load, common = portions_of(amount, rows * top, limit, lean, True), portions_of(amount, rows * top, limit, lean, False)
    places = jnp.arange(amount)

    def named(sizes, rotation):
        used = int((sizes > 0).sum())
        fixed = max(1, used // 4)
        passed = fixed + (places - fixed + rotation * (used - fixed)) % max(1, amount - fixed)
        return jnp.zeros((amount,), jnp.int32).at[ranking[jnp.where(places < fixed, places, passed)]].set(jnp.asarray(sizes, jnp.int32))

    sizes = jnp.where(number % 4 == 0, named(heavy_load, number // 4), named(common, number - number // 4 - 1))
    mixed = jax.random.permutation(jax.random.fold_in(own, 3), amount)
    giver, sink = mixed[0:amount // 2 * 2:2], mixed[1:amount // 2 * 2:2]
    margin = jnp.minimum(sizes[giver] - 1, limit - sizes[sink]) // 2
    margin = jnp.where((giver == ranking[0]) | (sink == ranking[0]) | (sizes[sink] == 0), 0, jnp.maximum(margin, 0))
    passed = jax.random.randint(jax.random.fold_in(own, 4), (amount // 2,), 0, 1 << 20) % (margin + 1)
    sizes = sizes.at[giver].add(-passed).at[sink].add(passed)
    labels = jnp.searchsorted(jnp.cumsum(sizes), jnp.arange(rows * top), side="right").astype(jnp.int32)
    listing = labels.reshape(top, rows).T
    listing = listing[jax.random.permutation(jax.random.fold_in(own, 1), rows)]
    rotation = jax.random.randint(jax.random.fold_in(own, 2), (rows, 1), 0, top)
    return jnp.take_along_axis(listing, (jnp.arange(top)[None, :] + rotation) % top, axis=1)


def portions_of(number_of, total, bound, lean, full):
    loads = [(1 << 20) // math.isqrt(grade ** lean) + 1 for grade in range(1, number_of + 1)]
    largest = bound if full else min(bound, max(-(-total // number_of), total * loads[0] // sum(loads)))
    least = 1 if total - largest >= number_of - 1 else 0
    given, rest = [largest] + [least] * (number_of - 1), total - largest - least * (number_of - 1)
    while rest > 0:
        free = [i for i in range(1, number_of) if given[i] < largest] or [i for i in range(1, number_of) if given[i] < bound]
        pool, remaining = sum([loads[i] for i in free]), rest
        for i in free:
            extra = min(bound - given[i], max(1, remaining * loads[i] // pool), rest)
            given[i] = given[i] + extra
            rest = rest - extra
    return np.array(given)


def scatter_about(own_key, dims, spread, reach, shards=(), kind=jnp.bfloat16):
    drawn = spread * jax.random.normal(own_key, dims, jnp.float32)
    if shards:
        drawn = drawn * shard_levels(own_key, dims, shards, -0.22, 0.18)
    return jnp.clip(drawn, -reach, reach).astype(kind)


def setup_inputs(seed: int = 0) -> dict:
    splits = jax.random.split(jax.random.key(seed), 9)
    feats = scatter_about(splits[0], (GROUPS, NODE_DEV, D), 1.0, 6.0, ((0, 512),))
    history = scatter_about(splits[1], (HROWS, 2 * D), 1.0, 6.0, ((0, 32),))
    weight = scatter_about(splits[2], (D, D), D ** -0.5, 0.21875)
    edge_coef = scatter_about(splits[3], (GROUPS, NODE_DEV, TPB * TILE), (TPB * TILE) ** -0.5, 0.375, ((0, 512),))
    tile_map = jax.vmap(lambda own: jax.random.permutation(own, SLOT_BLK))(jax.random.split(splits[4], GROUPS)).reshape((GROUPS, SLOT_BLK)).astype(jnp.int32)
    nbr_owner_keys = jax.random.split(jax.random.fold_in(splits[5], 1), GROUPS * SLOTS // SLOTS)
    nbr_owner_turns = jax.random.permutation(jax.random.fold_in(splits[5], 3), GROUPS * SLOTS // SLOTS)
    nbr_owner = jax.vmap(lambda own, number: shared_out(jax.random.fold_in(splits[5], 2), own, number, SLOTS, N_HIST, 1, CAP, 2))(nbr_owner_keys, nbr_owner_turns).reshape((GROUPS, SLOTS, 1))
    nbr_row = with_ends(jax.random.randint(splits[6], (GROUPS, SLOTS), 0, NODE_DEV + HIST_DEV), jax.random.fold_in(splits[6], 1), 0, (NODE_DEV + HIST_DEV) - 1).astype(jnp.int32)
    grad_out = scatter_about(splits[7], (GROUPS, NODE_DEV, D), 1.0, 6.0, ((0, 512),))
    return {"feats": feats, "history": history, "weight": weight, "edge_coef": edge_coef, "tile_map": tile_map, "nbr_owner": nbr_owner, "nbr_row": nbr_row, "grad_out": grad_out}


def arrange(values, tile_order):
    blocks = values.reshape(SLOT_BLK, TILE, D)[tile_order]
    return blocks.reshape(DST_BLK, TPB * TILE, D).astype(jnp.float32)


def reference(feats, history, weight, edge_coef, tile_map, nbr_owner, nbr_row, grad_out):
    feats_flat = feats.reshape(GROUPS * NODE_DEV, D)

    def group_step(state, group):
        returned, grad_weight = state
        batch_idx = group // N_HIST
        owners = nbr_owner[group, :, 0]
        slot_rows = nbr_row[group]
        inside = slot_rows < NODE_DEV
        feat_index = ((batch_idx * N_HIST + owners) * NODE_DEV + jnp.minimum(slot_rows, NODE_DEV - 1)).astype(jnp.int32)
        hist_index = (owners * HIST_DEV + jnp.maximum(slot_rows - NODE_DEV, 0)).astype(jnp.int32)
        hist_taken = history[hist_index]
        pulled_emb = jnp.where(inside[:, None], feats_flat[feat_index], hist_taken[:, :D])
        pulled_aux = jnp.where(inside[:, None], jnp.zeros_like(hist_taken[:, D:]), hist_taken[:, D:])
        tile_order = tile_map[group]
        edge_tiles = edge_coef[group].reshape(DST_BLK, TILE, TPB * TILE).astype(jnp.float32)
        aggregate = jnp.einsum('cik,ckd->cid', edge_tiles, arrange(pulled_emb, tile_order)).reshape(NODE_DEV, D)
        compensation = jnp.einsum('cik,ckd->cid', edge_tiles, arrange(pulled_aux, tile_order)).reshape(NODE_DEV, D)
        mixed_rows = (feats[group].astype(jnp.float32) + aggregate).astype(jnp.bfloat16)
        pre_act = jnp.dot(mixed_rows, weight, preferred_element_type=jnp.float32)
        sigmoid_pre = jax.nn.sigmoid(pre_act)
        out_rows = (pre_act * sigmoid_pre).astype(jnp.bfloat16)
        grad_pre = (grad_out[group].astype(jnp.float32) * sigmoid_pre * (1.0 + pre_act * (1.0 - sigmoid_pre))).astype(jnp.bfloat16)
        grad_weight = grad_weight + lax.dot_general(mixed_rows, grad_pre, (((0,), (0,)), ((), ())), preferred_element_type=jnp.float32)
        grad_mixed = jnp.dot(grad_pre, weight.T, preferred_element_type=jnp.float32).astype(jnp.bfloat16)
        slot_tiles = jnp.einsum('cik,cid->ckd', edge_tiles, grad_mixed.reshape(DST_BLK, TILE, D).astype(jnp.float32))
        slot_tiles = slot_tiles.reshape(SLOT_BLK, TILE, D)
        slot_grad = jnp.zeros((SLOT_BLK, TILE, D), jnp.float32).at[tile_order].set(slot_tiles)
        slot_grad = slot_grad.reshape(SLOTS, D).astype(jnp.bfloat16)
        slot_grad = jnp.where(inside[:, None], slot_grad, jnp.zeros_like(slot_grad))
        returned = returned.at[feat_index].add(slot_grad.astype(jnp.float32))
        partial_grad = grad_mixed.astype(jnp.float32) + compensation
        return (returned, grad_weight), (out_rows, partial_grad)

    start_state = (jnp.zeros((GROUPS * NODE_DEV, D), jnp.float32), jnp.zeros((D, D), jnp.float32))
    (returned, grad_weight), (out, partial_grad) = lax.scan(group_step, start_state, jnp.arange(GROUPS, dtype=jnp.int32))
    grad_feats = (partial_grad + returned.reshape(GROUPS, NODE_DEV, D)).astype(jnp.bfloat16)
    return out, grad_feats, grad_weight
```

```python
import functools

import jax
import jax.numpy as jnp
from jax import lax
from jax.experimental import pallas as pl
from jax.experimental.pallas import tpu as pltpu
from jax.sharding import PartitionSpec as P

F32 = jnp.float32
BF16 = jnp.bfloat16
LANES = 128
CAP = 16
ROWS_T = (((1,), (1,)), ((), ()))
COLS_T = (((0,), (0,)), ((), ()))


def dot(a, b, dims=(((1,), (0,)), ((), ()))):
    return lax.dot_general(a, b, dims, preferred_element_type=F32)


def in_edge_order(first_tile, values):
    half = values.shape[1] // 2
    swapped = jnp.concatenate([values[:, half:], values[:, :half]], axis=1)
    return jnp.where(first_tile == 0, values, swapped)


def slot_places(owners, peers):
    slots = owners.shape[1]
    named = lax.broadcasted_iota(jnp.int32, (peers, slots), 0) == owners
    named = jnp.where(named, 1.0, 0.0)
    earlier = (
        lax.broadcasted_iota(jnp.int32, (slots, slots), 0)
        < lax.broadcasted_iota(jnp.int32, (slots, slots), 1)
    )
    rank = dot(named.astype(BF16), jnp.where(earlier, 1.0, 0.0).astype(BF16))
    return named, jnp.sum(named * rank, axis=0, keepdims=True).astype(jnp.int32)


def request_kernel(tile_ref, owner_ref, row_ref, ids_ref):
    peers = ids_ref.shape[0]
    first = tile_ref[0, 0]
    owners = in_edge_order(first, owner_ref[...])
    rows = in_edge_order(first, row_ref[...])
    named, place = slot_places(owners, peers)
    spot = lax.broadcasted_iota(jnp.int32, (LANES, rows.shape[1]), 0) == place
    spot = jnp.where(spot, 1.0, 0.0).astype(BF16)
    low = (rows % LANES).astype(F32)
    high = (rows // LANES).astype(F32)
    ids = dot((named * low).astype(BF16), spot, ROWS_T) + LANES * dot(
        (named * high).astype(BF16), spot, ROWS_T
    )
    ids_ref[...] = ids.astype(jnp.int32).reshape(ids_ref.shape)


def coef_kernel(peers, node_rows, tile_ref, owner_ref, row_ref, edge_ref, all_ref, inside_ref):
    first = tile_ref[0, 0]
    owners = in_edge_order(first, owner_ref[...])
    rows = in_edge_order(first, row_ref[...])
    _, place = slot_places(owners, peers)
    target = owners * CAP + place
    total = all_ref.shape[1]
    at = lax.broadcasted_iota(jnp.int32, (total, target.shape[1]), 0) == target
    moved = jnp.where(at, 1.0, 0.0)
    edge = edge_ref[...]
    all_ref[...] = dot(edge, moved.astype(BF16), ROWS_T).astype(BF16)
    kept = jnp.where(rows < node_rows, moved, 0.0).astype(BF16)
    inside_ref[...] = dot(edge, kept, ROWS_T).astype(BF16)


def gather_kernel(ids_ref, feats_ref, history_ref, taken_ref, pick_ref):
    node_rows, width = feats_ref.shape
    table_rows = history_ref.shape[0]
    peers = ids_ref.shape[0]
    ids = ids_ref[...].reshape(peers, LANES).astype(F32)
    ids = jnp.concatenate([ids, jnp.zeros((LANES - peers, LANES), F32)], axis=0)
    by_place = ids.T.astype(jnp.int32)
    columns = lax.broadcasted_iota(jnp.int32, (CAP, node_rows + table_rows), 1)
    part = peers // 4
    for start in range(0, peers, part):
        picks = [
            jnp.where(columns == by_place[:CAP, g : g + 1], 1.0, 0.0).astype(BF16)
            for g in range(start, start + part)
        ]
        pick = jnp.concatenate(picks, axis=0)
        near, far = pick[:, :node_rows], pick[:, node_rows:]
        pick_ref[start * CAP : (start + part) * CAP, :] = near
        emb = dot(near, feats_ref[...]) + dot(far, history_ref[:, :width])
        aux = dot(far, history_ref[:, width:])
        taken_ref[start : start + part, :, :width] = emb.astype(BF16).reshape(part, CAP, width)
        taken_ref[start : start + part, :, width:] = aux.astype(BF16).reshape(part, CAP, width)


def layer_kernel(
    pulled_ref, all_ref, inside_ref, feats_ref, weight_ref, grad_ref, out_ref, part_ref, send_ref
):
    peers = pulled_ref.shape[0]
    node_rows, width = feats_ref.shape
    pulled = pulled_ref[...].reshape(peers * CAP, 2 * width)
    both = dot(all_ref[...], pulled)
    mixed = (feats_ref[...].astype(F32) + both[:, :width]).astype(BF16)
    pre = dot(mixed, weight_ref[...])
    gate = jax.nn.sigmoid(pre)
    out_ref[...] = (pre * gate).astype(BF16)
    grad_pre = (grad_ref[...].astype(F32) * gate * (1.0 + pre * (1.0 - gate))).astype(BF16)
    grad_mixed = dot(grad_pre, weight_ref[...], ROWS_T).astype(BF16)
    part_ref[...] = grad_mixed.astype(F32) + both[:, width:]
    slot_grad = dot(inside_ref[...], grad_mixed, COLS_T).astype(BF16)
    send_ref[:, :, :width] = slot_grad.reshape(peers, CAP, width)
    share = width // peers
    rest = share - CAP
    half = width // 2
    for chunk in range(2):
        span = width // 2
        term = dot(mixed[:, chunk * span : (chunk + 1) * span], grad_pre, COLS_T)
        for i in range(peers // 2):
            peer = chunk * (peers // 2) + i
            rows = term[i * share : (i + 1) * share, :]
            tail = rows[CAP:, :]
            tail = jnp.concatenate([tail[:, :half], tail[:, half:]], axis=0)
            send_ref[peer, :, width : 2 * width] = rows[:CAP, :].astype(BF16)
            send_ref[peer, :, 2 * width :] = tail.astype(BF16)


def weight_kernel(back_ref, near_ref):
    width = near_ref.shape[2]
    terms = jnp.sum(back_ref[:, :, width:].astype(F32), axis=0)
    head = terms[:, :width]
    tail = terms[:, width:]
    half = tail.shape[0] // 2
    tail = jnp.concatenate([tail[:half, :], tail[half:, :]], axis=1)
    share = jnp.concatenate([head, tail], axis=0).astype(BF16)
    for i in range(near_ref.shape[0]):
        near_ref[i] = share


def final_kernel(back_ref, pick_ref, part_ref, grad_ref):
    peers = back_ref.shape[0]
    width = part_ref.shape[1]
    slots = back_ref[:, :, :width].reshape(peers * CAP, width)
    returned = dot(pick_ref[...], slots, COLS_T)
    grad_ref[...] = (part_ref[...] + returned).astype(BF16)


def call(kernel, out_shape, *args, smem=0, cost=None):
    in_specs = [
        pl.BlockSpec(memory_space=pltpu.SMEM if i < smem else pltpu.VMEM) for i in range(len(args))
    ]
    single = not isinstance(out_shape, (list, tuple))
    out_specs = pl.BlockSpec(memory_space=pltpu.VMEM)
    return pl.pallas_call(
        kernel,
        out_shape=out_shape,
        in_specs=in_specs,
        out_specs=out_specs if single else [out_specs] * len(out_shape),
        compiler_params=pltpu.CompilerParams(vmem_limit_bytes=40 << 20),
        cost_estimate=cost,
    )(*args)


def swap(values, axis, groups=None):
    return lax.all_to_all(
        values, axis, split_axis=0, concat_axis=0, tiled=True, axis_index_groups=groups
    )


def body(feats, history, weight, edge_coef, tile_map, nbr_owner, nbr_row, grad_out):
    peers = lax.axis_size("hist")
    planes = lax.axis_size("batch")
    node_rows, width = feats.shape[1:]
    slots = nbr_row.shape[1]
    capacity = 2 * slots // peers
    assert capacity == CAP
    shape = jax.ShapeDtypeStruct
    owners = nbr_owner.reshape(1, slots)
    ids = call(
        request_kernel, shape((peers, 1, LANES), jnp.int32), tile_map, owners, nbr_row, smem=1
    )
    received = swap(ids, "hist")
    coef, coef_inside = call(
        functools.partial(coef_kernel, peers, node_rows),
        [shape((node_rows, peers * CAP), BF16)] * 2,
        tile_map,
        owners,
        nbr_row,
        edge_coef[0],
        smem=1,
    )
    taken, pick = call(
        gather_kernel,
        [shape((peers, CAP, 2 * width), BF16), shape((peers * CAP, node_rows), BF16)],
        received,
        feats[0],
        history,
    )
    pulled = swap(taken, "hist")
    share = width // peers
    sent_width = width + share * width // CAP
    out_rows, part, sent = call(
        layer_kernel,
        [
            shape((node_rows, width), BF16),
            shape((node_rows, width), F32),
            shape((peers, CAP, sent_width), BF16),
        ],
        pulled,
        coef,
        coef_inside,
        feats[0],
        weight,
        grad_out[0],
    )
    back = swap(sent, "hist")
    side = 4
    near = [[a * side + i for i in range(side)] for a in range(planes // side)]
    far = [[a + side * i for i in range(planes // side)] for a in range(side)]
    term = call(weight_kernel, shape((side, share, width), BF16), back)
    term = swap(term, "batch", near)
    grad_rows = call(final_kernel, shape((node_rows, width), BF16), back, pick, part)
    term = jnp.sum(term.astype(F32), axis=0).astype(BF16)
    term = jnp.broadcast_to(term[None], (planes // side, share, width))
    term = swap(term, "batch", far)
    weight_share = jnp.sum(term.astype(F32), axis=0)
    return (out_rows[None], grad_rows[None], weight_share)


def solution(mesh):
    return jax.shard_map(
        body,
        mesh=mesh,
        in_specs=(
            P(("batch", "hist"), None, None),
            P("hist", None),
            P(),
            P(("batch", "hist"), None, None),
            P(("batch", "hist"), None),
            P(("batch", "hist"), None, None),
            P(("batch", "hist"), None),
            P(("batch", "hist"), None, None),
        ),
        out_specs=(
            P(("batch", "hist"), None, None),
            P(("batch", "hist"), None, None),
            P("hist", None),
        ),
        check_vma=False,
    )
```

```python
import functools

import jax
import jax.numpy as jnp
from jax import lax
from jax.experimental import pallas as pl
from jax.experimental.pallas import tpu as pltpu
from jax.sharding import PartitionSpec as P

F32 = jnp.float32
BF16 = jnp.bfloat16
LANES = 128
CAP = 16
ROWS_T = (((1,), (1,)), ((), ()))
COLS_T = (((0,), (0,)), ((), ()))


def dot(a, b, dims=(((1,), (0,)), ((), ()))):
    return lax.dot_general(a, b, dims, preferred_element_type=F32)


def in_edge_order(first_tile, values):
    half = values.shape[1] // 2
    swapped = jnp.concatenate([values[:, half:], values[:, :half]], axis=1)
    return jnp.where(first_tile == 0, values, swapped)


def slot_places(owners, peers):
    slots = owners.shape[1]
    named = lax.broadcasted_iota(jnp.int32, (peers, slots), 0) == owners
    named = jnp.where(named, 1.0, 0.0)
    earlier = (
        lax.broadcasted_iota(jnp.int32, (slots, slots), 0)
        < lax.broadcasted_iota(jnp.int32, (slots, slots), 1)
    )
    rank = dot(named.astype(BF16), jnp.where(earlier, 1.0, 0.0).astype(BF16))
    return named, jnp.sum(named * rank, axis=0, keepdims=True).astype(jnp.int32)


def request_kernel(tile_in, owner_in, row_in, ids_ref, tile_ref, owner_ref, row_ref, sems):
    copies = [
        pltpu.make_async_copy(tile_in, tile_ref, sems.at[0]),
        pltpu.make_async_copy(owner_in, owner_ref, sems.at[1]),
        pltpu.make_async_copy(row_in, row_ref, sems.at[2]),
    ]
    for copy in copies:
        copy.start()
    for copy in copies:
        copy.wait()
    peers = ids_ref.shape[0]
    first = tile_ref[0, 0]
    owners = in_edge_order(first, owner_ref[...])
    rows = in_edge_order(first, row_ref[...])
    named, place = slot_places(owners, peers)
    spot = lax.broadcasted_iota(jnp.int32, (LANES, rows.shape[1]), 0) == place
    spot = jnp.where(spot, 1.0, 0.0).astype(BF16)
    low = (rows % LANES).astype(F32)
    high = (rows // LANES).astype(F32)
    ids = dot((named * low).astype(BF16), spot, ROWS_T) + LANES * dot(
        (named * high).astype(BF16), spot, ROWS_T
    )
    ids_ref[...] = ids.astype(jnp.int32).reshape(ids_ref.shape)


def gather_kernel(ids_ref, feats_in, history_in, taken_ref, pick_out, feats, history, pick, sems):
    node_rows, width = feats.shape
    table_rows = history.shape[0]
    peers = ids_ref.shape[0]
    load_feats = pltpu.make_async_copy(feats_in, feats, sems.at[0])
    load_history = pltpu.make_async_copy(history_in.at[:, :width], history, sems.at[1])
    load_feats.start()
    load_history.start()
    ids = ids_ref[...].reshape(peers, LANES).astype(F32)
    ids = jnp.concatenate([ids, jnp.zeros((LANES - peers, LANES), F32)], axis=0)
    by_place = ids.T.astype(jnp.int32)
    columns = lax.broadcasted_iota(jnp.int32, (CAP, node_rows + table_rows), 1)
    for g in range(peers):
        chosen = columns == by_place[:CAP, g : g + 1]
        pick[g * CAP : (g + 1) * CAP, :] = jnp.where(chosen, 1.0, 0.0).astype(BF16)
    store = pltpu.make_async_copy(pick, pick_out, sems.at[2])
    store.start()
    load_feats.wait()
    load_history.wait()
    part = peers // 4
    for start in range(0, peers, part):
        near = pick[start * CAP : (start + part) * CAP, :node_rows]
        far = pick[start * CAP : (start + part) * CAP, node_rows:]
        emb = dot(near, feats[...]) + dot(far, history[...])
        taken_ref[start : start + part] = emb.astype(BF16).reshape(part, CAP, width)
    store.wait()


def forward_kernel(
    peers,
    tile_ref,
    owner_ref,
    row_ref,
    edge_ref,
    pulled_ref,
    feats_ref,
    weight_ref,
    grad_ref,
    out_ref,
    pre_ref,
    own_ref,
    away_ref,
    all_ref,
    inside_ref,
):
    node_rows, width = feats_ref.shape
    half = width // 2
    first = tile_ref[0, 0]
    owners = in_edge_order(first, owner_ref[...])
    rows = in_edge_order(first, row_ref[...])
    _, place = slot_places(owners, peers)
    target = owners * CAP + place
    at = lax.broadcasted_iota(jnp.int32, (peers * CAP, target.shape[1]), 0) == target
    moved = jnp.where(at, 1.0, 0.0)
    coef = dot(edge_ref[...], moved.astype(BF16), ROWS_T).astype(BF16)
    pulled = pulled_ref[...].reshape(peers * CAP, width)
    mixed = (feats_ref[...].astype(F32) + dot(coef, pulled)).astype(BF16)
    pre = dot(mixed, weight_ref[...])
    gate = jax.nn.sigmoid(pre)
    grad_pre = (grad_ref[...].astype(F32) * gate * (1.0 + pre * (1.0 - gate))).astype(BF16)
    second_core = lax.axis_index("hist") % 2 == 1
    left, right = grad_pre[:, :half], grad_pre[:, half:]
    own_ref[:, :width] = mixed
    own_ref[:, width:] = jnp.where(second_core, right, left)
    away_ref[:, :width] = mixed
    away_ref[:, width:] = jnp.where(second_core, left, right)
    pre_ref[...] = grad_pre
    out_ref[...] = (pre * gate).astype(BF16)
    all_ref[...] = coef
    kept = jnp.where(rows < node_rows, moved, 0.0).astype(BF16)
    inside_ref[...] = dot(edge_ref[...], kept, ROWS_T).astype(BF16)


def term_kernel(peers, width, own_ref, away_ref, term_ref):
    mixed = jnp.concatenate([own_ref[:, :width], away_ref[:, :width]], axis=0)
    grad_pre = jnp.concatenate([own_ref[:, width:], away_ref[:, width:]], axis=0)
    share = width // peers
    step = 8
    term = dot(mixed, grad_pre, COLS_T)
    for peer in range(peers):
        blocks = [
            term[peer * share + i : peer * share + i + step, :] for i in range(0, share, step)
        ]
        term_ref[peer] = jnp.concatenate(blocks, axis=1).astype(BF16)


def backward_kernel(
    pre_ref, weight_ref, inside_ref, pick_in, history_in, send_ref, mixed_ref, pick, aux, sems
):
    node_rows, width = mixed_ref.shape
    peers = send_ref.shape[0]
    load_pick = pltpu.make_async_copy(pick_in, pick, sems.at[0])
    load_aux = pltpu.make_async_copy(history_in.at[:, width:], aux, sems.at[1])
    load_pick.start()
    load_aux.start()
    grad_mixed = dot(pre_ref[...], weight_ref[...], ROWS_T).astype(BF16)
    mixed_ref[...] = grad_mixed
    slot_grad = dot(inside_ref[...], grad_mixed, COLS_T).astype(BF16)
    send_ref[:, :, :width] = slot_grad.reshape(peers, CAP, width)
    load_pick.wait()
    load_aux.wait()
    taken = dot(pick[:, node_rows:], aux[...]).astype(BF16)
    send_ref[:, :, width:] = taken.reshape(peers, CAP, width)


def weight_kernel(terms_ref, sum_ref):
    peers, step = terms_ref.shape[:2]
    for core in range(2):
        total = terms_ref[core].astype(F32)
        for peer in range(core + 2, peers, 2):
            total = total + terms_ref[peer].astype(F32)
        sum_ref[core * step : (core + 1) * step, :] = total.astype(BF16)


def add_kernel(a_ref, b_ref, c_ref, d_ref, sum_ref):
    total = a_ref[...].astype(F32) + b_ref[...].astype(F32)
    total = total + (c_ref[...].astype(F32) + d_ref[...].astype(F32))
    sum_ref[...] = total.astype(BF16)


def share_kernel(a_ref, b_ref, c_ref, d_ref, share_ref):
    total = a_ref[...].astype(F32) + b_ref[...].astype(F32)
    total = total + (c_ref[...].astype(F32) + d_ref[...].astype(F32))
    share, width = share_ref.shape
    half = width // 2
    step = total.shape[0] // 2
    for i in range(share // step):
        for core in range(2):
            share_ref[i * step : (i + 1) * step, core * half : (core + 1) * half] = total[
                core * step : (core + 1) * step, i * half : (i + 1) * half
            ]


def final_kernel(back_ref, pick_ref, all_ref, mixed_ref, grad_ref):
    peers = back_ref.shape[0]
    node_rows, width = mixed_ref.shape
    slots = back_ref[:, :, :width].reshape(peers * CAP, width)
    aux = back_ref[:, :, width:].reshape(peers * CAP, width)
    returned = dot(pick_ref[:, :node_rows], slots, COLS_T)
    compensation = dot(all_ref[...], aux)
    total = mixed_ref[...].astype(F32) + returned + compensation
    grad_ref[...] = total.astype(BF16)


def call(kernel, out_shape, *args, smem=(), hbm=(), hbm_out=(), scratch=()):
    spaces = [
        pltpu.SMEM if i in smem else pltpu.HBM if i in hbm else pltpu.VMEM
        for i in range(len(args))
    ]
    single = not isinstance(out_shape, (list, tuple))
    out_shape = [out_shape] if single else out_shape
    out_spaces = [pltpu.HBM if i in hbm_out else pltpu.VMEM for i in range(len(out_shape))]
    result = pl.pallas_call(
        kernel,
        out_shape=out_shape,
        in_specs=[pl.BlockSpec(memory_space=space) for space in spaces],
        out_specs=[pl.BlockSpec(memory_space=space) for space in out_spaces],
        scratch_shapes=list(scratch),
        compiler_params=pltpu.CompilerParams(vmem_limit_bytes=32 << 20),
    )(*args)
    return result[0] if single else result


def swap(values):
    return lax.all_to_all(values, "hist", split_axis=0, concat_axis=0, tiled=True)


def shift(values, axis, by):
    count = lax.axis_size(axis)
    return lax.ppermute(values, axis, [(i, (i + by) % count) for i in range(count)])


def body(feats, history, weight, edge_coef, tile_map, nbr_owner, nbr_row, grad_out):
    peers = lax.axis_size("hist")
    planes = lax.axis_size("batch")
    node_rows, width = feats.shape[1:]
    table_rows = history.shape[0]
    slots = nbr_row.shape[1]
    assert 2 * slots // peers == CAP and planes == 16
    share = width // peers
    shape = jax.ShapeDtypeStruct
    owners = nbr_owner.reshape(1, slots)
    ids = call(
        request_kernel,
        shape((peers, 1, LANES), jnp.int32),
        tile_map,
        owners,
        nbr_row,
        hbm=(0, 1, 2),
        scratch=(
            pltpu.SMEM(tile_map.shape, jnp.int32),
            pltpu.VMEM(owners.shape, jnp.int32),
            pltpu.VMEM(nbr_row.shape, jnp.int32),
            pltpu.SemaphoreType.DMA((3,)),
        ),
    )
    received = swap(ids)
    table = node_rows + table_rows
    taken, pick = call(
        gather_kernel,
        [shape((peers, CAP, width), BF16), shape((peers * CAP, table), BF16)],
        received,
        feats[0],
        history,
        hbm=(1, 2),
        hbm_out=(1,),
        scratch=(
            pltpu.VMEM((node_rows, width), BF16),
            pltpu.VMEM((table_rows, width), BF16),
            pltpu.VMEM((peers * CAP, table), BF16),
            pltpu.SemaphoreType.DMA((3,)),
        ),
    )
    pulled = swap(taken)
    out_rows, grad_pre, own, away, coef, coef_inside = call(
        functools.partial(forward_kernel, peers),
        [
            shape((node_rows, width), BF16),
            shape((node_rows, width), BF16),
            shape((node_rows, width + width // 2), BF16),
            shape((node_rows, width + width // 2), BF16),
            shape((node_rows, peers * CAP), BF16),
            shape((node_rows, peers * CAP), BF16),
        ],
        tile_map,
        owners,
        nbr_row,
        edge_coef[0],
        pulled,
        feats[0],
        weight,
        grad_out[0],
        smem=(0,),
    )
    away = lax.ppermute(away, "hist", [(i, i ^ 1) for i in range(peers)])
    terms = call(
        functools.partial(term_kernel, peers, width),
        shape((peers, 8, share * width // 16), BF16),
        own,
        away,
    )
    grad_pre, terms = lax.optimization_barrier((grad_pre, terms))
    terms = swap(terms)
    sent, grad_mixed = call(
        backward_kernel,
        [shape((peers, CAP, 2 * width), BF16), shape((node_rows, width), BF16)],
        grad_pre,
        weight,
        coef_inside,
        pick,
        history,
        hbm=(3, 4),
        scratch=(
            pltpu.VMEM((peers * CAP, table), BF16),
            pltpu.VMEM((table_rows, width), BF16),
            pltpu.SemaphoreType.DMA((2,)),
        ),
    )
    sent, terms = lax.optimization_barrier((sent, terms))
    back = swap(sent)
    term = call(weight_kernel, shape((16, share * width // 16), BF16), terms)
    near = [shift(term, "batch", by) for by in (1, -1, 2)]
    term = call(add_kernel, shape(term.shape, BF16), term, *near)
    far = [shift(term, "batch", by) for by in (4, -4, 8)]
    weight_share = call(share_kernel, shape((share, width), F32), term, *far)
    grad_rows = call(
        final_kernel, shape((node_rows, width), BF16), back, pick, coef, grad_mixed
    )
    return (out_rows[None], grad_rows[None], weight_share)


def solution(mesh):
    return jax.shard_map(
        body,
        mesh=mesh,
        in_specs=(
            P(("batch", "hist"), None, None),
            P("hist", None),
            P(),
            P(("batch", "hist"), None, None),
            P(("batch", "hist"), None),
            P(("batch", "hist"), None, None),
            P(("batch", "hist"), None),
            P(("batch", "hist"), None, None),
        ),
        out_specs=(
            P(("batch", "hist"), None, None),
            P(("batch", "hist"), None, None),
            P("hist", None),
        ),
        check_vma=False,
    )
```

```python
import functools

import jax
import jax.numpy as jnp
from jax import lax
from jax.experimental import pallas as pl
from jax.experimental.pallas import tpu as pltpu
from jax.sharding import PartitionSpec as P

F32 = jnp.float32
BF16 = jnp.bfloat16
LANES = 128
CAP = 16
ROWS_T = (((1,), (1,)), ((), ()))
COLS_T = (((0,), (0,)), ((), ()))


def dot(a, b, dims=(((1,), (0,)), ((), ()))):
    return lax.dot_general(a, b, dims, preferred_element_type=F32)


def in_edge_order(first_tile, values):
    half = values.shape[1] // 2
    swapped = jnp.concatenate([values[:, half:], values[:, :half]], axis=1)
    return jnp.where(first_tile == 0, values, swapped)


def slot_places(owners, peers):
    slots = owners.shape[1]
    named = lax.broadcasted_iota(jnp.int32, (peers, slots), 0) == owners
    named = jnp.where(named, 1.0, 0.0)
    earlier = (
        lax.broadcasted_iota(jnp.int32, (slots, slots), 0)
        < lax.broadcasted_iota(jnp.int32, (slots, slots), 1)
    )
    rank = dot(named.astype(BF16), jnp.where(earlier, 1.0, 0.0).astype(BF16))
    return named, jnp.sum(named * rank, axis=0, keepdims=True).astype(jnp.int32)


def request_kernel(tile_in, owner_in, row_in, ids_ref, tile_ref, owner_ref, row_ref, sems):
    copies = [
        pltpu.make_async_copy(tile_in, tile_ref, sems.at[0]),
        pltpu.make_async_copy(owner_in, owner_ref, sems.at[1]),
        pltpu.make_async_copy(row_in, row_ref, sems.at[2]),
    ]
    for copy in copies:
        copy.start()
    for copy in copies:
        copy.wait()
    peers = ids_ref.shape[0]
    first = tile_ref[0, 0]
    owners = in_edge_order(first, owner_ref[...])
    rows = in_edge_order(first, row_ref[...])
    named, place = slot_places(owners, peers)
    spot = lax.broadcasted_iota(jnp.int32, (LANES, rows.shape[1]), 0) == place
    spot = jnp.where(spot, 1.0, 0.0).astype(BF16)
    low = (rows % LANES).astype(F32)
    high = (rows // LANES).astype(F32)
    ids = dot((named * low).astype(BF16), spot, ROWS_T) + LANES * dot(
        (named * high).astype(BF16), spot, ROWS_T
    )
    ids_ref[...] = ids.astype(jnp.int32).reshape(ids_ref.shape)


def gather_kernel(ids_ref, feats_in, history_in, taken_ref, pick_out, feats, history, pick, sems):
    node_rows, width = feats.shape
    table_rows = history.shape[0]
    peers = ids_ref.shape[0]
    load_feats = pltpu.make_async_copy(feats_in, feats, sems.at[0])
    load_history = pltpu.make_async_copy(history_in.at[:, :width], history, sems.at[1])
    load_feats.start()
    load_history.start()
    ids = ids_ref[...].reshape(peers, LANES).astype(F32)
    ids = jnp.concatenate([ids, jnp.zeros((LANES - peers, LANES), F32)], axis=0)
    by_place = ids.T.astype(jnp.int32)
    columns = lax.broadcasted_iota(jnp.int32, (CAP, node_rows + table_rows), 1)
    for g in range(peers):
        chosen = columns == by_place[:CAP, g : g + 1]
        pick[g * CAP : (g + 1) * CAP, :] = jnp.where(chosen, 1.0, 0.0).astype(BF16)
    store = pltpu.make_async_copy(pick, pick_out, sems.at[2])
    store.start()
    load_feats.wait()
    load_history.wait()
    part = peers // 4
    for start in range(0, peers, part):
        near = pick[start * CAP : (start + part) * CAP, :node_rows]
        far = pick[start * CAP : (start + part) * CAP, node_rows:]
        emb = dot(near, feats[...]) + dot(far, history[...])
        taken_ref[start : start + part] = emb.astype(BF16).reshape(part, CAP, width)
    store.wait()


def forward_kernel(
    peers,
    tile_ref,
    owner_ref,
    row_ref,
    edge_ref,
    pulled_ref,
    feats_ref,
    weight_ref,
    grad_ref,
    out_ref,
    pre_ref,
    own_ref,
    away_ref,
    all_ref,
    inside_ref,
):
    node_rows, width = feats_ref.shape
    half = width // 2
    first = tile_ref[0, 0]
    owners = in_edge_order(first, owner_ref[...])
    rows = in_edge_order(first, row_ref[...])
    _, place = slot_places(owners, peers)
    target = owners * CAP + place
    at = lax.broadcasted_iota(jnp.int32, (peers * CAP, target.shape[1]), 0) == target
    moved = jnp.where(at, 1.0, 0.0)
    coef = dot(edge_ref[...], moved.astype(BF16), ROWS_T).astype(BF16)
    pulled = pulled_ref[...].reshape(peers * CAP, width)
    mixed = (feats_ref[...].astype(F32) + dot(coef, pulled)).astype(BF16)
    pre = dot(mixed, weight_ref[...])
    gate = jax.nn.sigmoid(pre)
    grad_pre = (grad_ref[...].astype(F32) * gate * (1.0 + pre * (1.0 - gate))).astype(BF16)
    second_core = lax.axis_index("hist") % 2 == 1
    left, right = grad_pre[:, :half], grad_pre[:, half:]
    own_ref[:, :width] = mixed
    own_ref[:, width:] = jnp.where(second_core, right, left)
    away_ref[:, :width] = mixed
    away_ref[:, width:] = jnp.where(second_core, left, right)
    pre_ref[...] = grad_pre
    out_ref[...] = (pre * gate).astype(BF16)
    all_ref[...] = coef
    kept = jnp.where(rows < node_rows, moved, 0.0).astype(BF16)
    inside_ref[...] = dot(edge_ref[...], kept, ROWS_T).astype(BF16)


def term_kernel(peers, width, own_ref, away_ref, term_ref):
    mixed = jnp.concatenate([own_ref[:, :width], away_ref[:, :width]], axis=0)
    grad_pre = jnp.concatenate([own_ref[:, width:], away_ref[:, width:]], axis=0)
    share = width // peers
    step = 8
    term = dot(mixed, grad_pre, COLS_T)
    for peer in range(peers):
        blocks = [
            term[peer * share + i : peer * share + i + step, :] for i in range(0, share, step)
        ]
        term_ref[peer] = jnp.concatenate(blocks, axis=1).astype(BF16)


def backward_kernel(
    pre_ref, weight_ref, inside_ref, pick_in, history_in, send_ref, mixed_ref, pick, aux, sems
):
    node_rows, width = mixed_ref.shape
    peers = send_ref.shape[0]
    load_pick = pltpu.make_async_copy(pick_in, pick, sems.at[0])
    load_aux = pltpu.make_async_copy(history_in.at[:, width:], aux, sems.at[1])
    load_pick.start()
    load_aux.start()
    grad_mixed = dot(pre_ref[...], weight_ref[...], ROWS_T).astype(BF16)
    mixed_ref[...] = grad_mixed
    slot_grad = dot(inside_ref[...], grad_mixed, COLS_T).astype(BF16)
    send_ref[:, :, :width] = slot_grad.reshape(peers, CAP, width)
    load_pick.wait()
    load_aux.wait()
    taken = dot(pick[:, node_rows:], aux[...]).astype(BF16)
    send_ref[:, :, width:] = taken.reshape(peers, CAP, width)


def weight_kernel(terms_ref, sum_ref):
    peers, step = terms_ref.shape[:2]
    for core in range(2):
        total = terms_ref[core].astype(F32)
        for peer in range(core + 2, peers, 2):
            total = total + terms_ref[peer].astype(F32)
        total = total.astype(BF16)
        for plane in range(sum_ref.shape[0]):
            sum_ref[plane, core * step : (core + 1) * step, :] = total


def add_kernel(near_ref, sum_ref):
    sum_ref[...] = jnp.sum(near_ref[...].astype(F32), axis=0).astype(BF16)


def share_kernel(a_ref, b_ref, c_ref, d_ref, share_ref):
    total = a_ref[...].astype(F32) + b_ref[...].astype(F32)
    total = total + (c_ref[...].astype(F32) + d_ref[...].astype(F32))
    share, width = share_ref.shape
    half = width // 2
    step = total.shape[0] // 2
    for i in range(share // step):
        for core in range(2):
            share_ref[i * step : (i + 1) * step, core * half : (core + 1) * half] = total[
                core * step : (core + 1) * step, i * half : (i + 1) * half
            ]


def final_kernel(back_ref, pick_ref, all_ref, mixed_ref, grad_ref):
    peers = back_ref.shape[0]
    node_rows, width = mixed_ref.shape
    slots = back_ref[:, :, :width].reshape(peers * CAP, width)
    aux = back_ref[:, :, width:].reshape(peers * CAP, width)
    returned = dot(pick_ref[:, :node_rows], slots, COLS_T)
    compensation = dot(all_ref[...], aux)
    total = mixed_ref[...].astype(F32) + returned + compensation
    grad_ref[...] = total.astype(BF16)


def call(kernel, out_shape, *args, smem=(), hbm=(), hbm_out=(), scratch=(), vmem=32):
    spaces = [
        pltpu.SMEM if i in smem else pltpu.HBM if i in hbm else pltpu.VMEM
        for i in range(len(args))
    ]
    single = not isinstance(out_shape, (list, tuple))
    out_shape = [out_shape] if single else out_shape
    out_spaces = [pltpu.HBM if i in hbm_out else pltpu.VMEM for i in range(len(out_shape))]
    result = pl.pallas_call(
        kernel,
        out_shape=out_shape,
        in_specs=[pl.BlockSpec(memory_space=space) for space in spaces],
        out_specs=[pl.BlockSpec(memory_space=space) for space in out_spaces],
        scratch_shapes=list(scratch),
        compiler_params=pltpu.CompilerParams(vmem_limit_bytes=vmem << 20),
    )(*args)
    return result[0] if single else result


def swap(values, axis="hist", groups=None):
    return lax.all_to_all(
        values, axis, split_axis=0, concat_axis=0, tiled=True, axis_index_groups=groups
    )


def shift(values, axis, by):
    count = lax.axis_size(axis)
    return lax.ppermute(values, axis, [(i, (i + by) % count) for i in range(count)])


def body(feats, history, weight, edge_coef, tile_map, nbr_owner, nbr_row, grad_out):
    peers = lax.axis_size("hist")
    planes = lax.axis_size("batch")
    node_rows, width = feats.shape[1:]
    table_rows = history.shape[0]
    slots = nbr_row.shape[1]
    assert 2 * slots // peers == CAP and planes == 16
    share = width // peers
    shape = jax.ShapeDtypeStruct
    owners = nbr_owner.reshape(1, slots)
    ids = call(
        request_kernel,
        shape((peers, 1, LANES), jnp.int32),
        tile_map,
        owners,
        nbr_row,
        hbm=(0, 1, 2),
        vmem=60,
        scratch=(
            pltpu.SMEM(tile_map.shape, jnp.int32),
            pltpu.VMEM(owners.shape, jnp.int32),
            pltpu.VMEM(nbr_row.shape, jnp.int32),
            pltpu.SemaphoreType.DMA((3,)),
        ),
    )
    received = swap(ids)
    table = node_rows + table_rows
    taken, pick = call(
        gather_kernel,
        [shape((peers, CAP, width), BF16), shape((peers * CAP, table), BF16)],
        received,
        feats[0],
        history,
        hbm=(1, 2),
        hbm_out=(1,),
        vmem=60,
        scratch=(
            pltpu.VMEM((node_rows, width), BF16),
            pltpu.VMEM((table_rows, width), BF16),
            pltpu.VMEM((peers * CAP, table), BF16),
            pltpu.SemaphoreType.DMA((3,)),
        ),
    )
    pulled = swap(taken)
    out_rows, grad_pre, own, away, coef, coef_inside = call(
        functools.partial(forward_kernel, peers),
        [
            shape((node_rows, width), BF16),
            shape((node_rows, width), BF16),
            shape((node_rows, width + width // 2), BF16),
            shape((node_rows, width + width // 2), BF16),
            shape((node_rows, peers * CAP), BF16),
            shape((node_rows, peers * CAP), BF16),
        ],
        tile_map,
        owners,
        nbr_row,
        edge_coef[0],
        pulled,
        feats[0],
        weight,
        grad_out[0],
        smem=(0,),
    )
    away = lax.ppermute(away, "hist", [(i, i ^ 1) for i in range(peers)])
    terms = call(
        functools.partial(term_kernel, peers, width),
        shape((peers, 8, share * width // 16), BF16),
        own,
        away,
    )
    grad_pre, terms = lax.optimization_barrier((grad_pre, terms))
    terms = swap(terms)
    sent, grad_mixed = call(
        backward_kernel,
        [shape((peers, CAP, 2 * width), BF16), shape((node_rows, width), BF16)],
        grad_pre,
        weight,
        coef_inside,
        pick,
        history,
        hbm=(3, 4),
        scratch=(
            pltpu.VMEM((peers * CAP, table), BF16),
            pltpu.VMEM((table_rows, width), BF16),
            pltpu.SemaphoreType.DMA((2,)),
        ),
    )
    side = 4
    near = [[a * side + i for i in range(side)] for a in range(planes // side)]
    term = call(weight_kernel, shape((side, 16, share * width // 16), BF16), terms)
    term = swap(term, "batch", near)
    sent, term = lax.optimization_barrier((sent, term))
    back = swap(sent)
    term = call(add_kernel, shape(term.shape[1:], BF16), term)
    far = [shift(term, "batch", by) for by in (4, -4, 8)]
    weight_share = call(share_kernel, shape((share, width), F32), term, *far)
    grad_rows = call(
        final_kernel, shape((node_rows, width), BF16), back, pick, coef, grad_mixed
    )
    return (out_rows[None], grad_rows[None], weight_share)


def solution(mesh):
    return jax.shard_map(
        body,
        mesh=mesh,
        in_specs=(
            P(("batch", "hist"), None, None),
            P("hist", None),
            P(),
            P(("batch", "hist"), None, None),
            P(("batch", "hist"), None),
            P(("batch", "hist"), None, None),
            P(("batch", "hist"), None),
            P(("batch", "hist"), None, None),
        ),
        out_specs=(
            P(("batch", "hist"), None, None),
            P(("batch", "hist"), None, None),
            P("hist", None),
        ),
        check_vma=False,
    )
```

```python
import functools

import jax
import jax.numpy as jnp
from jax import lax
from jax.experimental import pallas as pl
from jax.experimental.pallas import tpu as pltpu
from jax.sharding import PartitionSpec as P

F32 = jnp.float32
BF16 = jnp.bfloat16
LANES = 128
CAP = 16
ROWS_T = (((1,), (1,)), ((), ()))
COLS_T = (((0,), (0,)), ((), ()))


def dot(a, b, dims=(((1,), (0,)), ((), ()))):
    return lax.dot_general(a, b, dims, preferred_element_type=F32)


def in_edge_order(first_tile, values):
    half = values.shape[1] // 2
    swapped = jnp.concatenate([values[:, half:], values[:, :half]], axis=1)
    return jnp.where(first_tile == 0, values, swapped)


def slot_places(owners, peers):
    slots = owners.shape[1]
    named = lax.broadcasted_iota(jnp.int32, (peers, slots), 0) == owners
    named = jnp.where(named, 1.0, 0.0)
    earlier = (
        lax.broadcasted_iota(jnp.int32, (slots, slots), 0)
        < lax.broadcasted_iota(jnp.int32, (slots, slots), 1)
    )
    rank = dot(named.astype(BF16), jnp.where(earlier, 1.0, 0.0).astype(BF16))
    return named, jnp.sum(named * rank, axis=0, keepdims=True).astype(jnp.int32)


def request_kernel(tile_in, owner_in, row_in, ids_ref, tile_ref, owner_ref, row_ref, sems):
    copies = [
        pltpu.make_async_copy(tile_in, tile_ref, sems.at[0]),
        pltpu.make_async_copy(owner_in, owner_ref, sems.at[1]),
        pltpu.make_async_copy(row_in, row_ref, sems.at[2]),
    ]
    for copy in copies:
        copy.start()
    for copy in copies:
        copy.wait()
    peers = ids_ref.shape[0]
    first = tile_ref[0, 0]
    owners = in_edge_order(first, owner_ref[...])
    rows = in_edge_order(first, row_ref[...])
    named, place = slot_places(owners, peers)
    spot = lax.broadcasted_iota(jnp.int32, (LANES, rows.shape[1]), 0) == place
    spot = jnp.where(spot, 1.0, 0.0).astype(BF16)
    low = (rows % LANES).astype(F32)
    high = (rows // LANES).astype(F32)
    ids = dot((named * low).astype(BF16), spot, ROWS_T) + LANES * dot(
        (named * high).astype(BF16), spot, ROWS_T
    )
    ids_ref[...] = ids.astype(jnp.int32).reshape(ids_ref.shape)


def gather_kernel(ids_ref, table_ref, taken_ref, pick):
    table_rows, width = table_ref.shape
    peers = ids_ref.shape[0]
    ids = ids_ref[...].reshape(peers, LANES).astype(F32)
    ids = jnp.concatenate([ids, jnp.zeros((LANES - peers, LANES), F32)], axis=0)
    by_place = ids.T.astype(jnp.int32)
    columns = lax.broadcasted_iota(jnp.int32, (CAP, table_rows), 1)
    for g in range(peers):
        chosen = columns == by_place[:CAP, g : g + 1]
        pick[g * CAP : (g + 1) * CAP, :] = jnp.where(chosen, 1.0, 0.0).astype(BF16)
    part = peers // 4
    for start in range(0, peers, part):
        emb = dot(pick[start * CAP : (start + part) * CAP, :], table_ref[...])
        taken_ref[start : start + part] = emb.astype(BF16).reshape(part, CAP, width)


def coef_kernel(
    peers, node_rows, tile_in, owner_in, row_in, edge_in, all_ref, inside_ref, tile_ref, owner_ref,
    row_ref, edge_ref, sems
):
    copies = [
        pltpu.make_async_copy(tile_in, tile_ref, sems.at[0]),
        pltpu.make_async_copy(owner_in, owner_ref, sems.at[1]),
        pltpu.make_async_copy(row_in, row_ref, sems.at[2]),
        pltpu.make_async_copy(edge_in, edge_ref, sems.at[3]),
    ]
    for copy in copies:
        copy.start()
    for copy in copies:
        copy.wait()
    first = tile_ref[0, 0]
    owners = in_edge_order(first, owner_ref[...])
    rows = in_edge_order(first, row_ref[...])
    _, place = slot_places(owners, peers)
    target = owners * CAP + place
    at = lax.broadcasted_iota(jnp.int32, (peers * CAP, target.shape[1]), 0) == target
    moved = jnp.where(at, 1.0, 0.0)
    all_ref[...] = dot(edge_ref[...], moved.astype(BF16), ROWS_T).astype(BF16)
    kept = jnp.where(rows < node_rows, moved, 0.0).astype(BF16)
    inside_ref[...] = dot(edge_ref[...], kept, ROWS_T).astype(BF16)


def forward_kernel(
    pulled_ref,
    all_ref,
    feats_ref,
    weight_ref,
    grad_ref,
    out_ref,
    pre_ref,
    own_ref,
    away_ref,
):
    width = feats_ref.shape[1]
    half = width // 2
    pulled = pulled_ref[...].reshape(-1, width)
    mixed = (feats_ref[...].astype(F32) + dot(all_ref[...], pulled)).astype(BF16)
    pre = dot(mixed, weight_ref[...])
    gate = jax.nn.sigmoid(pre)
    grad_pre = (grad_ref[...].astype(F32) * gate * (1.0 + pre * (1.0 - gate))).astype(BF16)
    second_core = lax.axis_index("hist") % 2 == 1
    left, right = grad_pre[:, :half], grad_pre[:, half:]
    own_ref[:, :width] = mixed
    own_ref[:, width:] = jnp.where(second_core, right, left)
    away_ref[:, :width] = mixed
    away_ref[:, width:] = jnp.where(second_core, left, right)
    pre_ref[...] = grad_pre
    out_ref[...] = (pre * gate).astype(BF16)


def term_kernel(peers, width, own_ref, away_ref, term_ref):
    mixed = jnp.concatenate([own_ref[:, :width], away_ref[:, :width]], axis=0)
    grad_pre = jnp.concatenate([own_ref[:, width:], away_ref[:, width:]], axis=0)
    share = width // peers
    step = 8
    term = dot(mixed, grad_pre, COLS_T)
    for peer in range(peers):
        blocks = [
            term[peer * share + i : peer * share + i + step, :] for i in range(0, share, step)
        ]
        term_ref[peer] = jnp.concatenate(blocks, axis=1).astype(BF16)


def backward_kernel(
    pre_ref, weight_ref, inside_ref, pick_in, history_in, send_ref, mixed_ref, pick, aux, sems
):
    node_rows, width = mixed_ref.shape
    peers = send_ref.shape[0]
    load_pick = pltpu.make_async_copy(pick_in, pick, sems.at[0])
    load_aux = pltpu.make_async_copy(history_in.at[:, width:], aux, sems.at[1])
    load_pick.start()
    load_aux.start()
    grad_mixed = dot(pre_ref[...], weight_ref[...], ROWS_T).astype(BF16)
    mixed_ref[...] = grad_mixed
    slot_grad = dot(inside_ref[...], grad_mixed, COLS_T).astype(BF16)
    send_ref[:, :, :width] = slot_grad.reshape(peers, CAP, width)
    load_pick.wait()
    load_aux.wait()
    taken = dot(pick[:, node_rows:], aux[...]).astype(BF16)
    send_ref[:, :, width:] = taken.reshape(peers, CAP, width)


def weight_kernel(terms_ref, sum_ref):
    peers, step = terms_ref.shape[:2]
    for core in range(2):
        total = terms_ref[core].astype(F32)
        for peer in range(core + 2, peers, 2):
            total = total + terms_ref[peer].astype(F32)
        total = total.astype(BF16)
        for plane in range(sum_ref.shape[0]):
            sum_ref[plane, core * step : (core + 1) * step, :] = total


def add_kernel(near_ref, sum_ref):
    sum_ref[...] = jnp.sum(near_ref[...].astype(F32), axis=0).astype(BF16)


def share_kernel(a_ref, b_ref, c_ref, d_ref, share_ref):
    total = a_ref[...].astype(F32) + b_ref[...].astype(F32)
    total = total + (c_ref[...].astype(F32) + d_ref[...].astype(F32))
    share, width = share_ref.shape
    half = width // 2
    step = total.shape[0] // 2
    for i in range(share // step):
        for core in range(2):
            share_ref[i * step : (i + 1) * step, core * half : (core + 1) * half] = total[
                core * step : (core + 1) * step, i * half : (i + 1) * half
            ]


def final_kernel(back_ref, pick_ref, all_ref, mixed_ref, grad_ref):
    peers = back_ref.shape[0]
    node_rows, width = mixed_ref.shape
    slots = back_ref[:, :, :width].reshape(peers * CAP, width)
    aux = back_ref[:, :, width:].reshape(peers * CAP, width)
    returned = dot(pick_ref[:, :node_rows], slots, COLS_T)
    compensation = dot(all_ref[...], aux)
    total = mixed_ref[...].astype(F32) + returned + compensation
    grad_ref[...] = total.astype(BF16)


def call(kernel, out_shape, *args, smem=(), hbm=(), hbm_out=(), scratch=(), vmem=32, cost=None):
    spaces = [
        pltpu.SMEM if i in smem else pltpu.HBM if i in hbm else pltpu.VMEM
        for i in range(len(args))
    ]
    single = not isinstance(out_shape, (list, tuple))
    out_shape = [out_shape] if single else out_shape
    out_spaces = [pltpu.HBM if i in hbm_out else pltpu.VMEM for i in range(len(out_shape))]
    result = pl.pallas_call(
        kernel,
        out_shape=out_shape,
        in_specs=[pl.BlockSpec(memory_space=space) for space in spaces],
        out_specs=[pl.BlockSpec(memory_space=space) for space in out_spaces],
        scratch_shapes=list(scratch),
        compiler_params=pltpu.CompilerParams(vmem_limit_bytes=vmem << 20),
        cost_estimate=cost,
    )(*args)
    return result[0] if single else result


def swap(values, axis="hist", groups=None):
    return lax.all_to_all(
        values, axis, split_axis=0, concat_axis=0, tiled=True, axis_index_groups=groups
    )


def shift(values, axis, by):
    count = lax.axis_size(axis)
    return lax.ppermute(values, axis, [(i, (i + by) % count) for i in range(count)])


def body(feats, history, weight, edge_coef, tile_map, nbr_owner, nbr_row, grad_out):
    peers = lax.axis_size("hist")
    planes = lax.axis_size("batch")
    node_rows, width = feats.shape[1:]
    table_rows = history.shape[0]
    slots = nbr_row.shape[1]
    assert 2 * slots // peers == CAP and planes == 16
    share = width // peers
    shape = jax.ShapeDtypeStruct
    owners = nbr_owner.reshape(1, slots)
    ids = call(
        request_kernel,
        shape((peers, 1, LANES), jnp.int32),
        tile_map,
        owners,
        nbr_row,
        hbm=(0, 1, 2),
        vmem=60,
        scratch=(
            pltpu.SMEM(tile_map.shape, jnp.int32),
            pltpu.VMEM(owners.shape, jnp.int32),
            pltpu.VMEM(nbr_row.shape, jnp.int32),
            pltpu.SemaphoreType.DMA((3,)),
        ),
    )
    received = swap(ids)
    coef, coef_inside = call(
        functools.partial(coef_kernel, peers, node_rows),
        [shape((node_rows, peers * CAP), BF16)] * 2,
        tile_map,
        owners,
        nbr_row,
        edge_coef[0],
        hbm=(0, 1, 2, 3),
        vmem=60,
        scratch=(
            pltpu.SMEM(tile_map.shape, jnp.int32),
            pltpu.VMEM(owners.shape, jnp.int32),
            pltpu.VMEM(nbr_row.shape, jnp.int32),
            pltpu.VMEM(edge_coef.shape[1:], BF16),
            pltpu.SemaphoreType.DMA((4,)),
        ),
    )
    table = node_rows + table_rows
    received, coef, coef_inside = lax.optimization_barrier((received, coef, coef_inside))
    taken, pick = call(
        gather_kernel,
        [shape((peers, CAP, width), BF16), shape((peers * CAP, table), BF16)],
        received,
        jnp.concatenate([feats[0], history[:, :width]], axis=0),
    )
    pulled = swap(taken)
    out_rows, grad_pre, own, away = call(
        forward_kernel,
        [
            shape((node_rows, width), BF16),
            shape((node_rows, width), BF16),
            shape((node_rows, width + width // 2), BF16),
            shape((node_rows, width + width // 2), BF16),
        ],
        pulled,
        coef,
        feats[0],
        weight,
        grad_out[0],
    )
    away = lax.ppermute(away, "hist", [(i, i ^ 1) for i in range(peers)])
    terms = call(
        functools.partial(term_kernel, peers, width),
        shape((peers, 8, share * width // 16), BF16),
        own,
        away,
    )
    grad_pre, terms = lax.optimization_barrier((grad_pre, terms))
    terms = swap(terms)
    sent, grad_mixed = call(
        backward_kernel,
        [shape((peers, CAP, 2 * width), BF16), shape((node_rows, width), BF16)],
        grad_pre,
        weight,
        coef_inside,
        pick,
        history,
        hbm=(3, 4),
        scratch=(
            pltpu.VMEM((peers * CAP, table), BF16),
            pltpu.VMEM((table_rows, width), BF16),
            pltpu.SemaphoreType.DMA((2,)),
        ),
    )
    side = 4
    near = [[a * side + i for i in range(side)] for a in range(planes // side)]
    term = call(weight_kernel, shape((side, 16, share * width // 16), BF16), terms)
    term = swap(term, "batch", near)
    sent, term = lax.optimization_barrier((sent, term))
    back = swap(sent)
    term = call(add_kernel, shape(term.shape[1:], BF16), term)
    far = [shift(term, "batch", by) for by in (8, 4, -4)]
    weight_share = call(share_kernel, shape((share, width), F32), term, *far)
    grad_rows = call(
        final_kernel, shape((node_rows, width), BF16), back, pick, coef, grad_mixed
    )
    return (out_rows[None], grad_rows[None], weight_share)


def solution(mesh):
    return jax.shard_map(
        body,
        mesh=mesh,
        in_specs=(
            P(("batch", "hist"), None, None),
            P("hist", None),
            P(),
            P(("batch", "hist"), None, None),
            P(("batch", "hist"), None),
            P(("batch", "hist"), None, None),
            P(("batch", "hist"), None),
            P(("batch", "hist"), None, None),
        ),
        out_specs=(
            P(("batch", "hist"), None, None),
            P(("batch", "hist"), None, None),
            P("hist", None),
        ),
        check_vma=False,
    )
```

```python
import functools

import jax
import jax.numpy as jnp
from jax import lax
from jax.experimental import pallas as pl
from jax.experimental.pallas import tpu as pltpu
from jax.sharding import PartitionSpec as P

F32 = jnp.float32
BF16 = jnp.bfloat16
LANES = 128
CAP = 16
ROWS_T = (((1,), (1,)), ((), ()))
COLS_T = (((0,), (0,)), ((), ()))


def dot(a, b, dims=(((1,), (0,)), ((), ()))):
    return lax.dot_general(a, b, dims, preferred_element_type=F32)


def in_edge_order(first_tile, values):
    half = values.shape[1] // 2
    swapped = jnp.concatenate([values[:, half:], values[:, :half]], axis=1)
    return jnp.where(first_tile == 0, values, swapped)


def slot_places(owners, peers):
    slots = owners.shape[1]
    named = lax.broadcasted_iota(jnp.int32, (peers, slots), 0) == owners
    named = jnp.where(named, 1.0, 0.0)
    earlier = (
        lax.broadcasted_iota(jnp.int32, (slots, slots), 0)
        < lax.broadcasted_iota(jnp.int32, (slots, slots), 1)
    )
    rank = dot(named.astype(BF16), jnp.where(earlier, 1.0, 0.0).astype(BF16))
    return named, jnp.sum(named * rank, axis=0, keepdims=True).astype(jnp.int32)


def request_kernel(tile_in, owner_in, row_in, ids_ref, tile_ref, owner_ref, row_ref, sems):
    copies = [
        pltpu.make_async_copy(tile_in, tile_ref, sems.at[0]),
        pltpu.make_async_copy(owner_in, owner_ref, sems.at[1]),
        pltpu.make_async_copy(row_in, row_ref, sems.at[2]),
    ]
    for copy in copies:
        copy.start()
    for copy in copies:
        copy.wait()
    peers = ids_ref.shape[0]
    first = tile_ref[0, 0]
    owners = in_edge_order(first, owner_ref[...])
    rows = in_edge_order(first, row_ref[...])
    named, place = slot_places(owners, peers)
    spot = lax.broadcasted_iota(jnp.int32, (LANES, rows.shape[1]), 0) == place
    spot = jnp.where(spot, 1.0, 0.0).astype(BF16)
    low = (rows % LANES).astype(F32)
    high = (rows // LANES).astype(F32)
    ids = dot((named * low).astype(BF16), spot, ROWS_T) + LANES * dot(
        (named * high).astype(BF16), spot, ROWS_T
    )
    ids_ref[...] = ids.astype(jnp.int32).reshape(ids_ref.shape)


def gather_kernel(ids_ref, table_ref, taken_ref, pick):
    table_rows, width = table_ref.shape
    peers = ids_ref.shape[0]
    ids = ids_ref[...].reshape(peers, LANES).astype(F32)
    ids = jnp.concatenate([ids, jnp.zeros((LANES - peers, LANES), F32)], axis=0)
    by_place = ids.T.astype(jnp.int32)
    columns = lax.broadcasted_iota(jnp.int32, (CAP, table_rows), 1)
    for g in range(peers):
        chosen = columns == by_place[:CAP, g : g + 1]
        pick[g * CAP : (g + 1) * CAP, :] = jnp.where(chosen, 1.0, 0.0).astype(BF16)
    part = peers // 4
    for start in range(0, peers, part):
        emb = dot(pick[start * CAP : (start + part) * CAP, :], table_ref[...])
        taken_ref[start : start + part] = emb.astype(BF16).reshape(part, CAP, width)


def coef_kernel(
    peers, node_rows, tile_in, owner_in, row_in, edge_in, all_ref, inside_ref, tile_ref, owner_ref,
    row_ref, edge_ref, sems
):
    copies = [
        pltpu.make_async_copy(tile_in, tile_ref, sems.at[0]),
        pltpu.make_async_copy(owner_in, owner_ref, sems.at[1]),
        pltpu.make_async_copy(row_in, row_ref, sems.at[2]),
        pltpu.make_async_copy(edge_in, edge_ref, sems.at[3]),
    ]
    for copy in copies:
        copy.start()
    for copy in copies:
        copy.wait()
    first = tile_ref[0, 0]
    owners = in_edge_order(first, owner_ref[...])
    rows = in_edge_order(first, row_ref[...])
    _, place = slot_places(owners, peers)
    target = owners * CAP + place
    at = lax.broadcasted_iota(jnp.int32, (peers * CAP, target.shape[1]), 0) == target
    moved = jnp.where(at, 1.0, 0.0)
    all_ref[...] = dot(edge_ref[...], moved.astype(BF16), ROWS_T).astype(BF16)
    kept = jnp.where(rows < node_rows, moved, 0.0).astype(BF16)
    inside_ref[...] = dot(edge_ref[...], kept, ROWS_T).astype(BF16)


def forward_kernel(
    pulled_ref,
    all_ref,
    feats_ref,
    weight_ref,
    grad_ref,
    out_ref,
    pre_ref,
    own_ref,
    away_ref,
):
    width = feats_ref.shape[1]
    half = width // 2
    pulled = pulled_ref[...].reshape(-1, width)
    mixed = (feats_ref[...].astype(F32) + dot(all_ref[...], pulled)).astype(BF16)
    pre = dot(mixed, weight_ref[...])
    gate = jax.nn.sigmoid(pre)
    grad_pre = (grad_ref[...].astype(F32) * gate * (1.0 + pre * (1.0 - gate))).astype(BF16)
    second_core = lax.axis_index("hist") % 2 == 1
    left, right = grad_pre[:, :half], grad_pre[:, half:]
    own_ref[:, :width] = mixed
    own_ref[:, width:] = jnp.where(second_core, right, left)
    away_ref[:, :width] = mixed
    away_ref[:, width:] = jnp.where(second_core, left, right)
    pre_ref[...] = grad_pre
    out_ref[...] = (pre * gate).astype(BF16)


def term_kernel(peers, width, own_ref, away_ref, term_ref):
    mixed = jnp.concatenate([own_ref[:, :width], away_ref[:, :width]], axis=0)
    grad_pre = jnp.concatenate([own_ref[:, width:], away_ref[:, width:]], axis=0)
    share = width // peers
    step = 8
    term = dot(mixed, grad_pre, COLS_T)
    for peer in range(peers):
        blocks = [
            term[peer * share + i : peer * share + i + step, :] for i in range(0, share, step)
        ]
        term_ref[peer] = jnp.concatenate(blocks, axis=1).astype(BF16)


def backward_kernel(
    pre_ref, weight_ref, inside_ref, pick_in, history_in, send_ref, mixed_ref, pick, aux, sems
):
    node_rows, width = mixed_ref.shape
    peers = send_ref.shape[0]
    load_pick = pltpu.make_async_copy(pick_in, pick, sems.at[0])
    load_aux = pltpu.make_async_copy(history_in.at[:, width:], aux, sems.at[1])
    load_pick.start()
    load_aux.start()
    grad_mixed = dot(pre_ref[...], weight_ref[...], ROWS_T).astype(BF16)
    mixed_ref[...] = grad_mixed
    slot_grad = dot(inside_ref[...], grad_mixed, COLS_T).astype(BF16)
    send_ref[:, :, :width] = slot_grad.reshape(peers, CAP, width)
    load_pick.wait()
    load_aux.wait()
    taken = dot(pick[:, node_rows:], aux[...]).astype(BF16)
    send_ref[:, :, width:] = taken.reshape(peers, CAP, width)


def weight_kernel(terms_ref, sum_ref):
    peers, step = terms_ref.shape[:2]
    for core in range(2):
        total = terms_ref[core].astype(F32)
        for peer in range(core + 2, peers, 2):
            total = total + terms_ref[peer].astype(F32)
        total = total.astype(BF16)
        for plane in range(sum_ref.shape[0]):
            sum_ref[plane, core * step : (core + 1) * step, :] = total


def add_kernel(near_ref, sum_ref):
    sum_ref[...] = jnp.sum(near_ref[...].astype(F32), axis=0).astype(BF16)


def final_kernel(
    back_ref, pick_ref, all_ref, mixed_ref, far_ref, grad_ref, share_ref
):
    total = jnp.sum(far_ref[...].astype(F32), axis=0)
    share, width = share_ref.shape
    half = width // 2
    step = total.shape[0] // 2
    for i in range(share // step):
        for core in range(2):
            share_ref[i * step : (i + 1) * step, core * half : (core + 1) * half] = total[
                core * step : (core + 1) * step, i * half : (i + 1) * half
            ]
    peers = back_ref.shape[0]
    node_rows = mixed_ref.shape[0]
    slots = back_ref[:, :, :width].reshape(peers * CAP, width)
    aux = back_ref[:, :, width:].reshape(peers * CAP, width)
    returned = dot(pick_ref[:, :node_rows], slots, COLS_T)
    compensation = dot(all_ref[...], aux)
    grad = mixed_ref[...].astype(F32) + returned + compensation
    grad_ref[...] = grad.astype(BF16)


def call(kernel, out_shape, *args, smem=(), hbm=(), hbm_out=(), scratch=(), vmem=32, cost=None):
    spaces = [
        pltpu.SMEM if i in smem else pltpu.HBM if i in hbm else pltpu.VMEM
        for i in range(len(args))
    ]
    single = not isinstance(out_shape, (list, tuple))
    out_shape = [out_shape] if single else out_shape
    out_spaces = [pltpu.HBM if i in hbm_out else pltpu.VMEM for i in range(len(out_shape))]
    result = pl.pallas_call(
        kernel,
        out_shape=out_shape,
        in_specs=[pl.BlockSpec(memory_space=space) for space in spaces],
        out_specs=[pl.BlockSpec(memory_space=space) for space in out_spaces],
        scratch_shapes=list(scratch),
        compiler_params=pltpu.CompilerParams(vmem_limit_bytes=vmem << 20),
        cost_estimate=cost,
    )(*args)
    return result[0] if single else result


def swap(values, axis="hist", groups=None):
    return lax.all_to_all(
        values, axis, split_axis=0, concat_axis=0, tiled=True, axis_index_groups=groups
    )


def body(feats, history, weight, edge_coef, tile_map, nbr_owner, nbr_row, grad_out):
    peers = lax.axis_size("hist")
    planes = lax.axis_size("batch")
    node_rows, width = feats.shape[1:]
    table_rows = history.shape[0]
    slots = nbr_row.shape[1]
    assert 2 * slots // peers == CAP and planes == 16
    share = width // peers
    shape = jax.ShapeDtypeStruct
    owners = nbr_owner.reshape(1, slots)
    ids = call(
        request_kernel,
        shape((peers, 1, LANES), jnp.int32),
        tile_map,
        owners,
        nbr_row,
        hbm=(0, 1, 2),
        vmem=60,
        scratch=(
            pltpu.SMEM(tile_map.shape, jnp.int32),
            pltpu.VMEM(owners.shape, jnp.int32),
            pltpu.VMEM(nbr_row.shape, jnp.int32),
            pltpu.SemaphoreType.DMA((3,)),
        ),
    )
    received = swap(ids)
    coef, coef_inside = call(
        functools.partial(coef_kernel, peers, node_rows),
        [shape((node_rows, peers * CAP), BF16)] * 2,
        tile_map,
        owners,
        nbr_row,
        edge_coef[0],
        hbm=(0, 1, 2, 3),
        vmem=60,
        scratch=(
            pltpu.SMEM(tile_map.shape, jnp.int32),
            pltpu.VMEM(owners.shape, jnp.int32),
            pltpu.VMEM(nbr_row.shape, jnp.int32),
            pltpu.VMEM(edge_coef.shape[1:], BF16),
            pltpu.SemaphoreType.DMA((4,)),
        ),
    )
    table = node_rows + table_rows
    received, coef, coef_inside = lax.optimization_barrier((received, coef, coef_inside))
    taken, pick = call(
        gather_kernel,
        [shape((peers, CAP, width), BF16), shape((peers * CAP, table), BF16)],
        received,
        jnp.concatenate([feats[0], history[:, :width]], axis=0),
    )
    pulled = swap(taken)
    out_rows, grad_pre, own, away = call(
        forward_kernel,
        [
            shape((node_rows, width), BF16),
            shape((node_rows, width), BF16),
            shape((node_rows, width + width // 2), BF16),
            shape((node_rows, width + width // 2), BF16),
        ],
        pulled,
        coef,
        feats[0],
        weight,
        grad_out[0],
    )
    away = lax.ppermute(away, "hist", [(i, i ^ 1) for i in range(peers)])
    terms = call(
        functools.partial(term_kernel, peers, width),
        shape((peers, 8, share * width // 16), BF16),
        own,
        away,
    )
    grad_pre, terms = lax.optimization_barrier((grad_pre, terms))
    terms = swap(terms)
    sent, grad_mixed = call(
        backward_kernel,
        [shape((peers, CAP, 2 * width), BF16), shape((node_rows, width), BF16)],
        grad_pre,
        weight,
        coef_inside,
        pick,
        history,
        hbm=(3, 4),
        scratch=(
            pltpu.VMEM((peers * CAP, table), BF16),
            pltpu.VMEM((table_rows, width), BF16),
            pltpu.SemaphoreType.DMA((2,)),
        ),
    )
    side = 4
    near = [[a * side + i for i in range(side)] for a in range(planes // side)]
    term = call(weight_kernel, shape((side, 16, share * width // 16), BF16), terms)
    term = swap(term, "batch", near)
    sent, term = lax.optimization_barrier((sent, term))
    back = swap(sent)
    term = call(add_kernel, shape(term.shape[1:], BF16), term)
    far = [[a + side * i for i in range(planes // side)] for a in range(side)]
    term = lax.all_gather(term, "batch", axis=0, axis_index_groups=far)
    grad_rows, weight_share = call(
        final_kernel,
        [shape((node_rows, width), BF16), shape((share, width), F32)],
        back,
        pick,
        coef,
        grad_mixed,
        term,
    )
    return (out_rows[None], grad_rows[None], weight_share)


def solution(mesh):
    return jax.shard_map(
        body,
        mesh=mesh,
        in_specs=(
            P(("batch", "hist"), None, None),
            P("hist", None),
            P(),
            P(("batch", "hist"), None, None),
            P(("batch", "hist"), None),
            P(("batch", "hist"), None, None),
            P(("batch", "hist"), None),
            P(("batch", "hist"), None, None),
        ),
        out_specs=(
            P(("batch", "hist"), None, None),
            P(("batch", "hist"), None, None),
            P("hist", None),
        ),
        check_vma=False,
    )
```

```python
import functools

import jax
import jax.numpy as jnp
from jax import lax
from jax.experimental import pallas as pl
from jax.experimental.pallas import tpu as pltpu
from jax.sharding import PartitionSpec as P

F32 = jnp.float32
BF16 = jnp.bfloat16
LANES = 128
CAP = 16
ROWS_T = (((1,), (1,)), ((), ()))
COLS_T = (((0,), (0,)), ((), ()))


def dot(a, b, dims=(((1,), (0,)), ((), ()))):
    return lax.dot_general(a, b, dims, preferred_element_type=F32)


def in_edge_order(first_tile, values):
    half = values.shape[1] // 2
    swapped = jnp.concatenate([values[:, half:], values[:, :half]], axis=1)
    return jnp.where(first_tile == 0, values, swapped)


def earlier_slots(slots):
    earlier = (
        lax.broadcasted_iota(jnp.int32, (slots, slots), 0)
        < lax.broadcasted_iota(jnp.int32, (slots, slots), 1)
    )
    return jnp.where(earlier, 1.0, 0.0).astype(BF16)


def slot_places(owners, peers, earlier):
    slots = owners.shape[1]
    named = lax.broadcasted_iota(jnp.int32, (peers, slots), 0) == owners
    named = jnp.where(named, 1.0, 0.0)
    rank = dot(named.astype(BF16), earlier)
    return named, jnp.sum(named * rank, axis=0, keepdims=True).astype(jnp.int32)


def request_kernel(tile_in, owner_in, row_in, ids_ref, tile_ref, owner_ref, row_ref, sems):
    copies = [
        pltpu.make_async_copy(tile_in, tile_ref, sems.at[0]),
        pltpu.make_async_copy(owner_in, owner_ref, sems.at[1]),
        pltpu.make_async_copy(row_in, row_ref, sems.at[2]),
    ]
    for copy in copies:
        copy.start()
    earlier = earlier_slots(owner_ref.shape[1])
    for copy in copies:
        copy.wait()
    peers = ids_ref.shape[0]
    first = tile_ref[0, 0]
    owners = in_edge_order(first, owner_ref[...])
    rows = in_edge_order(first, row_ref[...])
    named, place = slot_places(owners, peers, earlier)
    spot = lax.broadcasted_iota(jnp.int32, (LANES, rows.shape[1]), 0) == place
    spot = jnp.where(spot, 1.0, 0.0).astype(BF16)
    low = (rows % LANES).astype(F32)
    high = (rows // LANES).astype(F32)
    ids = dot((named * low).astype(BF16), spot, ROWS_T) + LANES * dot(
        (named * high).astype(BF16), spot, ROWS_T
    )
    ids_ref[...] = ids.astype(jnp.int32).reshape(ids_ref.shape)


def gather_kernel(ids_ref, table_ref, taken_ref, pick):
    table_rows, width = table_ref.shape
    peers = ids_ref.shape[0]
    ids = ids_ref[...].reshape(peers, LANES).astype(F32)
    ids = jnp.concatenate([ids, jnp.zeros((LANES - peers, LANES), F32)], axis=0)
    by_place = ids.T.astype(jnp.int32)
    columns = lax.broadcasted_iota(jnp.int32, (CAP, table_rows), 1)
    for g in range(peers):
        chosen = columns == by_place[:CAP, g : g + 1]
        pick[g * CAP : (g + 1) * CAP, :] = jnp.where(chosen, 1.0, 0.0).astype(BF16)
    part = peers // 4
    for start in range(0, peers, part):
        emb = dot(pick[start * CAP : (start + part) * CAP, :], table_ref[...])
        taken_ref[start : start + part] = emb.astype(BF16).reshape(part, CAP, width)


def coef_kernel(
    peers, node_rows, tile_in, owner_in, row_in, edge_in, all_ref, inside_ref, tile_ref, owner_ref,
    row_ref, edge_ref, sems
):
    copies = [
        pltpu.make_async_copy(tile_in, tile_ref, sems.at[0]),
        pltpu.make_async_copy(owner_in, owner_ref, sems.at[1]),
        pltpu.make_async_copy(row_in, row_ref, sems.at[2]),
        pltpu.make_async_copy(edge_in, edge_ref, sems.at[3]),
    ]
    for copy in copies:
        copy.start()
    earlier = earlier_slots(owner_ref.shape[1])
    for copy in copies:
        copy.wait()
    first = tile_ref[0, 0]
    owners = in_edge_order(first, owner_ref[...])
    rows = in_edge_order(first, row_ref[...])
    _, place = slot_places(owners, peers, earlier)
    target = owners * CAP + place
    at = lax.broadcasted_iota(jnp.int32, (peers * CAP, target.shape[1]), 0) == target
    moved = jnp.where(at, 1.0, 0.0)
    all_ref[...] = dot(edge_ref[...], moved.astype(BF16), ROWS_T).astype(BF16)
    kept = jnp.where(rows < node_rows, moved, 0.0).astype(BF16)
    inside_ref[...] = dot(edge_ref[...], kept, ROWS_T).astype(BF16)


def forward_kernel(
    pulled_ref,
    all_ref,
    feats_ref,
    weight_ref,
    grad_ref,
    out_ref,
    pair_ref,
):
    width = feats_ref.shape[1]
    pulled = pulled_ref[...].reshape(-1, width)
    mixed = (feats_ref[...].astype(F32) + dot(all_ref[...], pulled)).astype(BF16)
    pre = dot(mixed, weight_ref[...])
    gate = jax.nn.sigmoid(pre)
    grad_pre = (grad_ref[...].astype(F32) * gate * (1.0 + pre * (1.0 - gate))).astype(BF16)
    pair_ref[:, :width] = mixed
    pair_ref[:, width:] = grad_pre
    out_ref[...] = (pre * gate).astype(BF16)


def term_kernel(peers, width, pairs_ref, term_ref):
    half = width // 2
    second_core = lax.axis_index("hist") % 2 == 1
    pairs = pairs_ref[...].reshape(-1, 2 * width)
    mixed = pairs[:, :width]
    left, right = pairs[:, width : width + half], pairs[:, width + half :]
    grad_pre = jnp.where(second_core, right, left)
    share = width // peers
    step = 8
    term = dot(mixed, grad_pre, COLS_T)
    for peer in range(peers):
        blocks = [
            term[peer * share + i : peer * share + i + step, :] for i in range(0, share, step)
        ]
        term_ref[peer] = jnp.concatenate(blocks, axis=1).astype(BF16)


def backward_kernel(
    pair_ref, weight_ref, inside_ref, pick_in, history_in, send_ref, mixed_ref, pick, aux, sems
):
    node_rows, width = mixed_ref.shape
    peers = send_ref.shape[0]
    load_pick = pltpu.make_async_copy(pick_in, pick, sems.at[0])
    load_aux = pltpu.make_async_copy(history_in.at[:, width:], aux, sems.at[1])
    load_pick.start()
    load_aux.start()
    grad_mixed = dot(pair_ref[:, width:], weight_ref[...], ROWS_T).astype(BF16)
    mixed_ref[...] = grad_mixed
    slot_grad = dot(inside_ref[...], grad_mixed, COLS_T).astype(BF16)
    send_ref[:, :, :width] = slot_grad.reshape(peers, CAP, width)
    load_pick.wait()
    load_aux.wait()
    taken = dot(pick[:, node_rows:], aux[...]).astype(BF16)
    send_ref[:, :, width:] = taken.reshape(peers, CAP, width)


def weight_kernel(terms_ref, sum_ref):
    peers, step = terms_ref.shape[:2]
    for core in range(2):
        total = terms_ref[core].astype(F32)
        for peer in range(core + 2, peers, 2):
            total = total + terms_ref[peer].astype(F32)
        total = total.astype(BF16)
        for plane in range(sum_ref.shape[0]):
            sum_ref[plane, core * step : (core + 1) * step, :] = total


def add_kernel(near_ref, sum_ref):
    sum_ref[...] = jnp.sum(near_ref[...].astype(F32), axis=0)


def final_kernel(
    back_ref, pick_ref, all_ref, mixed_ref, far_ref, grad_ref, share_ref
):
    total = jnp.sum(far_ref[...], axis=0)
    share, width = share_ref.shape
    half = width // 2
    step = total.shape[0] // 2
    for i in range(share // step):
        for core in range(2):
            share_ref[i * step : (i + 1) * step, core * half : (core + 1) * half] = total[
                core * step : (core + 1) * step, i * half : (i + 1) * half
            ]
    peers = back_ref.shape[0]
    node_rows = mixed_ref.shape[0]
    slots = back_ref[:, :, :width].reshape(peers * CAP, width)
    aux = back_ref[:, :, width:].reshape(peers * CAP, width)
    returned = dot(pick_ref[:, :node_rows], slots, COLS_T)
    compensation = dot(all_ref[...], aux)
    grad = mixed_ref[...].astype(F32) + returned + compensation
    grad_ref[...] = grad.astype(BF16)


def call(kernel, out_shape, *args, smem=(), hbm=(), hbm_out=(), scratch=(), vmem=32, cost=None):
    spaces = [
        pltpu.SMEM if i in smem else pltpu.HBM if i in hbm else pltpu.VMEM
        for i in range(len(args))
    ]
    single = not isinstance(out_shape, (list, tuple))
    out_shape = [out_shape] if single else out_shape
    out_spaces = [pltpu.HBM if i in hbm_out else pltpu.VMEM for i in range(len(out_shape))]
    result = pl.pallas_call(
        kernel,
        out_shape=out_shape,
        in_specs=[pl.BlockSpec(memory_space=space) for space in spaces],
        out_specs=[pl.BlockSpec(memory_space=space) for space in out_spaces],
        scratch_shapes=list(scratch),
        compiler_params=pltpu.CompilerParams(vmem_limit_bytes=vmem << 20),
        cost_estimate=cost,
    )(*args)
    return result[0] if single else result


def swap(values, axis="hist", groups=None):
    return lax.all_to_all(
        values, axis, split_axis=0, concat_axis=0, tiled=True, axis_index_groups=groups
    )


def body(feats, history, weight, edge_coef, tile_map, nbr_owner, nbr_row, grad_out):
    peers = lax.axis_size("hist")
    planes = lax.axis_size("batch")
    node_rows, width = feats.shape[1:]
    table_rows = history.shape[0]
    slots = nbr_row.shape[1]
    assert 2 * slots // peers == CAP and planes == 16
    share = width // peers
    shape = jax.ShapeDtypeStruct
    owners = nbr_owner.reshape(1, slots)
    ids = call(
        request_kernel,
        shape((peers, 1, LANES), jnp.int32),
        tile_map,
        owners,
        nbr_row,
        hbm=(0, 1, 2),
        vmem=60,
        scratch=(
            pltpu.SMEM(tile_map.shape, jnp.int32),
            pltpu.VMEM(owners.shape, jnp.int32),
            pltpu.VMEM(nbr_row.shape, jnp.int32),
            pltpu.SemaphoreType.DMA((3,)),
        ),
    )
    received = swap(ids)
    coef, coef_inside = call(
        functools.partial(coef_kernel, peers, node_rows),
        [shape((node_rows, peers * CAP), BF16)] * 2,
        tile_map,
        owners,
        nbr_row,
        edge_coef[0],
        hbm=(0, 1, 2, 3),
        vmem=60,
        scratch=(
            pltpu.SMEM(tile_map.shape, jnp.int32),
            pltpu.VMEM(owners.shape, jnp.int32),
            pltpu.VMEM(nbr_row.shape, jnp.int32),
            pltpu.VMEM(edge_coef.shape[1:], BF16),
            pltpu.SemaphoreType.DMA((4,)),
        ),
    )
    table = node_rows + table_rows
    received, coef, coef_inside = lax.optimization_barrier((received, coef, coef_inside))
    taken, pick = call(
        gather_kernel,
        [shape((peers, CAP, width), BF16), shape((peers * CAP, table), BF16)],
        received,
        jnp.concatenate([feats[0], history[:, :width]], axis=0),
    )
    pulled = swap(taken)
    out_rows, pair = call(
        forward_kernel,
        [shape((node_rows, width), BF16), shape((node_rows, 2 * width), BF16)],
        pulled,
        coef,
        feats[0],
        weight,
        grad_out[0],
    )
    chips = [[i, i + 1] for i in range(0, peers, 2)]
    pairs = lax.all_gather(pair, "hist", axis=0, axis_index_groups=chips)
    terms = call(
        functools.partial(term_kernel, peers, width),
        shape((peers, 8, share * width // 16), BF16),
        pairs,
    )
    pair, terms = lax.optimization_barrier((pair, terms))
    terms = swap(terms)
    sent, grad_mixed = call(
        backward_kernel,
        [shape((peers, CAP, 2 * width), BF16), shape((node_rows, width), BF16)],
        pair,
        weight,
        coef_inside,
        pick,
        history,
        hbm=(3, 4),
        scratch=(
            pltpu.VMEM((peers * CAP, table), BF16),
            pltpu.VMEM((table_rows, width), BF16),
            pltpu.SemaphoreType.DMA((2,)),
        ),
    )
    side = 4
    near = [[a * side + i for i in range(side)] for a in range(planes // side)]
    term = call(weight_kernel, shape((side, 16, share * width // 16), BF16), terms)
    term = swap(term, "batch", near)
    sent, term = lax.optimization_barrier((sent, term))
    back = swap(sent)
    term = call(add_kernel, shape(term.shape[1:], F32), term)
    far = [[a + side * i for i in range(planes // side)] for a in range(side)]
    term = lax.all_gather(term, "batch", axis=0, axis_index_groups=far)
    grad_rows, weight_share = call(
        final_kernel,
        [shape((node_rows, width), BF16), shape((share, width), F32)],
        back,
        pick,
        coef,
        grad_mixed,
        term,
    )
    return (out_rows[None], grad_rows[None], weight_share)


def solution(mesh):
    return jax.shard_map(
        body,
        mesh=mesh,
        in_specs=(
            P(("batch", "hist"), None, None),
            P("hist", None),
            P(),
            P(("batch", "hist"), None, None),
            P(("batch", "hist"), None),
            P(("batch", "hist"), None, None),
            P(("batch", "hist"), None),
            P(("batch", "hist"), None, None),
        ),
        out_specs=(
            P(("batch", "hist"), None, None),
            P(("batch", "hist"), None, None),
            P("hist", None),
        ),
        check_vma=False,
    )
```

```python
import functools

import jax
import jax.numpy as jnp
from jax import lax
from jax.experimental import pallas as pl
from jax.experimental.pallas import tpu as pltpu
from jax.sharding import PartitionSpec as P

F32 = jnp.float32
BF16 = jnp.bfloat16
LANES = 128
CAP = 16
ROWS_T = (((1,), (1,)), ((), ()))
COLS_T = (((0,), (0,)), ((), ()))


def dot(a, b, dims=(((1,), (0,)), ((), ()))):
    return lax.dot_general(a, b, dims, preferred_element_type=F32)


def in_edge_order(first_tile, values):
    half = values.shape[1] // 2
    swapped = jnp.concatenate([values[:, half:], values[:, :half]], axis=1)
    return jnp.where(first_tile == 0, values, swapped)


def earlier_slots(slots):
    earlier = (
        lax.broadcasted_iota(jnp.int32, (slots, slots), 0)
        < lax.broadcasted_iota(jnp.int32, (slots, slots), 1)
    )
    return jnp.where(earlier, 1.0, 0.0).astype(BF16)


def slot_places(owners, peers, earlier):
    slots = owners.shape[1]
    named = lax.broadcasted_iota(jnp.int32, (peers, slots), 0) == owners
    named = jnp.where(named, 1.0, 0.0)
    rank = dot(named.astype(BF16), earlier)
    return named, jnp.sum(named * rank, axis=0, keepdims=True).astype(jnp.int32)


def request_kernel(tile_in, owner_in, row_in, ids_ref, tile_ref, owner_ref, row_ref, sems):
    copies = [
        pltpu.make_async_copy(tile_in, tile_ref, sems.at[0]),
        pltpu.make_async_copy(owner_in, owner_ref, sems.at[1]),
        pltpu.make_async_copy(row_in, row_ref, sems.at[2]),
    ]
    for copy in copies:
        copy.start()
    earlier = earlier_slots(owner_ref.shape[1])
    for copy in copies:
        copy.wait()
    peers = ids_ref.shape[0]
    first = tile_ref[0, 0]
    owners = in_edge_order(first, owner_ref[...])
    rows = in_edge_order(first, row_ref[...])
    named, place = slot_places(owners, peers, earlier)
    spot = lax.broadcasted_iota(jnp.int32, (LANES, rows.shape[1]), 0) == place
    spot = jnp.where(spot, 1.0, 0.0).astype(BF16)
    low = (rows % LANES).astype(F32)
    high = (rows // LANES).astype(F32)
    ids = dot((named * low).astype(BF16), spot, ROWS_T) + LANES * dot(
        (named * high).astype(BF16), spot, ROWS_T
    )
    ids_ref[...] = ids.astype(jnp.int32).reshape(ids_ref.shape)


def gather_kernel(ids_ref, table_ref, taken_ref, pick):
    table_rows, width = table_ref.shape
    peers = ids_ref.shape[0]
    ids = ids_ref[...].reshape(peers, LANES).astype(F32)
    ids = jnp.concatenate([ids, jnp.zeros((LANES - peers, LANES), F32)], axis=0)
    by_place = ids.T.astype(jnp.int32)
    columns = lax.broadcasted_iota(jnp.int32, (CAP, table_rows), 1)
    for g in range(peers):
        chosen = columns == by_place[:CAP, g : g + 1]
        pick[g * CAP : (g + 1) * CAP, :] = jnp.where(chosen, 1.0, 0.0).astype(BF16)
    part = peers // 4
    for start in range(0, peers, part):
        emb = dot(pick[start * CAP : (start + part) * CAP, :], table_ref[...])
        taken_ref[start : start + part] = emb.astype(BF16).reshape(part, CAP, width)


def coef_kernel(
    peers, node_rows, tile_in, owner_in, row_in, edge_in, all_ref, inside_ref, tile_ref, owner_ref,
    row_ref, edge_ref, sems
):
    copies = [
        pltpu.make_async_copy(tile_in, tile_ref, sems.at[0]),
        pltpu.make_async_copy(owner_in, owner_ref, sems.at[1]),
        pltpu.make_async_copy(row_in, row_ref, sems.at[2]),
        pltpu.make_async_copy(edge_in, edge_ref, sems.at[3]),
    ]
    for copy in copies:
        copy.start()
    earlier = earlier_slots(owner_ref.shape[1])
    for copy in copies:
        copy.wait()
    first = tile_ref[0, 0]
    owners = in_edge_order(first, owner_ref[...])
    rows = in_edge_order(first, row_ref[...])
    _, place = slot_places(owners, peers, earlier)
    target = owners * CAP + place
    at = lax.broadcasted_iota(jnp.int32, (peers * CAP, target.shape[1]), 0) == target
    moved = jnp.where(at, 1.0, 0.0)
    all_ref[...] = dot(edge_ref[...], moved.astype(BF16), ROWS_T).astype(BF16)
    kept = jnp.where(rows < node_rows, moved, 0.0).astype(BF16)
    inside_ref[...] = dot(edge_ref[...], kept, ROWS_T).astype(BF16)


def forward_kernel(
    pulled_ref,
    all_ref,
    feats_ref,
    weight_ref,
    grad_ref,
    out_ref,
    pair_ref,
):
    width = feats_ref.shape[1]
    pulled = pulled_ref[...].reshape(-1, width)
    mixed = (feats_ref[...].astype(F32) + dot(all_ref[...], pulled)).astype(BF16)
    pre = dot(mixed, weight_ref[...])
    gate = jax.nn.sigmoid(pre)
    grad_pre = (grad_ref[...].astype(F32) * gate * (1.0 + pre * (1.0 - gate))).astype(BF16)
    pair_ref[:, :width] = mixed
    pair_ref[:, width:] = grad_pre
    out_ref[...] = (pre * gate).astype(BF16)


def term_kernel(peers, width, pairs_ref, term_ref):
    half = width // 2
    second_core = lax.axis_index("hist") % 2 == 1
    pairs = pairs_ref[...].reshape(-1, 2 * width)
    mixed = pairs[:, :width]
    left, right = pairs[:, width : width + half], pairs[:, width + half :]
    grad_pre = jnp.where(second_core, right, left)
    share = width // peers
    step = 8
    term = dot(mixed, grad_pre, COLS_T)
    for peer in range(peers):
        blocks = [
            term[peer * share + i : peer * share + i + step, :] for i in range(0, share, step)
        ]
        term_ref[peer] = jnp.concatenate(blocks, axis=1).astype(BF16)


def backward_kernel(
    pair_ref, weight_ref, inside_ref, pick_in, history_in, send_ref, mixed_ref, pick, aux, sems
):
    node_rows, width = mixed_ref.shape
    peers = send_ref.shape[0]
    load_pick = pltpu.make_async_copy(pick_in, pick, sems.at[0])
    load_aux = pltpu.make_async_copy(history_in.at[:, width:], aux, sems.at[1])
    load_pick.start()
    load_aux.start()
    grad_mixed = dot(pair_ref[:, width:], weight_ref[...], ROWS_T).astype(BF16)
    mixed_ref[...] = grad_mixed
    slot_grad = dot(inside_ref[...], grad_mixed, COLS_T).astype(BF16)
    send_ref[:, :, :width] = slot_grad.reshape(peers, CAP, width)
    load_pick.wait()
    load_aux.wait()
    taken = dot(pick[:, node_rows:], aux[...]).astype(BF16)
    send_ref[:, :, width:] = taken.reshape(peers, CAP, width)


def weight_kernel(terms_ref, sum_ref):
    peers, step = terms_ref.shape[:2]
    for core in range(2):
        total = terms_ref[core].astype(F32)
        for peer in range(core + 2, peers, 2):
            total = total + terms_ref[peer].astype(F32)
        total = total.astype(BF16)
        for plane in range(sum_ref.shape[0]):
            sum_ref[plane, core * step : (core + 1) * step, :] = total


def add_kernel(near_ref, sum_ref):
    sum_ref[...] = jnp.sum(near_ref[...].astype(F32), axis=0).astype(BF16)


def final_kernel(
    back_ref, pick_ref, all_ref, mixed_ref, far_ref, grad_ref, share_ref
):
    total = jnp.sum(far_ref[...].astype(F32), axis=0)
    share, width = share_ref.shape
    half = width // 2
    step = total.shape[0] // 2
    for i in range(share // step):
        for core in range(2):
            share_ref[i * step : (i + 1) * step, core * half : (core + 1) * half] = total[
                core * step : (core + 1) * step, i * half : (i + 1) * half
            ]
    peers = back_ref.shape[0]
    node_rows = mixed_ref.shape[0]
    slots = back_ref[:, :, :width].reshape(peers * CAP, width)
    aux = back_ref[:, :, width:].reshape(peers * CAP, width)
    returned = dot(pick_ref[:, :node_rows], slots, COLS_T)
    compensation = dot(all_ref[...], aux)
    grad = mixed_ref[...].astype(F32) + returned + compensation
    grad_ref[...] = grad.astype(BF16)


def call(kernel, out_shape, *args, smem=(), hbm=(), hbm_out=(), scratch=(), vmem=32, cost=None):
    spaces = [
        pltpu.SMEM if i in smem else pltpu.HBM if i in hbm else pltpu.VMEM
        for i in range(len(args))
    ]
    single = not isinstance(out_shape, (list, tuple))
    out_shape = [out_shape] if single else out_shape
    out_spaces = [pltpu.HBM if i in hbm_out else pltpu.VMEM for i in range(len(out_shape))]
    result = pl.pallas_call(
        kernel,
        out_shape=out_shape,
        in_specs=[pl.BlockSpec(memory_space=space) for space in spaces],
        out_specs=[pl.BlockSpec(memory_space=space) for space in out_spaces],
        scratch_shapes=list(scratch),
        compiler_params=pltpu.CompilerParams(vmem_limit_bytes=vmem << 20),
        cost_estimate=cost,
    )(*args)
    return result[0] if single else result


def swap(values, axis="hist", groups=None):
    return lax.all_to_all(
        values, axis, split_axis=0, concat_axis=0, tiled=True, axis_index_groups=groups
    )


def body(feats, history, weight, edge_coef, tile_map, nbr_owner, nbr_row, grad_out):
    peers = lax.axis_size("hist")
    planes = lax.axis_size("batch")
    node_rows, width = feats.shape[1:]
    table_rows = history.shape[0]
    slots = nbr_row.shape[1]
    assert 2 * slots // peers == CAP and planes == 16
    share = width // peers
    shape = jax.ShapeDtypeStruct
    owners = nbr_owner.reshape(1, slots)
    ids = call(
        request_kernel,
        shape((peers, 1, LANES), jnp.int32),
        tile_map,
        owners,
        nbr_row,
        hbm=(0, 1, 2),
        vmem=60,
        scratch=(
            pltpu.SMEM(tile_map.shape, jnp.int32),
            pltpu.VMEM(owners.shape, jnp.int32),
            pltpu.VMEM(nbr_row.shape, jnp.int32),
            pltpu.SemaphoreType.DMA((3,)),
        ),
    )
    received = swap(ids)
    coef, coef_inside = call(
        functools.partial(coef_kernel, peers, node_rows),
        [shape((node_rows, peers * CAP), BF16)] * 2,
        tile_map,
        owners,
        nbr_row,
        edge_coef[0],
        hbm=(0, 1, 2, 3),
        vmem=60,
        scratch=(
            pltpu.SMEM(tile_map.shape, jnp.int32),
            pltpu.VMEM(owners.shape, jnp.int32),
            pltpu.VMEM(nbr_row.shape, jnp.int32),
            pltpu.VMEM(edge_coef.shape[1:], BF16),
            pltpu.SemaphoreType.DMA((4,)),
        ),
    )
    table = node_rows + table_rows
    received, coef, coef_inside = lax.optimization_barrier((received, coef, coef_inside))
    taken, pick = call(
        gather_kernel,
        [shape((peers, CAP, width), BF16), shape((peers * CAP, table), BF16)],
        received,
        jnp.concatenate([feats[0], history[:, :width]], axis=0),
    )
    pulled = swap(taken)
    out_rows, pair = call(
        forward_kernel,
        [shape((node_rows, width), BF16), shape((node_rows, 2 * width), BF16)],
        pulled,
        coef,
        feats[0],
        weight,
        grad_out[0],
    )
    chips = [[i, i + 1] for i in range(0, peers, 2)]
    pairs = lax.all_gather(pair, "hist", axis=0, axis_index_groups=chips)
    terms = call(
        functools.partial(term_kernel, peers, width),
        shape((peers, 8, share * width // 16), BF16),
        pairs,
    )
    pair, terms = lax.optimization_barrier((pair, terms))
    terms = swap(terms)
    sent, grad_mixed = call(
        backward_kernel,
        [shape((peers, CAP, 2 * width), BF16), shape((node_rows, width), BF16)],
        pair,
        weight,
        coef_inside,
        pick,
        history,
        hbm=(3, 4),
        scratch=(
            pltpu.VMEM((peers * CAP, table), BF16),
            pltpu.VMEM((table_rows, width), BF16),
            pltpu.SemaphoreType.DMA((2,)),
        ),
    )
    side = 4
    near = [[a * side + i for i in range(side)] for a in range(planes // side)]
    term = call(weight_kernel, shape((side, 16, share * width // 16), BF16), terms)
    term = swap(term, "batch", near)
    sent, term = lax.optimization_barrier((sent, term))
    back = swap(sent)
    term = call(add_kernel, shape(term.shape[1:], BF16), term)
    far = [[a + side * i for i in range(planes // side)] for a in range(side)]
    term = lax.all_gather(term, "batch", axis=0, axis_index_groups=far)
    grad_rows, weight_share = call(
        final_kernel,
        [shape((node_rows, width), BF16), shape((share, width), F32)],
        back,
        pick,
        coef,
        grad_mixed,
        term,
    )
    return (out_rows[None], grad_rows[None], weight_share)


def solution(mesh):
    return jax.shard_map(
        body,
        mesh=mesh,
        in_specs=(
            P(("batch", "hist"), None, None),
            P("hist", None),
            P(),
            P(("batch", "hist"), None, None),
            P(("batch", "hist"), None),
            P(("batch", "hist"), None, None),
            P(("batch", "hist"), None),
            P(("batch", "hist"), None, None),
        ),
        out_specs=(
            P(("batch", "hist"), None, None),
            P(("batch", "hist"), None, None),
            P("hist", None),
        ),
        check_vma=False,
    )
```

```python
import functools

import jax
import jax.numpy as jnp
from jax import lax
from jax.experimental import pallas as pl
from jax.experimental.pallas import tpu as pltpu
from jax.sharding import PartitionSpec as P

F32 = jnp.float32
BF16 = jnp.bfloat16
LANES = 128
CAP = 16
ROWS_T = (((1,), (1,)), ((), ()))
COLS_T = (((0,), (0,)), ((), ()))


def dot(a, b, dims=(((1,), (0,)), ((), ()))):
    return lax.dot_general(a, b, dims, preferred_element_type=F32)


def in_edge_order(first_tile, values):
    half = values.shape[1] // 2
    swapped = jnp.concatenate([values[:, half:], values[:, :half]], axis=1)
    return jnp.where(first_tile == 0, values, swapped)


def earlier_slots(slots):
    earlier = (
        lax.broadcasted_iota(jnp.int32, (slots, slots), 0)
        < lax.broadcasted_iota(jnp.int32, (slots, slots), 1)
    )
    return jnp.where(earlier, 1.0, 0.0).astype(BF16)


def slot_places(owners, peers, earlier):
    slots = owners.shape[1]
    named = lax.broadcasted_iota(jnp.int32, (peers, slots), 0) == owners
    named = jnp.where(named, 1.0, 0.0)
    rank = dot(named.astype(BF16), earlier)
    return named, jnp.sum(named * rank, axis=0, keepdims=True).astype(jnp.int32)


def request_kernel(tile_in, owner_in, row_in, ids_ref, tile_ref, owner_ref, row_ref, sems):
    copies = [
        pltpu.make_async_copy(tile_in, tile_ref, sems.at[0]),
        pltpu.make_async_copy(owner_in, owner_ref, sems.at[1]),
        pltpu.make_async_copy(row_in, row_ref, sems.at[2]),
    ]
    for copy in copies:
        copy.start()
    earlier = earlier_slots(owner_ref.shape[1])
    for copy in copies:
        copy.wait()
    peers = ids_ref.shape[0]
    first = tile_ref[0, 0]
    owners = in_edge_order(first, owner_ref[...])
    rows = in_edge_order(first, row_ref[...])
    named, place = slot_places(owners, peers, earlier)
    spot = lax.broadcasted_iota(jnp.int32, (LANES, rows.shape[1]), 0) == place
    spot = jnp.where(spot, 1.0, 0.0).astype(BF16)
    low = (rows % LANES).astype(F32)
    high = (rows // LANES).astype(F32)
    ids = dot((named * low).astype(BF16), spot, ROWS_T) + LANES * dot(
        (named * high).astype(BF16), spot, ROWS_T
    )
    ids_ref[...] = ids.astype(jnp.int32).reshape(ids_ref.shape)


def gather_kernel(ids_ref, table_ref, taken_ref, pick):
    table_rows, width = table_ref.shape
    peers = ids_ref.shape[0]
    ids = ids_ref[...].reshape(peers, LANES).astype(F32)
    ids = jnp.concatenate([ids, jnp.zeros((LANES - peers, LANES), F32)], axis=0)
    by_place = ids.T.astype(jnp.int32)
    columns = lax.broadcasted_iota(jnp.int32, (CAP, table_rows), 1)
    for g in range(peers):
        chosen = columns == by_place[:CAP, g : g + 1]
        pick[g * CAP : (g + 1) * CAP, :] = jnp.where(chosen, 1.0, 0.0).astype(BF16)
    part = peers // 4
    for start in range(0, peers, part):
        emb = dot(pick[start * CAP : (start + part) * CAP, :], table_ref[...])
        taken_ref[start : start + part] = emb.astype(BF16).reshape(part, CAP, width)


def coef_kernel(
    peers, node_rows, tile_in, owner_in, row_in, edge_in, all_ref, inside_ref, tile_ref, owner_ref,
    row_ref, edge_ref, sems
):
    copies = [
        pltpu.make_async_copy(tile_in, tile_ref, sems.at[0]),
        pltpu.make_async_copy(owner_in, owner_ref, sems.at[1]),
        pltpu.make_async_copy(row_in, row_ref, sems.at[2]),
        pltpu.make_async_copy(edge_in, edge_ref, sems.at[3]),
    ]
    for copy in copies:
        copy.start()
    earlier = earlier_slots(owner_ref.shape[1])
    for copy in copies:
        copy.wait()
    first = tile_ref[0, 0]
    owners = in_edge_order(first, owner_ref[...])
    rows = in_edge_order(first, row_ref[...])
    _, place = slot_places(owners, peers, earlier)
    target = owners * CAP + place
    at = lax.broadcasted_iota(jnp.int32, (peers * CAP, target.shape[1]), 0) == target
    moved = jnp.where(at, 1.0, 0.0)
    all_ref[...] = dot(edge_ref[...], moved.astype(BF16), ROWS_T).astype(BF16)
    kept = jnp.where(rows < node_rows, moved, 0.0).astype(BF16)
    inside_ref[...] = dot(edge_ref[...], kept, ROWS_T).astype(BF16)


def forward_kernel(
    pulled_ref,
    all_ref,
    feats_ref,
    weight_ref,
    grad_ref,
    pair_ref,
):
    width = feats_ref.shape[1]
    pulled = pulled_ref[...].reshape(-1, width)
    mixed = (feats_ref[...].astype(F32) + dot(all_ref[...], pulled)).astype(BF16)
    pre = dot(mixed, weight_ref[...])
    gate = jax.nn.sigmoid(pre)
    grad_pre = (grad_ref[...].astype(F32) * gate * (1.0 + pre * (1.0 - gate))).astype(BF16)
    pair_ref[:, :width] = mixed
    pair_ref[:, width:] = grad_pre


def term_kernel(peers, width, pairs_ref, term_ref):
    half = width // 2
    second_core = lax.axis_index("hist") % 2 == 1
    pairs = pairs_ref[...].reshape(-1, 2 * width)
    mixed = pairs[:, :width]
    left, right = pairs[:, width : width + half], pairs[:, width + half :]
    grad_pre = jnp.where(second_core, right, left)
    share = width // peers
    step = 8
    term = dot(mixed, grad_pre, COLS_T)
    for peer in range(peers):
        blocks = [
            term[peer * share + i : peer * share + i + step, :] for i in range(0, share, step)
        ]
        term_ref[peer] = jnp.concatenate(blocks, axis=1).astype(BF16)


def backward_kernel(
    pair_ref,
    weight_ref,
    inside_ref,
    pick_in,
    history_in,
    send_ref,
    mixed_ref,
    out_ref,
    pick,
    aux,
    sems,
):
    node_rows, width = mixed_ref.shape
    peers = send_ref.shape[0]
    load_pick = pltpu.make_async_copy(pick_in, pick, sems.at[0])
    load_aux = pltpu.make_async_copy(history_in.at[:, width:], aux, sems.at[1])
    load_pick.start()
    load_aux.start()
    grad_mixed = dot(pair_ref[:, width:], weight_ref[...], ROWS_T).astype(BF16)
    mixed_ref[...] = grad_mixed
    slot_grad = dot(inside_ref[...], grad_mixed, COLS_T).astype(BF16)
    send_ref[:, :, :width] = slot_grad.reshape(peers, CAP, width)
    pre = dot(pair_ref[:, :width], weight_ref[...])
    out_ref[...] = (pre * jax.nn.sigmoid(pre)).astype(BF16)
    load_pick.wait()
    load_aux.wait()
    taken = dot(pick[:, node_rows:], aux[...]).astype(BF16)
    send_ref[:, :, width:] = taken.reshape(peers, CAP, width)


def weight_kernel(terms_ref, sum_ref):
    peers, step = terms_ref.shape[:2]
    for core in range(2):
        total = terms_ref[core].astype(F32)
        for peer in range(core + 2, peers, 2):
            total = total + terms_ref[peer].astype(F32)
        total = total.astype(BF16)
        for plane in range(sum_ref.shape[0]):
            sum_ref[plane, core * step : (core + 1) * step, :] = total


def add_kernel(near_ref, sum_ref):
    sum_ref[...] = jnp.sum(near_ref[...].astype(F32), axis=0).astype(BF16)


def final_kernel(
    back_ref, pick_ref, all_ref, mixed_ref, far_ref, grad_ref, share_ref
):
    total = jnp.sum(far_ref[...].astype(F32), axis=0)
    share, width = share_ref.shape
    half = width // 2
    step = total.shape[0] // 2
    for i in range(share // step):
        for core in range(2):
            share_ref[i * step : (i + 1) * step, core * half : (core + 1) * half] = total[
                core * step : (core + 1) * step, i * half : (i + 1) * half
            ]
    peers = back_ref.shape[0]
    node_rows = mixed_ref.shape[0]
    slots = back_ref[:, :, :width].reshape(peers * CAP, width)
    aux = back_ref[:, :, width:].reshape(peers * CAP, width)
    returned = dot(pick_ref[:, :node_rows], slots, COLS_T)
    compensation = dot(all_ref[...], aux)
    grad = mixed_ref[...].astype(F32) + returned + compensation
    grad_ref[...] = grad.astype(BF16)


def call(kernel, out_shape, *args, smem=(), hbm=(), hbm_out=(), scratch=(), vmem=32, cost=None):
    spaces = [
        pltpu.SMEM if i in smem else pltpu.HBM if i in hbm else pltpu.VMEM
        for i in range(len(args))
    ]
    single = not isinstance(out_shape, (list, tuple))
    out_shape = [out_shape] if single else out_shape
    out_spaces = [pltpu.HBM if i in hbm_out else pltpu.VMEM for i in range(len(out_shape))]
    result = pl.pallas_call(
        kernel,
        out_shape=out_shape,
        in_specs=[pl.BlockSpec(memory_space=space) for space in spaces],
        out_specs=[pl.BlockSpec(memory_space=space) for space in out_spaces],
        scratch_shapes=list(scratch),
        compiler_params=pltpu.CompilerParams(vmem_limit_bytes=vmem << 20),
        cost_estimate=cost,
    )(*args)
    return result[0] if single else result


def swap(values, axis="hist", groups=None):
    return lax.all_to_all(
        values, axis, split_axis=0, concat_axis=0, tiled=True, axis_index_groups=groups
    )


def body(feats, history, weight, edge_coef, tile_map, nbr_owner, nbr_row, grad_out):
    peers = lax.axis_size("hist")
    planes = lax.axis_size("batch")
    node_rows, width = feats.shape[1:]
    table_rows = history.shape[0]
    slots = nbr_row.shape[1]
    assert 2 * slots // peers == CAP and planes == 16
    share = width // peers
    shape = jax.ShapeDtypeStruct
    owners = nbr_owner.reshape(1, slots)
    ids = call(
        request_kernel,
        shape((peers, 1, LANES), jnp.int32),
        tile_map,
        owners,
        nbr_row,
        hbm=(0, 1, 2),
        vmem=60,
        scratch=(
            pltpu.SMEM(tile_map.shape, jnp.int32),
            pltpu.VMEM(owners.shape, jnp.int32),
            pltpu.VMEM(nbr_row.shape, jnp.int32),
            pltpu.SemaphoreType.DMA((3,)),
        ),
    )
    received = swap(ids)
    coef, coef_inside = call(
        functools.partial(coef_kernel, peers, node_rows),
        [shape((node_rows, peers * CAP), BF16)] * 2,
        tile_map,
        owners,
        nbr_row,
        edge_coef[0],
        hbm=(0, 1, 2, 3),
        vmem=60,
        scratch=(
            pltpu.SMEM(tile_map.shape, jnp.int32),
            pltpu.VMEM(owners.shape, jnp.int32),
            pltpu.VMEM(nbr_row.shape, jnp.int32),
            pltpu.VMEM(edge_coef.shape[1:], BF16),
            pltpu.SemaphoreType.DMA((4,)),
        ),
    )
    table = node_rows + table_rows
    received, coef, coef_inside = lax.optimization_barrier((received, coef, coef_inside))
    taken, pick = call(
        gather_kernel,
        [shape((peers, CAP, width), BF16), shape((peers * CAP, table), BF16)],
        received,
        jnp.concatenate([feats[0], history[:, :width]], axis=0),
    )
    pulled = swap(taken)
    pair = call(
        forward_kernel,
        shape((node_rows, 2 * width), BF16),
        pulled,
        coef,
        feats[0],
        weight,
        grad_out[0],
    )
    chips = [[i, i + 1] for i in range(0, peers, 2)]
    pairs = lax.all_gather(pair, "hist", axis=0, axis_index_groups=chips)
    terms = call(
        functools.partial(term_kernel, peers, width),
        shape((peers, 8, share * width // 16), BF16),
        pairs,
    )
    pair, terms = lax.optimization_barrier((pair, terms))
    terms = swap(terms)
    sent, grad_mixed, out_rows = call(
        backward_kernel,
        [
            shape((peers, CAP, 2 * width), BF16),
            shape((node_rows, width), BF16),
            shape((node_rows, width), BF16),
        ],
        pair,
        weight,
        coef_inside,
        pick,
        history,
        hbm=(3, 4),
        scratch=(
            pltpu.VMEM((peers * CAP, table), BF16),
            pltpu.VMEM((table_rows, width), BF16),
            pltpu.SemaphoreType.DMA((2,)),
        ),
    )
    sent, terms = lax.optimization_barrier((sent, terms))
    side = 4
    near = [[a * side + i for i in range(side)] for a in range(planes // side)]
    term = call(weight_kernel, shape((side, 16, share * width // 16), BF16), terms)
    term = swap(term, "batch", near)
    sent, term = lax.optimization_barrier((sent, term))
    back = swap(sent)
    term = call(add_kernel, shape(term.shape[1:], BF16), term)
    far = [[a + side * i for i in range(planes // side)] for a in range(side)]
    term = lax.all_gather(term, "batch", axis=0, axis_index_groups=far)
    grad_rows, weight_share = call(
        final_kernel,
        [shape((node_rows, width), BF16), shape((share, width), F32)],
        back,
        pick,
        coef,
        grad_mixed,
        term,
    )
    return (out_rows[None], grad_rows[None], weight_share)


def solution(mesh):
    return jax.shard_map(
        body,
        mesh=mesh,
        in_specs=(
            P(("batch", "hist"), None, None),
            P("hist", None),
            P(),
            P(("batch", "hist"), None, None),
            P(("batch", "hist"), None),
            P(("batch", "hist"), None, None),
            P(("batch", "hist"), None),
            P(("batch", "hist"), None, None),
        ),
        out_specs=(
            P(("batch", "hist"), None, None),
            P(("batch", "hist"), None, None),
            P("hist", None),
        ),
        check_vma=False,
    )
```

```python
import functools

import jax
import jax.numpy as jnp
from jax import lax
from jax.experimental import pallas as pl
from jax.experimental.pallas import tpu as pltpu
from jax.sharding import PartitionSpec as P

F32 = jnp.float32
BF16 = jnp.bfloat16
LANES = 128
CAP = 16
ROWS_T = (((1,), (1,)), ((), ()))
COLS_T = (((0,), (0,)), ((), ()))


def dot(a, b, dims=(((1,), (0,)), ((), ()))):
    return lax.dot_general(a, b, dims, preferred_element_type=F32)


def in_edge_order(first_tile, values):
    half = values.shape[1] // 2
    swapped = jnp.concatenate([values[:, half:], values[:, :half]], axis=1)
    return jnp.where(first_tile == 0, values, swapped)


def earlier_slots(slots):
    earlier = (
        lax.broadcasted_iota(jnp.int32, (slots, slots), 0)
        < lax.broadcasted_iota(jnp.int32, (slots, slots), 1)
    )
    return jnp.where(earlier, 1.0, 0.0).astype(BF16)


def slot_places(owners, peers, earlier):
    slots = owners.shape[1]
    named = lax.broadcasted_iota(jnp.int32, (peers, slots), 0) == owners
    named = jnp.where(named, 1.0, 0.0)
    rank = dot(named.astype(BF16), earlier)
    return named, jnp.sum(named * rank, axis=0, keepdims=True).astype(jnp.int32)


def request_kernel(tile_in, owner_in, row_in, ids_ref, tile_ref, owner_ref, row_ref, sems):
    copies = [
        pltpu.make_async_copy(tile_in, tile_ref, sems.at[0]),
        pltpu.make_async_copy(owner_in, owner_ref, sems.at[1]),
        pltpu.make_async_copy(row_in, row_ref, sems.at[2]),
    ]
    for copy in copies:
        copy.start()
    earlier = earlier_slots(owner_ref.shape[1])
    for copy in copies:
        copy.wait()
    peers = ids_ref.shape[0]
    first = tile_ref[0, 0]
    owners = in_edge_order(first, owner_ref[...])
    rows = in_edge_order(first, row_ref[...])
    named, place = slot_places(owners, peers, earlier)
    spot = lax.broadcasted_iota(jnp.int32, (LANES, rows.shape[1]), 0) == place
    spot = jnp.where(spot, 1.0, 0.0).astype(BF16)
    low = (rows % LANES).astype(F32)
    high = (rows // LANES).astype(F32)
    ids = dot((named * low).astype(BF16), spot, ROWS_T) + LANES * dot(
        (named * high).astype(BF16), spot, ROWS_T
    )
    ids_ref[...] = ids.astype(jnp.int32).reshape(ids_ref.shape)


def gather_kernel(ids_ref, table_ref, taken_ref, pick):
    table_rows, width = table_ref.shape
    peers = ids_ref.shape[0]
    ids = ids_ref[...].reshape(peers, LANES).astype(F32)
    ids = jnp.concatenate([ids, jnp.zeros((LANES - peers, LANES), F32)], axis=0)
    by_place = ids.T.astype(jnp.int32)
    columns = lax.broadcasted_iota(jnp.int32, (CAP, table_rows), 1)
    for g in range(peers):
        chosen = columns == by_place[:CAP, g : g + 1]
        pick[g * CAP : (g + 1) * CAP, :] = jnp.where(chosen, 1.0, 0.0).astype(BF16)
    part = peers // 4
    for start in range(0, peers, part):
        emb = dot(pick[start * CAP : (start + part) * CAP, :], table_ref[...])
        taken_ref[start : start + part] = emb.astype(BF16).reshape(part, CAP, width)


def coef_kernel(
    peers, node_rows, tile_in, owner_in, row_in, edge_in, all_ref, inside_ref, tile_ref, owner_ref,
    row_ref, edge_ref, sems
):
    copies = [
        pltpu.make_async_copy(tile_in, tile_ref, sems.at[0]),
        pltpu.make_async_copy(owner_in, owner_ref, sems.at[1]),
        pltpu.make_async_copy(row_in, row_ref, sems.at[2]),
        pltpu.make_async_copy(edge_in, edge_ref, sems.at[3]),
    ]
    for copy in copies:
        copy.start()
    earlier = earlier_slots(owner_ref.shape[1])
    for copy in copies:
        copy.wait()
    first = tile_ref[0, 0]
    owners = in_edge_order(first, owner_ref[...])
    rows = in_edge_order(first, row_ref[...])
    _, place = slot_places(owners, peers, earlier)
    target = owners * CAP + place
    at = lax.broadcasted_iota(jnp.int32, (peers * CAP, target.shape[1]), 0) == target
    moved = jnp.where(at, 1.0, 0.0)
    all_ref[...] = dot(edge_ref[...], moved.astype(BF16), ROWS_T).astype(BF16)
    kept = jnp.where(rows < node_rows, moved, 0.0).astype(BF16)
    inside_ref[...] = dot(edge_ref[...], kept, ROWS_T).astype(BF16)


def forward_kernel(
    pulled_ref,
    all_ref,
    feats_ref,
    weight_ref,
    grad_ref,
    pair_ref,
):
    width = feats_ref.shape[1]
    pulled = pulled_ref[...].reshape(-1, width)
    mixed = (feats_ref[...].astype(F32) + dot(all_ref[...], pulled)).astype(BF16)
    pre = dot(mixed, weight_ref[...])
    gate = jax.nn.sigmoid(pre)
    grad_pre = (grad_ref[...].astype(F32) * gate * (1.0 + pre * (1.0 - gate))).astype(BF16)
    pair_ref[:, :width] = mixed
    pair_ref[:, width:] = grad_pre


def term_kernel(peers, width, pairs_ref, term_ref):
    half = width // 2
    second_core = lax.axis_index("hist") % 2 == 1
    pairs = pairs_ref[...].reshape(-1, 2 * width)
    mixed = pairs[:, :width]
    left, right = pairs[:, width : width + half], pairs[:, width + half :]
    grad_pre = jnp.where(second_core, right, left)
    share = width // peers
    step = 8
    term = dot(mixed, grad_pre, COLS_T)
    for peer in range(peers):
        blocks = [
            term[peer * share + i : peer * share + i + step, :] for i in range(0, share, step)
        ]
        term_ref[peer] = jnp.concatenate(blocks, axis=1).astype(BF16)


def backward_kernel(
    pair_ref,
    weight_ref,
    inside_ref,
    pick_in,
    history_in,
    send_ref,
    mixed_ref,
    out_ref,
    pick,
    aux,
    sems,
):
    node_rows, width = mixed_ref.shape
    peers = send_ref.shape[0]
    load_pick = pltpu.make_async_copy(pick_in, pick, sems.at[0])
    load_aux = pltpu.make_async_copy(history_in.at[:, width:], aux, sems.at[1])
    load_pick.start()
    load_aux.start()
    grad_mixed = dot(pair_ref[:, width:], weight_ref[...], ROWS_T).astype(BF16)
    mixed_ref[...] = grad_mixed
    slot_grad = dot(inside_ref[...], grad_mixed, COLS_T).astype(BF16)
    send_ref[:, :, :width] = slot_grad.reshape(peers, CAP, width)
    pre = dot(pair_ref[:, :width], weight_ref[...])
    out_ref[...] = (pre * jax.nn.sigmoid(pre)).astype(BF16)
    load_pick.wait()
    load_aux.wait()
    taken = dot(pick[:, node_rows:], aux[...]).astype(BF16)
    send_ref[:, :, width:] = taken.reshape(peers, CAP, width)


def weight_kernel(terms_ref, sum_ref):
    peers, step = terms_ref.shape[:2]
    for core in range(2):
        total = terms_ref[core].astype(F32)
        for peer in range(core + 2, peers, 2):
            total = total + terms_ref[peer].astype(F32)
        total = total.astype(BF16)
        for plane in range(sum_ref.shape[0]):
            sum_ref[plane, core * step : (core + 1) * step, :] = total


def add_kernel(near_ref, sum_ref):
    sum_ref[...] = jnp.sum(near_ref[...].astype(F32), axis=0).astype(BF16)


def final_kernel(
    back_ref, pick_ref, all_ref, mixed_ref, far_ref, grad_ref, share_ref
):
    total = jnp.sum(far_ref[...].astype(F32), axis=0)
    share, width = share_ref.shape
    half = width // 2
    step = total.shape[0] // 2
    for i in range(share // step):
        for core in range(2):
            share_ref[i * step : (i + 1) * step, core * half : (core + 1) * half] = total[
                core * step : (core + 1) * step, i * half : (i + 1) * half
            ]
    peers = back_ref.shape[0]
    node_rows = mixed_ref.shape[0]
    slots = back_ref[:, :, :width].reshape(peers * CAP, width)
    aux = back_ref[:, :, width:].reshape(peers * CAP, width)
    returned = dot(pick_ref[:, :node_rows], slots, COLS_T)
    compensation = dot(all_ref[...], aux)
    grad = mixed_ref[...].astype(F32) + returned + compensation
    grad_ref[...] = grad.astype(BF16)


def call(kernel, out_shape, *args, smem=(), hbm=(), hbm_out=(), scratch=(), vmem=32, cost=None):
    spaces = [
        pltpu.SMEM if i in smem else pltpu.HBM if i in hbm else pltpu.VMEM
        for i in range(len(args))
    ]
    single = not isinstance(out_shape, (list, tuple))
    out_shape = [out_shape] if single else out_shape
    out_spaces = [pltpu.HBM if i in hbm_out else pltpu.VMEM for i in range(len(out_shape))]
    result = pl.pallas_call(
        kernel,
        out_shape=out_shape,
        in_specs=[pl.BlockSpec(memory_space=space) for space in spaces],
        out_specs=[pl.BlockSpec(memory_space=space) for space in out_spaces],
        scratch_shapes=list(scratch),
        compiler_params=pltpu.CompilerParams(vmem_limit_bytes=vmem << 20),
        cost_estimate=cost,
    )(*args)
    return result[0] if single else result


def swap(values, axis="hist", groups=None):
    return lax.all_to_all(
        values, axis, split_axis=0, concat_axis=0, tiled=True, axis_index_groups=groups
    )


def body(feats, history, weight, edge_coef, tile_map, nbr_owner, nbr_row, grad_out):
    peers = lax.axis_size("hist")
    planes = lax.axis_size("batch")
    node_rows, width = feats.shape[1:]
    table_rows = history.shape[0]
    slots = nbr_row.shape[1]
    assert 2 * slots // peers == CAP and planes == 16
    share = width // peers
    shape = jax.ShapeDtypeStruct
    owners = nbr_owner.reshape(1, slots)
    ids = call(
        request_kernel,
        shape((peers, 1, LANES), jnp.int32),
        tile_map,
        owners,
        nbr_row,
        hbm=(0, 1, 2),
        vmem=60,
        scratch=(
            pltpu.SMEM(tile_map.shape, jnp.int32),
            pltpu.VMEM(owners.shape, jnp.int32),
            pltpu.VMEM(nbr_row.shape, jnp.int32),
            pltpu.SemaphoreType.DMA((3,)),
        ),
    )
    received = swap(ids)
    coef, coef_inside = call(
        functools.partial(coef_kernel, peers, node_rows),
        [shape((node_rows, peers * CAP), BF16)] * 2,
        tile_map,
        owners,
        nbr_row,
        edge_coef[0],
        hbm=(0, 1, 2, 3),
        vmem=60,
        scratch=(
            pltpu.SMEM(tile_map.shape, jnp.int32),
            pltpu.VMEM(owners.shape, jnp.int32),
            pltpu.VMEM(nbr_row.shape, jnp.int32),
            pltpu.VMEM(edge_coef.shape[1:], BF16),
            pltpu.SemaphoreType.DMA((4,)),
        ),
    )
    table = node_rows + table_rows
    received, coef, coef_inside = lax.optimization_barrier((received, coef, coef_inside))
    taken, pick = call(
        gather_kernel,
        [shape((peers, CAP, width), BF16), shape((peers * CAP, table), BF16)],
        received,
        jnp.concatenate([feats[0], history[:, :width]], axis=0),
    )
    pulled = swap(taken)
    pair = call(
        forward_kernel,
        shape((node_rows, 2 * width), BF16),
        pulled,
        coef,
        feats[0],
        weight,
        grad_out[0],
    )
    chips = [[i, i + 1] for i in range(0, peers, 2)]
    pairs = lax.all_gather(pair, "hist", axis=0, axis_index_groups=chips)
    terms = call(
        functools.partial(term_kernel, peers, width),
        shape((peers, 8, share * width // 16), BF16),
        pairs,
    )
    pair, terms = lax.optimization_barrier((pair, terms))
    terms = swap(terms)
    sent, grad_mixed, out_rows = call(
        backward_kernel,
        [
            shape((peers, CAP, 2 * width), BF16),
            shape((node_rows, width), BF16),
            shape((node_rows, width), BF16),
        ],
        pair,
        weight,
        coef_inside,
        pick,
        history,
        hbm=(3, 4),
        scratch=(
            pltpu.VMEM((peers * CAP, table), BF16),
            pltpu.VMEM((table_rows, width), BF16),
            pltpu.SemaphoreType.DMA((2,)),
        ),
    )
    side = 4
    near = [[a * side + i for i in range(side)] for a in range(planes // side)]
    term = call(weight_kernel, shape((side, 16, share * width // 16), BF16), terms)
    term = swap(term, "batch", near)
    sent, term = lax.optimization_barrier((sent, term))
    back = swap(sent)
    term = call(add_kernel, shape(term.shape[1:], BF16), term)
    far = [[a + side * i for i in range(planes // side)] for a in range(side)]
    term = lax.all_gather(term, "batch", axis=0, axis_index_groups=far)
    grad_rows, weight_share = call(
        final_kernel,
        [shape((node_rows, width), BF16), shape((share, width), F32)],
        back,
        pick,
        coef,
        grad_mixed,
        term,
    )
    return (out_rows[None], grad_rows[None], weight_share)


def solution(mesh):
    return jax.shard_map(
        body,
        mesh=mesh,
        in_specs=(
            P(("batch", "hist"), None, None),
            P("hist", None),
            P(),
            P(("batch", "hist"), None, None),
            P(("batch", "hist"), None),
            P(("batch", "hist"), None, None),
            P(("batch", "hist"), None),
            P(("batch", "hist"), None, None),
        ),
        out_specs=(
            P(("batch", "hist"), None, None),
            P(("batch", "hist"), None, None),
            P("hist", None),
        ),
        check_vma=False,
    )
```

```python
import functools

import jax
import jax.numpy as jnp
from jax import lax
from jax.experimental import pallas as pl
from jax.experimental.pallas import tpu as pltpu
from jax.sharding import PartitionSpec as P

F32 = jnp.float32
BF16 = jnp.bfloat16
LANES = 128
CAP = 16
ROWS_T = (((1,), (1,)), ((), ()))
COLS_T = (((0,), (0,)), ((), ()))


def dot(a, b, dims=(((1,), (0,)), ((), ()))):
    return lax.dot_general(a, b, dims, preferred_element_type=F32)


def in_edge_order(first_tile, values):
    half = values.shape[1] // 2
    swapped = jnp.concatenate([values[:, half:], values[:, :half]], axis=1)
    return jnp.where(first_tile == 0, values, swapped)


def earlier_slots(slots):
    earlier = (
        lax.broadcasted_iota(jnp.int32, (slots, slots), 0)
        < lax.broadcasted_iota(jnp.int32, (slots, slots), 1)
    )
    return jnp.where(earlier, 1.0, 0.0).astype(BF16)


def slot_places(owners, peers, earlier):
    slots = owners.shape[1]
    named = lax.broadcasted_iota(jnp.int32, (peers, slots), 0) == owners
    named = jnp.where(named, 1.0, 0.0)
    rank = dot(named.astype(BF16), earlier)
    return named, jnp.sum(named * rank, axis=0, keepdims=True).astype(jnp.int32)


def request_kernel(tile_in, owner_in, row_in, ids_ref, tile_ref, owner_ref, row_ref, sems):
    copies = [
        pltpu.make_async_copy(tile_in, tile_ref, sems.at[0]),
        pltpu.make_async_copy(owner_in, owner_ref, sems.at[1]),
        pltpu.make_async_copy(row_in, row_ref, sems.at[2]),
    ]
    for copy in copies:
        copy.start()
    earlier = earlier_slots(owner_ref.shape[1])
    for copy in copies:
        copy.wait()
    peers = ids_ref.shape[0]
    first = tile_ref[0, 0]
    owners = in_edge_order(first, owner_ref[...])
    rows = in_edge_order(first, row_ref[...])
    named, place = slot_places(owners, peers, earlier)
    spot = lax.broadcasted_iota(jnp.int32, (LANES, rows.shape[1]), 0) == place
    spot = jnp.where(spot, 1.0, 0.0).astype(BF16)
    low = named * (rows % LANES).astype(F32)
    high = named * (rows // LANES).astype(F32)
    ids = dot(jnp.concatenate([low, high], axis=0).astype(BF16), spot, ROWS_T)
    ids = ids[:peers] + LANES * ids[peers:]
    ids_ref[...] = ids.astype(jnp.int32).reshape(ids_ref.shape)


def gather_kernel(ids_ref, table_ref, taken_ref, pick):
    table_rows, width = table_ref.shape
    peers = ids_ref.shape[0]
    ids = ids_ref[...].reshape(peers, LANES).astype(F32)
    ids = jnp.concatenate([ids, jnp.zeros((LANES - peers, LANES), F32)], axis=0)
    by_place = ids.T.astype(jnp.int32)
    columns = lax.broadcasted_iota(jnp.int32, (CAP, table_rows), 1)
    for g in range(peers):
        chosen = columns == by_place[:CAP, g : g + 1]
        pick[g * CAP : (g + 1) * CAP, :] = jnp.where(chosen, 1.0, 0.0).astype(BF16)
    part = peers // 4
    for start in range(0, peers, part):
        emb = dot(pick[start * CAP : (start + part) * CAP, :], table_ref[...])
        taken_ref[start : start + part] = emb.astype(BF16).reshape(part, CAP, width)


def coef_kernel(
    peers, node_rows, tile_in, owner_in, row_in, edge_in, all_ref, inside_ref, tile_ref, owner_ref,
    row_ref, edge_ref, sems
):
    copies = [
        pltpu.make_async_copy(tile_in, tile_ref, sems.at[0]),
        pltpu.make_async_copy(owner_in, owner_ref, sems.at[1]),
        pltpu.make_async_copy(row_in, row_ref, sems.at[2]),
        pltpu.make_async_copy(edge_in, edge_ref, sems.at[3]),
    ]
    for copy in copies:
        copy.start()
    earlier = earlier_slots(owner_ref.shape[1])
    for copy in copies:
        copy.wait()
    first = tile_ref[0, 0]
    owners = in_edge_order(first, owner_ref[...])
    rows = in_edge_order(first, row_ref[...])
    _, place = slot_places(owners, peers, earlier)
    target = owners * CAP + place
    at = lax.broadcasted_iota(jnp.int32, (peers * CAP, target.shape[1]), 0) == target
    moved = jnp.where(at, 1.0, 0.0)
    all_ref[...] = dot(edge_ref[...], moved.astype(BF16), ROWS_T).astype(BF16)
    kept = jnp.where(rows < node_rows, moved, 0.0).astype(BF16)
    inside_ref[...] = dot(edge_ref[...], kept, ROWS_T).astype(BF16)


def forward_kernel(
    pulled_ref,
    all_ref,
    feats_ref,
    weight_ref,
    grad_ref,
    pair_ref,
):
    width = feats_ref.shape[1]
    pulled = pulled_ref[...].reshape(-1, width)
    mixed = (feats_ref[...].astype(F32) + dot(all_ref[...], pulled)).astype(BF16)
    pre = dot(mixed, weight_ref[...])
    gate = jax.nn.sigmoid(pre)
    grad_pre = (grad_ref[...].astype(F32) * gate * (1.0 + pre * (1.0 - gate))).astype(BF16)
    pair_ref[:, :width] = mixed
    pair_ref[:, width:] = grad_pre


def term_kernel(peers, width, pairs_ref, term_out, term_ref, sems):
    half = width // 2
    second_core = lax.axis_index("hist") % 2 == 1
    pairs = pairs_ref[...].reshape(-1, 2 * width)
    left, right = pairs[:, width : width + half], pairs[:, width + half :]
    grad_pre = jnp.where(second_core, right, left)
    share = width // peers
    step = 8
    copies = []
    terms = dot(pairs[:, :width], grad_pre, COLS_T)
    for part in range(2):
        term = terms[part * half : (part + 1) * half, :]
        first = part * (peers // 2)
        for peer in range(peers // 2):
            blocks = [
                term[peer * share + i : peer * share + i + step, :] for i in range(0, share, step)
            ]
            term_ref[first + peer] = jnp.concatenate(blocks, axis=1).astype(BF16)
        copies.append(
            pltpu.make_async_copy(
                term_ref.at[first : first + peers // 2],
                term_out.at[first : first + peers // 2],
                sems.at[part],
            )
        )
        copies[-1].start()
    for copy in copies:
        copy.wait()


def backward_kernel(
    pair_ref,
    weight_ref,
    inside_ref,
    pick_in,
    history_in,
    send_ref,
    mixed_ref,
    out_ref,
    pick,
    aux,
    sems,
):
    node_rows, width = mixed_ref.shape
    peers = send_ref.shape[0]
    load_pick = pltpu.make_async_copy(pick_in, pick, sems.at[0])
    load_aux = pltpu.make_async_copy(history_in.at[:, width:], aux, sems.at[1])
    load_pick.start()
    load_aux.start()
    grad_mixed = dot(pair_ref[:, width:], weight_ref[...], ROWS_T).astype(BF16)
    mixed_ref[...] = grad_mixed
    slot_grad = dot(inside_ref[...], grad_mixed, COLS_T).astype(BF16)
    send_ref[:, :, :width] = slot_grad.reshape(peers, CAP, width)
    pre = dot(pair_ref[:, :width], weight_ref[...])
    out_ref[...] = (pre * jax.nn.sigmoid(pre)).astype(BF16)
    load_pick.wait()
    load_aux.wait()
    taken = dot(pick[:, node_rows:], aux[...]).astype(BF16)
    send_ref[:, :, width:] = taken.reshape(peers, CAP, width)


def weight_kernel(terms_ref, sum_ref):
    peers, step = terms_ref.shape[:2]
    for core in range(2):
        total = terms_ref[core].astype(F32)
        for peer in range(core + 2, peers, 2):
            total = total + terms_ref[peer].astype(F32)
        total = total.astype(BF16)
        for plane in range(sum_ref.shape[0]):
            sum_ref[plane, core * step : (core + 1) * step, :] = total


def add_kernel(near_ref, sum_ref):
    sum_ref[...] = jnp.sum(near_ref[...].astype(F32), axis=0).astype(BF16)


def final_kernel(
    back_ref, pick_ref, all_ref, mixed_ref, far_ref, grad_ref, share_ref
):
    total = jnp.sum(far_ref[...].astype(F32), axis=0)
    share, width = share_ref.shape
    half = width // 2
    step = total.shape[0] // 2
    for i in range(share // step):
        for core in range(2):
            share_ref[i * step : (i + 1) * step, core * half : (core + 1) * half] = total[
                core * step : (core + 1) * step, i * half : (i + 1) * half
            ]
    peers = back_ref.shape[0]
    node_rows = mixed_ref.shape[0]
    slots = back_ref[:, :, :width].reshape(peers * CAP, width)
    aux = back_ref[:, :, width:].reshape(peers * CAP, width)
    returned = dot(pick_ref[:, :node_rows], slots, COLS_T)
    compensation = dot(all_ref[...], aux)
    grad = mixed_ref[...].astype(F32) + returned + compensation
    grad_ref[...] = grad.astype(BF16)


def call(kernel, out_shape, *args, smem=(), hbm=(), hbm_out=(), scratch=(), vmem=32, cost=None):
    spaces = [
        pltpu.SMEM if i in smem else pltpu.HBM if i in hbm else pltpu.VMEM
        for i in range(len(args))
    ]
    single = not isinstance(out_shape, (list, tuple))
    out_shape = [out_shape] if single else out_shape
    out_spaces = [pltpu.HBM if i in hbm_out else pltpu.VMEM for i in range(len(out_shape))]
    result = pl.pallas_call(
        kernel,
        out_shape=out_shape,
        in_specs=[pl.BlockSpec(memory_space=space) for space in spaces],
        out_specs=[pl.BlockSpec(memory_space=space) for space in out_spaces],
        scratch_shapes=list(scratch),
        compiler_params=pltpu.CompilerParams(vmem_limit_bytes=vmem << 20),
        cost_estimate=cost,
    )(*args)
    return result[0] if single else result


def swap(values, axis="hist", groups=None):
    return lax.all_to_all(
        values, axis, split_axis=0, concat_axis=0, tiled=True, axis_index_groups=groups
    )


def body(feats, history, weight, edge_coef, tile_map, nbr_owner, nbr_row, grad_out):
    peers = lax.axis_size("hist")
    planes = lax.axis_size("batch")
    node_rows, width = feats.shape[1:]
    table_rows = history.shape[0]
    slots = nbr_row.shape[1]
    assert 2 * slots // peers == CAP and planes == 16
    share = width // peers
    shape = jax.ShapeDtypeStruct
    owners = nbr_owner.reshape(1, slots)
    ids = call(
        request_kernel,
        shape((peers, 1, LANES), jnp.int32),
        tile_map,
        owners,
        nbr_row,
        hbm=(0, 1, 2),
        vmem=60,
        scratch=(
            pltpu.SMEM(tile_map.shape, jnp.int32),
            pltpu.VMEM(owners.shape, jnp.int32),
            pltpu.VMEM(nbr_row.shape, jnp.int32),
            pltpu.SemaphoreType.DMA((3,)),
        ),
    )
    received = swap(ids)
    coef, coef_inside = call(
        functools.partial(coef_kernel, peers, node_rows),
        [shape((node_rows, peers * CAP), BF16)] * 2,
        tile_map,
        owners,
        nbr_row,
        edge_coef[0],
        hbm=(0, 1, 2, 3),
        vmem=60,
        scratch=(
            pltpu.SMEM(tile_map.shape, jnp.int32),
            pltpu.VMEM(owners.shape, jnp.int32),
            pltpu.VMEM(nbr_row.shape, jnp.int32),
            pltpu.VMEM(edge_coef.shape[1:], BF16),
            pltpu.SemaphoreType.DMA((4,)),
        ),
    )
    table = node_rows + table_rows
    received, coef, coef_inside = lax.optimization_barrier((received, coef, coef_inside))
    taken, pick = call(
        gather_kernel,
        [shape((peers, CAP, width), BF16), shape((peers * CAP, table), BF16)],
        received,
        jnp.concatenate([feats[0], history[:, :width]], axis=0),
    )
    pulled = swap(taken)
    pair = call(
        forward_kernel,
        shape((node_rows, 2 * width), BF16),
        pulled,
        coef,
        feats[0],
        weight,
        grad_out[0],
    )
    chips = [[i, i + 1] for i in range(0, peers, 2)]
    pairs = lax.all_gather(pair, "hist", axis=0, axis_index_groups=chips)
    terms = call(
        functools.partial(term_kernel, peers, width),
        shape((peers, 8, share * width // 16), BF16),
        pairs,
        hbm_out=(0,),
        scratch=(
            pltpu.VMEM((peers, 8, share * width // 16), BF16),
            pltpu.SemaphoreType.DMA((2,)),
        ),
    )
    pair, terms = lax.optimization_barrier((pair, terms))
    terms = swap(terms)
    sent, grad_mixed, out_rows = call(
        backward_kernel,
        [
            shape((peers, CAP, 2 * width), BF16),
            shape((node_rows, width), BF16),
            shape((node_rows, width), BF16),
        ],
        pair,
        weight,
        coef_inside,
        pick,
        history,
        hbm=(3, 4),
        scratch=(
            pltpu.VMEM((peers * CAP, table), BF16),
            pltpu.VMEM((table_rows, width), BF16),
            pltpu.SemaphoreType.DMA((2,)),
        ),
    )
    sent, terms = lax.optimization_barrier((sent, terms))
    side = 4
    near = [[a * side + i for i in range(side)] for a in range(planes // side)]
    term = call(weight_kernel, shape((side, 16, share * width // 16), BF16), terms)
    term = swap(term, "batch", near)
    sent, term = lax.optimization_barrier((sent, term))
    back = swap(sent)
    term = call(add_kernel, shape(term.shape[1:], BF16), term)
    far = [[a + side * i for i in range(planes // side)] for a in range(side)]
    term = lax.all_gather(term, "batch", axis=0, axis_index_groups=far)
    grad_rows, weight_share = call(
        final_kernel,
        [shape((node_rows, width), BF16), shape((share, width), F32)],
        back,
        pick,
        coef,
        grad_mixed,
        term,
    )
    return (out_rows[None], grad_rows[None], weight_share)


def solution(mesh):
    return jax.shard_map(
        body,
        mesh=mesh,
        in_specs=(
            P(("batch", "hist"), None, None),
            P("hist", None),
            P(),
            P(("batch", "hist"), None, None),
            P(("batch", "hist"), None),
            P(("batch", "hist"), None, None),
            P(("batch", "hist"), None),
            P(("batch", "hist"), None, None),
        ),
        out_specs=(
            P(("batch", "hist"), None, None),
            P(("batch", "hist"), None, None),
            P("hist", None),
        ),
        check_vma=False,
    )
```

```python
import functools

import jax
import jax.numpy as jnp
from jax import lax
from jax.experimental import pallas as pl
from jax.experimental.pallas import tpu as pltpu
from jax.sharding import PartitionSpec as P

F32 = jnp.float32
BF16 = jnp.bfloat16
LANES = 128
CAP = 16
ROWS_T = (((1,), (1,)), ((), ()))
COLS_T = (((0,), (0,)), ((), ()))


def dot(a, b, dims=(((1,), (0,)), ((), ()))):
    return lax.dot_general(a, b, dims, preferred_element_type=F32)


def in_edge_order(first_tile, values):
    half = values.shape[1] // 2
    swapped = jnp.concatenate([values[:, half:], values[:, :half]], axis=1)
    return jnp.where(first_tile == 0, values, swapped)


def earlier_slots(slots):
    earlier = (
        lax.broadcasted_iota(jnp.int32, (slots, slots), 0)
        < lax.broadcasted_iota(jnp.int32, (slots, slots), 1)
    )
    return jnp.where(earlier, 1.0, 0.0).astype(BF16)


def slot_places(owners, peers, earlier):
    slots = owners.shape[1]
    named = lax.broadcasted_iota(jnp.int32, (peers, slots), 0) == owners
    named = jnp.where(named, 1.0, 0.0)
    rank = dot(named.astype(BF16), earlier)
    return named, jnp.sum(named * rank, axis=0, keepdims=True).astype(jnp.int32)


def request_kernel(tile_in, owner_in, row_in, ids_ref, tile_ref, owner_ref, row_ref, sems):
    copies = [
        pltpu.make_async_copy(tile_in, tile_ref, sems.at[0]),
        pltpu.make_async_copy(owner_in, owner_ref, sems.at[1]),
        pltpu.make_async_copy(row_in, row_ref, sems.at[2]),
    ]
    for copy in copies:
        copy.start()
    earlier = earlier_slots(owner_ref.shape[1])
    for copy in copies:
        copy.wait()
    peers = ids_ref.shape[0]
    first = tile_ref[0, 0]
    owners = in_edge_order(first, owner_ref[...])
    rows = in_edge_order(first, row_ref[...])
    named, place = slot_places(owners, peers, earlier)
    spot = lax.broadcasted_iota(jnp.int32, (LANES, rows.shape[1]), 0) == place
    spot = jnp.where(spot, 1.0, 0.0).astype(BF16)
    low = named * (rows % LANES).astype(F32)
    high = named * (rows // LANES).astype(F32)
    ids = dot(jnp.concatenate([low, high], axis=0).astype(BF16), spot, ROWS_T)
    ids = ids[:peers] + LANES * ids[peers:]
    ids_ref[...] = ids.astype(jnp.int32).reshape(ids_ref.shape)


def gather_kernel(ids_ref, table_ref, taken_ref, pick):
    table_rows, width = table_ref.shape
    peers = ids_ref.shape[0]
    ids = ids_ref[...].reshape(peers, LANES).astype(F32)
    ids = jnp.concatenate([ids, jnp.zeros((LANES - peers, LANES), F32)], axis=0)
    by_place = ids.T.astype(jnp.int32)
    columns = lax.broadcasted_iota(jnp.int32, (CAP, table_rows), 1)
    for g in range(peers):
        chosen = columns == by_place[:CAP, g : g + 1]
        pick[g * CAP : (g + 1) * CAP, :] = jnp.where(chosen, 1.0, 0.0).astype(BF16)
    part = peers // 4
    for start in range(0, peers, part):
        emb = dot(pick[start * CAP : (start + part) * CAP, :], table_ref[...])
        taken_ref[start : start + part] = emb.astype(BF16).reshape(part, CAP, width)


def coef_kernel(
    peers, node_rows, tile_in, owner_in, row_in, edge_in, all_ref, inside_ref, tile_ref, owner_ref,
    row_ref, edge_ref, sems
):
    copies = [
        pltpu.make_async_copy(tile_in, tile_ref, sems.at[0]),
        pltpu.make_async_copy(owner_in, owner_ref, sems.at[1]),
        pltpu.make_async_copy(row_in, row_ref, sems.at[2]),
        pltpu.make_async_copy(edge_in, edge_ref, sems.at[3]),
    ]
    for copy in copies:
        copy.start()
    earlier = earlier_slots(owner_ref.shape[1])
    for copy in copies:
        copy.wait()
    first = tile_ref[0, 0]
    owners = in_edge_order(first, owner_ref[...])
    rows = in_edge_order(first, row_ref[...])
    _, place = slot_places(owners, peers, earlier)
    target = owners * CAP + place
    at = lax.broadcasted_iota(jnp.int32, (peers * CAP, target.shape[1]), 0) == target
    moved = jnp.where(at, 1.0, 0.0)
    all_ref[...] = dot(edge_ref[...], moved.astype(BF16), ROWS_T).astype(BF16)
    kept = jnp.where(rows < node_rows, moved, 0.0).astype(BF16)
    inside_ref[...] = dot(edge_ref[...], kept, ROWS_T).astype(BF16)


def forward_kernel(
    pulled_ref,
    all_ref,
    feats_ref,
    weight_ref,
    grad_ref,
    pair_ref,
):
    width = feats_ref.shape[1]
    pulled = pulled_ref[...].reshape(-1, width)
    mixed = (feats_ref[...].astype(F32) + dot(all_ref[...], pulled)).astype(BF16)
    pre = dot(mixed, weight_ref[...])
    gate = jax.nn.sigmoid(pre)
    grad_pre = (grad_ref[...].astype(F32) * gate * (1.0 + pre * (1.0 - gate))).astype(BF16)
    pair_ref[:, :width] = mixed
    pair_ref[:, width:] = grad_pre


def term_kernel(peers, width, pairs_ref, term_out, term_ref, sems):
    half = width // 2
    second_core = lax.axis_index("hist") % 2 == 1
    pairs = pairs_ref[...].reshape(-1, 2 * width)
    left, right = pairs[:, width : width + half], pairs[:, width + half :]
    grad_pre = jnp.where(second_core, right, left)
    share = width // peers
    step = 8
    copies = []
    terms = dot(pairs[:, :width], grad_pre, COLS_T)
    for part in range(2):
        term = terms[part * half : (part + 1) * half, :]
        first = part * (peers // 2)
        for peer in range(peers // 2):
            blocks = [
                term[peer * share + i : peer * share + i + step, :] for i in range(0, share, step)
            ]
            term_ref[first + peer] = jnp.concatenate(blocks, axis=1).astype(BF16)
        copies.append(
            pltpu.make_async_copy(
                term_ref.at[first : first + peers // 2],
                term_out.at[first : first + peers // 2],
                sems.at[part],
            )
        )
        copies[-1].start()
    for copy in copies:
        copy.wait()


def backward_kernel(
    pair_ref,
    weight_ref,
    inside_ref,
    pick_in,
    history_in,
    send_ref,
    mixed_ref,
    out_ref,
    pick,
    aux,
    sems,
):
    node_rows, width = mixed_ref.shape
    peers = send_ref.shape[0]
    load_pick = pltpu.make_async_copy(pick_in, pick, sems.at[0])
    load_aux = pltpu.make_async_copy(history_in.at[:, width:], aux, sems.at[1])
    load_pick.start()
    load_aux.start()
    grad_mixed = dot(pair_ref[:, width:], weight_ref[...], ROWS_T).astype(BF16)
    mixed_ref[...] = grad_mixed
    slot_grad = dot(inside_ref[...], grad_mixed, COLS_T).astype(BF16)
    send_ref[:, :, :width] = slot_grad.reshape(peers, CAP, width)
    pre = dot(pair_ref[:, :width], weight_ref[...])
    out_ref[...] = (pre * jax.nn.sigmoid(pre)).astype(BF16)
    load_pick.wait()
    load_aux.wait()
    taken = dot(pick[:, node_rows:], aux[...]).astype(BF16)
    send_ref[:, :, width:] = taken.reshape(peers, CAP, width)


def weight_kernel(terms_ref, sum_ref):
    peers, step = terms_ref.shape[:2]
    for core in range(2):
        total = terms_ref[core].astype(F32)
        for peer in range(core + 2, peers, 2):
            total = total + terms_ref[peer].astype(F32)
        sum_ref[core * step : (core + 1) * step, :] = total.astype(BF16)


def add_kernel(near_ref, sum_ref):
    sum_ref[...] = jnp.sum(near_ref[...].astype(F32), axis=0).astype(BF16)


def final_kernel(
    back_ref, pick_ref, all_ref, mixed_ref, far_ref, grad_ref, share_ref
):
    total = jnp.sum(far_ref[...].astype(F32), axis=0)
    share, width = share_ref.shape
    half = width // 2
    step = total.shape[0] // 2
    for i in range(share // step):
        for core in range(2):
            share_ref[i * step : (i + 1) * step, core * half : (core + 1) * half] = total[
                core * step : (core + 1) * step, i * half : (i + 1) * half
            ]
    peers = back_ref.shape[0]
    node_rows = mixed_ref.shape[0]
    slots = back_ref[:, :, :width].reshape(peers * CAP, width)
    aux = back_ref[:, :, width:].reshape(peers * CAP, width)
    returned = dot(pick_ref[:, :node_rows], slots, COLS_T)
    compensation = dot(all_ref[...], aux)
    grad = mixed_ref[...].astype(F32) + returned + compensation
    grad_ref[...] = grad.astype(BF16)


def call(kernel, out_shape, *args, smem=(), hbm=(), hbm_out=(), scratch=(), vmem=32, cost=None):
    spaces = [
        pltpu.SMEM if i in smem else pltpu.HBM if i in hbm else pltpu.VMEM
        for i in range(len(args))
    ]
    single = not isinstance(out_shape, (list, tuple))
    out_shape = [out_shape] if single else out_shape
    out_spaces = [pltpu.HBM if i in hbm_out else pltpu.VMEM for i in range(len(out_shape))]
    result = pl.pallas_call(
        kernel,
        out_shape=out_shape,
        in_specs=[pl.BlockSpec(memory_space=space) for space in spaces],
        out_specs=[pl.BlockSpec(memory_space=space) for space in out_spaces],
        scratch_shapes=list(scratch),
        compiler_params=pltpu.CompilerParams(vmem_limit_bytes=vmem << 20),
        cost_estimate=cost,
    )(*args)
    return result[0] if single else result


def swap(values, axis="hist", groups=None):
    return lax.all_to_all(
        values, axis, split_axis=0, concat_axis=0, tiled=True, axis_index_groups=groups
    )


def body(feats, history, weight, edge_coef, tile_map, nbr_owner, nbr_row, grad_out):
    peers = lax.axis_size("hist")
    planes = lax.axis_size("batch")
    node_rows, width = feats.shape[1:]
    table_rows = history.shape[0]
    slots = nbr_row.shape[1]
    assert 2 * slots // peers == CAP and planes == 16
    share = width // peers
    shape = jax.ShapeDtypeStruct
    owners = nbr_owner.reshape(1, slots)
    ids = call(
        request_kernel,
        shape((peers, 1, LANES), jnp.int32),
        tile_map,
        owners,
        nbr_row,
        hbm=(0, 1, 2),
        vmem=60,
        scratch=(
            pltpu.SMEM(tile_map.shape, jnp.int32),
            pltpu.VMEM(owners.shape, jnp.int32),
            pltpu.VMEM(nbr_row.shape, jnp.int32),
            pltpu.SemaphoreType.DMA((3,)),
        ),
    )
    received = swap(ids)
    coef, coef_inside = call(
        functools.partial(coef_kernel, peers, node_rows),
        [shape((node_rows, peers * CAP), BF16)] * 2,
        tile_map,
        owners,
        nbr_row,
        edge_coef[0],
        hbm=(0, 1, 2, 3),
        vmem=60,
        scratch=(
            pltpu.SMEM(tile_map.shape, jnp.int32),
            pltpu.VMEM(owners.shape, jnp.int32),
            pltpu.VMEM(nbr_row.shape, jnp.int32),
            pltpu.VMEM(edge_coef.shape[1:], BF16),
            pltpu.SemaphoreType.DMA((4,)),
        ),
    )
    table = node_rows + table_rows
    received, coef, coef_inside = lax.optimization_barrier((received, coef, coef_inside))
    taken, pick = call(
        gather_kernel,
        [shape((peers, CAP, width), BF16), shape((peers * CAP, table), BF16)],
        received,
        jnp.concatenate([feats[0], history[:, :width]], axis=0),
    )
    pulled = swap(taken)
    pair = call(
        forward_kernel,
        shape((node_rows, 2 * width), BF16),
        pulled,
        coef,
        feats[0],
        weight,
        grad_out[0],
    )
    chips = [[i, i + 1] for i in range(0, peers, 2)]
    pairs = lax.all_gather(pair, "hist", axis=0, axis_index_groups=chips)
    terms = call(
        functools.partial(term_kernel, peers, width),
        shape((peers, 8, share * width // 16), BF16),
        pairs,
        hbm_out=(0,),
        scratch=(
            pltpu.VMEM((peers, 8, share * width // 16), BF16),
            pltpu.SemaphoreType.DMA((2,)),
        ),
    )
    pair, terms = lax.optimization_barrier((pair, terms))
    terms = swap(terms)
    sent, grad_mixed, out_rows = call(
        backward_kernel,
        [
            shape((peers, CAP, 2 * width), BF16),
            shape((node_rows, width), BF16),
            shape((node_rows, width), BF16),
        ],
        pair,
        weight,
        coef_inside,
        pick,
        history,
        hbm=(3, 4),
        scratch=(
            pltpu.VMEM((peers * CAP, table), BF16),
            pltpu.VMEM((table_rows, width), BF16),
            pltpu.SemaphoreType.DMA((2,)),
        ),
    )
    sent, terms = lax.optimization_barrier((sent, terms))
    back = swap(sent)
    side = 4
    term = call(weight_kernel, shape((16, share * width // 16), BF16), terms)
    for bit in (1, 2):
        twins = [[i, i + bit] for i in range(planes) if not i & bit]
        term = lax.all_gather(term, "batch", axis=0, axis_index_groups=twins)
        term = call(add_kernel, shape(term.shape[1:], BF16), term)
    far = [[a + side * i for i in range(planes // side)] for a in range(side)]
    term = lax.all_gather(term, "batch", axis=0, axis_index_groups=far)
    grad_rows, weight_share = call(
        final_kernel,
        [shape((node_rows, width), BF16), shape((share, width), F32)],
        back,
        pick,
        coef,
        grad_mixed,
        term,
    )
    return (out_rows[None], grad_rows[None], weight_share)


def solution(mesh):
    return jax.shard_map(
        body,
        mesh=mesh,
        in_specs=(
            P(("batch", "hist"), None, None),
            P("hist", None),
            P(),
            P(("batch", "hist"), None, None),
            P(("batch", "hist"), None),
            P(("batch", "hist"), None, None),
            P(("batch", "hist"), None),
            P(("batch", "hist"), None, None),
        ),
        out_specs=(
            P(("batch", "hist"), None, None),
            P(("batch", "hist"), None, None),
            P("hist", None),
        ),
        check_vma=False,
    )
```

```python
import functools

import jax
import jax.numpy as jnp
from jax import lax
from jax.experimental import pallas as pl
from jax.experimental.pallas import tpu as pltpu
from jax.sharding import PartitionSpec as P

F32 = jnp.float32
BF16 = jnp.bfloat16
LANES = 128
CAP = 16
ROWS_T = (((1,), (1,)), ((), ()))
COLS_T = (((0,), (0,)), ((), ()))


def dot(a, b, dims=(((1,), (0,)), ((), ()))):
    return lax.dot_general(a, b, dims, preferred_element_type=F32)


def in_edge_order(first_tile, values):
    half = values.shape[1] // 2
    swapped = jnp.concatenate([values[:, half:], values[:, :half]], axis=1)
    return jnp.where(first_tile == 0, values, swapped)


def earlier_slots(slots):
    earlier = (
        lax.broadcasted_iota(jnp.int32, (slots, slots), 0)
        < lax.broadcasted_iota(jnp.int32, (slots, slots), 1)
    )
    return jnp.where(earlier, 1.0, 0.0).astype(BF16)


def slot_places(owners, peers, earlier):
    slots = owners.shape[1]
    named = lax.broadcasted_iota(jnp.int32, (peers, slots), 0) == owners
    named = jnp.where(named, 1.0, 0.0)
    rank = dot(named.astype(BF16), earlier)
    return named, jnp.sum(named * rank, axis=0, keepdims=True).astype(jnp.int32)


def request_kernel(tile_in, owner_in, row_in, ids_ref, tile_ref, owner_ref, row_ref, sems):
    copies = [
        pltpu.make_async_copy(tile_in, tile_ref, sems.at[0]),
        pltpu.make_async_copy(owner_in, owner_ref, sems.at[1]),
        pltpu.make_async_copy(row_in, row_ref, sems.at[2]),
    ]
    for copy in copies:
        copy.start()
    earlier = earlier_slots(owner_ref.shape[1])
    for copy in copies:
        copy.wait()
    peers = ids_ref.shape[0]
    first = tile_ref[0, 0]
    owners = in_edge_order(first, owner_ref[...])
    rows = in_edge_order(first, row_ref[...])
    named, place = slot_places(owners, peers, earlier)
    spot = lax.broadcasted_iota(jnp.int32, (LANES, rows.shape[1]), 0) == place
    spot = jnp.where(spot, 1.0, 0.0).astype(BF16)
    low = named * (rows % LANES).astype(F32)
    high = named * (rows // LANES).astype(F32)
    ids = dot(jnp.concatenate([low, high], axis=0).astype(BF16), spot, ROWS_T)
    ids = ids[:peers] + LANES * ids[peers:]
    ids_ref[...] = ids.astype(jnp.int32).reshape(ids_ref.shape)


def gather_kernel(ids_ref, table_ref, taken_ref, pick):
    table_rows, width = table_ref.shape
    peers = ids_ref.shape[0]
    ids = ids_ref[...].reshape(peers, LANES).astype(F32)
    ids = jnp.concatenate([ids, jnp.zeros((LANES - peers, LANES), F32)], axis=0)
    by_place = ids.T.astype(jnp.int32)
    columns = lax.broadcasted_iota(jnp.int32, (CAP, table_rows), 1)
    for g in range(peers):
        chosen = columns == by_place[:CAP, g : g + 1]
        pick[g * CAP : (g + 1) * CAP, :] = jnp.where(chosen, 1.0, 0.0).astype(BF16)
    part = peers // 4
    for start in range(0, peers, part):
        emb = dot(pick[start * CAP : (start + part) * CAP, :], table_ref[...])
        taken_ref[start : start + part] = emb.astype(BF16).reshape(part, CAP, width)


def coef_kernel(
    peers, node_rows, tile_in, owner_in, row_in, edge_in, all_ref, inside_ref, tile_ref, owner_ref,
    row_ref, edge_ref, sems
):
    copies = [
        pltpu.make_async_copy(tile_in, tile_ref, sems.at[0]),
        pltpu.make_async_copy(owner_in, owner_ref, sems.at[1]),
        pltpu.make_async_copy(row_in, row_ref, sems.at[2]),
        pltpu.make_async_copy(edge_in, edge_ref, sems.at[3]),
    ]
    for copy in copies:
        copy.start()
    earlier = earlier_slots(owner_ref.shape[1])
    for copy in copies:
        copy.wait()
    first = tile_ref[0, 0]
    owners = in_edge_order(first, owner_ref[...])
    rows = in_edge_order(first, row_ref[...])
    _, place = slot_places(owners, peers, earlier)
    target = owners * CAP + place
    at = lax.broadcasted_iota(jnp.int32, (peers * CAP, target.shape[1]), 0) == target
    moved = jnp.where(at, 1.0, 0.0)
    all_ref[...] = dot(edge_ref[...], moved.astype(BF16), ROWS_T).astype(BF16)
    kept = jnp.where(rows < node_rows, moved, 0.0).astype(BF16)
    inside_ref[...] = dot(edge_ref[...], kept, ROWS_T).astype(BF16)


def forward_kernel(
    pulled_ref,
    all_ref,
    feats_ref,
    weight_ref,
    grad_ref,
    pair_ref,
):
    width = feats_ref.shape[1]
    pulled = pulled_ref[...].reshape(-1, width)
    mixed = (feats_ref[...].astype(F32) + dot(all_ref[...], pulled)).astype(BF16)
    pre = dot(mixed, weight_ref[...])
    gate = jax.nn.sigmoid(pre)
    grad_pre = (grad_ref[...].astype(F32) * gate * (1.0 + pre * (1.0 - gate))).astype(BF16)
    pair_ref[:, :width] = mixed
    pair_ref[:, width:] = grad_pre


def term_kernel(peers, width, pairs_ref, term_out, term_ref, sems):
    half = width // 2
    second_core = lax.axis_index("hist") % 2 == 1
    pairs = pairs_ref[...].reshape(-1, 2 * width)
    left, right = pairs[:, width : width + half], pairs[:, width + half :]
    grad_pre = jnp.where(second_core, right, left)
    share = width // peers
    step = 8
    copies = []
    terms = dot(pairs[:, :width], grad_pre, COLS_T)
    for part in range(2):
        term = terms[part * half : (part + 1) * half, :]
        first = part * (peers // 2)
        for peer in range(peers // 2):
            blocks = [
                term[peer * share + i : peer * share + i + step, :] for i in range(0, share, step)
            ]
            term_ref[first + peer] = jnp.concatenate(blocks, axis=1).astype(BF16)
        copies.append(
            pltpu.make_async_copy(
                term_ref.at[first : first + peers // 2],
                term_out.at[first : first + peers // 2],
                sems.at[part],
            )
        )
        copies[-1].start()
    for copy in copies:
        copy.wait()


def backward_kernel(
    pair_ref,
    weight_ref,
    inside_ref,
    pick_in,
    history_in,
    send_ref,
    mixed_ref,
    out_ref,
    pick,
    aux,
    sems,
):
    node_rows, width = mixed_ref.shape
    peers = send_ref.shape[0]
    load_pick = pltpu.make_async_copy(pick_in, pick, sems.at[0])
    load_aux = pltpu.make_async_copy(history_in.at[:, width:], aux, sems.at[1])
    load_pick.start()
    load_aux.start()
    grad_mixed = dot(pair_ref[:, width:], weight_ref[...], ROWS_T).astype(BF16)
    mixed_ref[...] = grad_mixed
    slot_grad = dot(inside_ref[...], grad_mixed, COLS_T).astype(BF16)
    send_ref[:, :, :width] = slot_grad.reshape(peers, CAP, width)
    pre = dot(pair_ref[:, :width], weight_ref[...])
    out_ref[...] = (pre * jax.nn.sigmoid(pre)).astype(BF16)
    load_pick.wait()
    load_aux.wait()
    taken = dot(pick[:, node_rows:], aux[...]).astype(BF16)
    send_ref[:, :, width:] = taken.reshape(peers, CAP, width)


def weight_kernel(terms_ref, sum_ref):
    peers, step = terms_ref.shape[:2]
    for core in range(2):
        total = terms_ref[core].astype(F32)
        for peer in range(core + 2, peers, 2):
            total = total + terms_ref[peer].astype(F32)
        sum_ref[core * step : (core + 1) * step, :] = total.astype(BF16)


def add_kernel(near_ref, sum_ref):
    sum_ref[...] = jnp.sum(near_ref[...].astype(F32), axis=0).astype(BF16)


def final_kernel(
    back_ref, pick_ref, all_ref, mixed_ref, far_ref, grad_ref, share_ref
):
    total = jnp.sum(far_ref[...].astype(F32), axis=0)
    share, width = share_ref.shape
    half = width // 2
    step = total.shape[0] // 2
    for i in range(share // step):
        for core in range(2):
            share_ref[i * step : (i + 1) * step, core * half : (core + 1) * half] = total[
                core * step : (core + 1) * step, i * half : (i + 1) * half
            ]
    peers = back_ref.shape[0]
    node_rows = mixed_ref.shape[0]
    slots = back_ref[:, :, :width].reshape(peers * CAP, width)
    aux = back_ref[:, :, width:].reshape(peers * CAP, width)
    returned = dot(pick_ref[:, :node_rows], slots, COLS_T)
    compensation = dot(all_ref[...], aux)
    grad = mixed_ref[...].astype(F32) + returned + compensation
    grad_ref[...] = grad.astype(BF16)


def call(kernel, out_shape, *args, smem=(), hbm=(), hbm_out=(), scratch=(), vmem=32, cost=None):
    spaces = [
        pltpu.SMEM if i in smem else pltpu.HBM if i in hbm else pltpu.VMEM
        for i in range(len(args))
    ]
    single = not isinstance(out_shape, (list, tuple))
    out_shape = [out_shape] if single else out_shape
    out_spaces = [pltpu.HBM if i in hbm_out else pltpu.VMEM for i in range(len(out_shape))]
    result = pl.pallas_call(
        kernel,
        out_shape=out_shape,
        in_specs=[pl.BlockSpec(memory_space=space) for space in spaces],
        out_specs=[pl.BlockSpec(memory_space=space) for space in out_spaces],
        scratch_shapes=list(scratch),
        compiler_params=pltpu.CompilerParams(vmem_limit_bytes=vmem << 20),
        cost_estimate=cost,
    )(*args)
    return result[0] if single else result


def swap(values, axis="hist", groups=None):
    return lax.all_to_all(
        values, axis, split_axis=0, concat_axis=0, tiled=True, axis_index_groups=groups
    )


def body(feats, history, weight, edge_coef, tile_map, nbr_owner, nbr_row, grad_out):
    peers = lax.axis_size("hist")
    planes = lax.axis_size("batch")
    node_rows, width = feats.shape[1:]
    table_rows = history.shape[0]
    slots = nbr_row.shape[1]
    assert 2 * slots // peers == CAP and planes == 16
    share = width // peers
    shape = jax.ShapeDtypeStruct
    owners = nbr_owner.reshape(1, slots)
    ids = call(
        request_kernel,
        shape((peers, 1, LANES), jnp.int32),
        tile_map,
        owners,
        nbr_row,
        hbm=(0, 1, 2),
        vmem=60,
        scratch=(
            pltpu.SMEM(tile_map.shape, jnp.int32),
            pltpu.VMEM(owners.shape, jnp.int32),
            pltpu.VMEM(nbr_row.shape, jnp.int32),
            pltpu.SemaphoreType.DMA((3,)),
        ),
    )
    received = swap(ids)
    coef, coef_inside = call(
        functools.partial(coef_kernel, peers, node_rows),
        [shape((node_rows, peers * CAP), BF16)] * 2,
        tile_map,
        owners,
        nbr_row,
        edge_coef[0],
        hbm=(0, 1, 2, 3),
        vmem=60,
        scratch=(
            pltpu.SMEM(tile_map.shape, jnp.int32),
            pltpu.VMEM(owners.shape, jnp.int32),
            pltpu.VMEM(nbr_row.shape, jnp.int32),
            pltpu.VMEM(edge_coef.shape[1:], BF16),
            pltpu.SemaphoreType.DMA((4,)),
        ),
    )
    table = node_rows + table_rows
    received, coef, coef_inside = lax.optimization_barrier((received, coef, coef_inside))
    taken, pick = call(
        gather_kernel,
        [shape((peers, CAP, width), BF16), shape((peers * CAP, table), BF16)],
        received,
        jnp.concatenate([feats[0], history[:, :width]], axis=0),
    )
    pulled = swap(taken)
    pair = call(
        forward_kernel,
        shape((node_rows, 2 * width), BF16),
        pulled,
        coef,
        feats[0],
        weight,
        grad_out[0],
    )
    chips = [[i, i + 1] for i in range(0, peers, 2)]
    pairs = lax.all_gather(pair, "hist", axis=0, axis_index_groups=chips)
    terms = call(
        functools.partial(term_kernel, peers, width),
        shape((peers, 8, share * width // 16), BF16),
        pairs,
        hbm_out=(0,),
        scratch=(
            pltpu.VMEM((peers, 8, share * width // 16), BF16),
            pltpu.SemaphoreType.DMA((2,)),
        ),
    )
    pair, terms = lax.optimization_barrier((pair, terms))
    terms = swap(terms)
    sent, grad_mixed, out_rows = call(
        backward_kernel,
        [
            shape((peers, CAP, 2 * width), BF16),
            shape((node_rows, width), BF16),
            shape((node_rows, width), BF16),
        ],
        pair,
        weight,
        coef_inside,
        pick,
        history,
        hbm=(3, 4),
        scratch=(
            pltpu.VMEM((peers * CAP, table), BF16),
            pltpu.VMEM((table_rows, width), BF16),
            pltpu.SemaphoreType.DMA((2,)),
        ),
    )
    sent, terms = lax.optimization_barrier((sent, terms))
    back = swap(sent)
    side = 4
    term = call(weight_kernel, shape((16, share * width // 16), BF16), terms)
    for bit in (1, 2):
        twins = [[i, i + bit] for i in range(planes) if not i & bit]
        term = lax.all_gather(term, "batch", axis=0, axis_index_groups=twins)
        term = call(add_kernel, shape(term.shape[1:], BF16), term)
    late = planes // 2
    far = [[(late + a + side * i) % planes for i in range(planes // side)] for a in range(side)]
    term = lax.all_gather(term, "batch", axis=0, axis_index_groups=far)
    grad_rows, weight_share = call(
        final_kernel,
        [shape((node_rows, width), BF16), shape((share, width), F32)],
        back,
        pick,
        coef,
        grad_mixed,
        term,
    )
    return (out_rows[None], grad_rows[None], weight_share)


def solution(mesh):
    return jax.shard_map(
        body,
        mesh=mesh,
        in_specs=(
            P(("batch", "hist"), None, None),
            P("hist", None),
            P(),
            P(("batch", "hist"), None, None),
            P(("batch", "hist"), None),
            P(("batch", "hist"), None, None),
            P(("batch", "hist"), None),
            P(("batch", "hist"), None, None),
        ),
        out_specs=(
            P(("batch", "hist"), None, None),
            P(("batch", "hist"), None, None),
            P("hist", None),
        ),
        check_vma=False,
    )
```

```python
import functools

import jax
import jax.numpy as jnp
from jax import lax
from jax.experimental import pallas as pl
from jax.experimental.pallas import tpu as pltpu
from jax.sharding import PartitionSpec as P

F32 = jnp.float32
BF16 = jnp.bfloat16
LANES = 128
CAP = 16
ROWS_T = (((1,), (1,)), ((), ()))
COLS_T = (((0,), (0,)), ((), ()))


def dot(a, b, dims=(((1,), (0,)), ((), ()))):
    return lax.dot_general(a, b, dims, preferred_element_type=F32)


def sigmoid(values):
    return 1.0 / (1.0 + jnp.exp(-values))


def in_edge_order(first_tile, values):
    half = values.shape[1] // 2
    swapped = jnp.concatenate([values[:, half:], values[:, :half]], axis=1)
    return jnp.where(first_tile == 0, values, swapped)


def earlier_slots(slots):
    earlier = (
        lax.broadcasted_iota(jnp.int32, (slots, slots), 0)
        < lax.broadcasted_iota(jnp.int32, (slots, slots), 1)
    )
    return jnp.where(earlier, 1.0, 0.0).astype(BF16)


def slot_places(owners, peers, earlier):
    slots = owners.shape[1]
    named = lax.broadcasted_iota(jnp.int32, (peers, slots), 0) == owners
    named = jnp.where(named, 1.0, 0.0)
    rank = dot(named.astype(BF16), earlier)
    return named, jnp.sum(named * rank, axis=0, keepdims=True).astype(jnp.int32)


def request_kernel(tile_in, owner_in, row_in, ids_ref, tile_ref, owner_ref, row_ref, sems):
    copies = [
        pltpu.make_async_copy(tile_in, tile_ref, sems.at[0]),
        pltpu.make_async_copy(owner_in, owner_ref, sems.at[1]),
        pltpu.make_async_copy(row_in, row_ref, sems.at[2]),
    ]
    for copy in copies:
        copy.start()
    earlier = earlier_slots(owner_ref.shape[1])
    for copy in copies:
        copy.wait()
    peers = ids_ref.shape[0]
    first = tile_ref[0, 0]
    owners = in_edge_order(first, owner_ref[...])
    rows = in_edge_order(first, row_ref[...])
    named, place = slot_places(owners, peers, earlier)
    spot = lax.broadcasted_iota(jnp.int32, (LANES, rows.shape[1]), 0) == place
    spot = jnp.where(spot, 1.0, 0.0).astype(BF16)
    low = (rows % LANES).astype(F32)
    high = (rows // LANES).astype(F32)
    ids = dot((named * low).astype(BF16), spot, ROWS_T) + LANES * dot(
        (named * high).astype(BF16), spot, ROWS_T
    )
    ids_ref[...] = ids.astype(jnp.int32).reshape(ids_ref.shape)


def gather_kernel(ids_ref, table_ref, taken_ref, pick):
    table_rows, width = table_ref.shape
    peers = ids_ref.shape[0]
    ids = ids_ref[...].reshape(peers, LANES).astype(F32)
    ids = jnp.concatenate([ids, jnp.zeros((LANES - peers, LANES), F32)], axis=0)
    by_place = ids.T.astype(jnp.int32)
    columns = lax.broadcasted_iota(jnp.int32, (CAP, table_rows), 1)
    for g in range(peers):
        chosen = columns == by_place[:CAP, g : g + 1]
        pick[g * CAP : (g + 1) * CAP, :] = jnp.where(chosen, 1.0, 0.0).astype(BF16)
    part = peers // 4
    for start in range(0, peers, part):
        emb = dot(pick[start * CAP : (start + part) * CAP, :], table_ref[...])
        taken_ref[start : start + part] = emb.astype(BF16).reshape(part, CAP, width)


def coef_kernel(
    peers, node_rows, tile_in, owner_in, row_in, edge_in, all_ref, inside_ref, tile_ref, owner_ref,
    row_ref, edge_ref, sems
):
    copies = [
        pltpu.make_async_copy(tile_in, tile_ref, sems.at[0]),
        pltpu.make_async_copy(owner_in, owner_ref, sems.at[1]),
        pltpu.make_async_copy(row_in, row_ref, sems.at[2]),
        pltpu.make_async_copy(edge_in, edge_ref, sems.at[3]),
    ]
    for copy in copies:
        copy.start()
    earlier = earlier_slots(owner_ref.shape[1])
    for copy in copies:
        copy.wait()
    first = tile_ref[0, 0]
    owners = in_edge_order(first, owner_ref[...])
    rows = in_edge_order(first, row_ref[...])
    _, place = slot_places(owners, peers, earlier)
    target = owners * CAP + place
    at = lax.broadcasted_iota(jnp.int32, (peers * CAP, target.shape[1]), 0) == target
    moved = jnp.where(at, 1.0, 0.0)
    all_ref[...] = dot(edge_ref[...], moved.astype(BF16), ROWS_T).astype(BF16)
    kept = jnp.where(rows < node_rows, moved, 0.0).astype(BF16)
    inside_ref[...] = dot(edge_ref[...], kept, ROWS_T).astype(BF16)


def forward_kernel(
    pulled_ref,
    all_ref,
    feats_ref,
    weight_ref,
    grad_ref,
    pair_ref,
):
    width = feats_ref.shape[1]
    pulled = pulled_ref[...].reshape(-1, width)
    mixed = (feats_ref[...].astype(F32) + dot(all_ref[...], pulled)).astype(BF16)
    pre = dot(mixed, weight_ref[...])
    gate = sigmoid(pre)
    grad_pre = (grad_ref[...].astype(F32) * gate * (1.0 + pre * (1.0 - gate))).astype(BF16)
    pair_ref[:, :width] = mixed
    pair_ref[:, width:] = grad_pre


def term_kernel(peers, width, pairs_ref, term_ref):
    half = width // 2
    second_core = lax.axis_index("hist") % 2 == 1
    pairs = pairs_ref[...].reshape(-1, 2 * width)
    mixed = pairs[:, :width]
    left, right = pairs[:, width : width + half], pairs[:, width + half :]
    grad_pre = jnp.where(second_core, right, left)
    share = width // peers
    step = 8
    term = dot(mixed, grad_pre, COLS_T)
    for peer in range(peers):
        blocks = [
            term[peer * share + i : peer * share + i + step, :] for i in range(0, share, step)
        ]
        term_ref[peer] = jnp.concatenate(blocks, axis=1).astype(BF16)


def backward_kernel(
    pair_ref,
    weight_ref,
    inside_ref,
    pick_in,
    history_in,
    send_ref,
    mixed_ref,
    out_ref,
    pick,
    aux,
    sems,
):
    node_rows, width = mixed_ref.shape
    peers = send_ref.shape[0]
    load_pick = pltpu.make_async_copy(pick_in, pick, sems.at[0])
    load_aux = pltpu.make_async_copy(history_in.at[:, width:], aux, sems.at[1])
    load_pick.start()
    load_aux.start()
    grad_mixed = dot(pair_ref[:, width:], weight_ref[...], ROWS_T).astype(BF16)
    mixed_ref[...] = grad_mixed
    slot_grad = dot(inside_ref[...], grad_mixed, COLS_T).astype(BF16)
    send_ref[:, :, :width] = slot_grad.reshape(peers, CAP, width)
    pre = dot(pair_ref[:, :width], weight_ref[...])
    out_ref[...] = (pre * sigmoid(pre)).astype(BF16)
    load_pick.wait()
    load_aux.wait()
    taken = dot(pick[:, node_rows:], aux[...]).astype(BF16)
    send_ref[:, :, width:] = taken.reshape(peers, CAP, width)


def weight_kernel(terms_ref, sum_ref):
    peers, step = terms_ref.shape[:2]
    for core in range(2):
        total = terms_ref[core].astype(F32)
        for peer in range(core + 2, peers, 2):
            total = total + terms_ref[peer].astype(F32)
        total = total.astype(BF16)
        for plane in range(sum_ref.shape[0]):
            sum_ref[plane, core * step : (core + 1) * step, :] = total


def add_kernel(near_ref, sum_ref):
    sum_ref[...] = jnp.sum(near_ref[...].astype(F32), axis=0).astype(BF16)


def final_kernel(
    back_ref, pick_ref, all_ref, mixed_ref, far_ref, grad_ref, share_ref
):
    total = jnp.sum(far_ref[...].astype(F32), axis=0)
    share, width = share_ref.shape
    half = width // 2
    step = total.shape[0] // 2
    for i in range(share // step):
        for core in range(2):
            share_ref[i * step : (i + 1) * step, core * half : (core + 1) * half] = total[
                core * step : (core + 1) * step, i * half : (i + 1) * half
            ]
    peers = back_ref.shape[0]
    node_rows = mixed_ref.shape[0]
    slots = back_ref[:, :, :width].reshape(peers * CAP, width)
    aux = back_ref[:, :, width:].reshape(peers * CAP, width)
    returned = dot(pick_ref[:, :node_rows], slots, COLS_T)
    compensation = dot(all_ref[...], aux)
    grad = mixed_ref[...].astype(F32) + returned + compensation
    grad_ref[...] = grad.astype(BF16)


def call(kernel, out_shape, *args, smem=(), hbm=(), hbm_out=(), scratch=(), vmem=32, cost=None):
    spaces = [
        pltpu.SMEM if i in smem else pltpu.HBM if i in hbm else pltpu.VMEM
        for i in range(len(args))
    ]
    single = not isinstance(out_shape, (list, tuple))
    out_shape = [out_shape] if single else out_shape
    out_spaces = [pltpu.HBM if i in hbm_out else pltpu.VMEM for i in range(len(out_shape))]
    result = pl.pallas_call(
        kernel,
        out_shape=out_shape,
        in_specs=[pl.BlockSpec(memory_space=space) for space in spaces],
        out_specs=[pl.BlockSpec(memory_space=space) for space in out_spaces],
        scratch_shapes=list(scratch),
        compiler_params=pltpu.CompilerParams(vmem_limit_bytes=vmem << 20),
        cost_estimate=cost,
    )(*args)
    return result[0] if single else result


def swap(values, axis="hist", groups=None):
    return lax.all_to_all(
        values, axis, split_axis=0, concat_axis=0, tiled=True, axis_index_groups=groups
    )


def body(feats, history, weight, edge_coef, tile_map, nbr_owner, nbr_row, grad_out):
    peers = lax.axis_size("hist")
    planes = lax.axis_size("batch")
    node_rows, width = feats.shape[1:]
    table_rows = history.shape[0]
    slots = nbr_row.shape[1]
    assert 2 * slots // peers == CAP and planes == 16
    share = width // peers
    shape = jax.ShapeDtypeStruct
    owners = nbr_owner.reshape(1, slots)
    ids = call(
        request_kernel,
        shape((peers, 1, LANES), jnp.int32),
        tile_map,
        owners,
        nbr_row,
        hbm=(0, 1, 2),
        vmem=60,
        scratch=(
            pltpu.SMEM(tile_map.shape, jnp.int32),
            pltpu.VMEM(owners.shape, jnp.int32),
            pltpu.VMEM(nbr_row.shape, jnp.int32),
            pltpu.SemaphoreType.DMA((3,)),
        ),
    )
    received = swap(ids)
    coef, coef_inside = call(
        functools.partial(coef_kernel, peers, node_rows),
        [shape((node_rows, peers * CAP), BF16)] * 2,
        tile_map,
        owners,
        nbr_row,
        edge_coef[0],
        hbm=(0, 1, 2, 3),
        vmem=60,
        scratch=(
            pltpu.SMEM(tile_map.shape, jnp.int32),
            pltpu.VMEM(owners.shape, jnp.int32),
            pltpu.VMEM(nbr_row.shape, jnp.int32),
            pltpu.VMEM(edge_coef.shape[1:], BF16),
            pltpu.SemaphoreType.DMA((4,)),
        ),
    )
    table = node_rows + table_rows
    received, coef, coef_inside = lax.optimization_barrier((received, coef, coef_inside))
    taken, pick = call(
        gather_kernel,
        [shape((peers, CAP, width), BF16), shape((peers * CAP, table), BF16)],
        received,
        jnp.concatenate([feats[0], history[:, :width]], axis=0),
    )
    pulled = swap(taken)
    pair = call(
        forward_kernel,
        shape((node_rows, 2 * width), BF16),
        pulled,
        coef,
        feats[0],
        weight,
        grad_out[0],
    )
    chips = [[i, i + 1] for i in range(0, peers, 2)]
    pairs = lax.all_gather(pair, "hist", axis=0, axis_index_groups=chips)
    terms = call(
        functools.partial(term_kernel, peers, width),
        shape((peers, 8, share * width // 16), BF16),
        pairs,
    )
    pair, terms = lax.optimization_barrier((pair, terms))
    terms = swap(terms)
    sent, grad_mixed, out_rows = call(
        backward_kernel,
        [
            shape((peers, CAP, 2 * width), BF16),
            shape((node_rows, width), BF16),
            shape((node_rows, width), BF16),
        ],
        pair,
        weight,
        coef_inside,
        pick,
        history,
        hbm=(3, 4),
        scratch=(
            pltpu.VMEM((peers * CAP, table), BF16),
            pltpu.VMEM((table_rows, width), BF16),
            pltpu.SemaphoreType.DMA((2,)),
        ),
    )
    side = 4
    near = [[a * side + i for i in range(side)] for a in range(planes // side)]
    term = call(weight_kernel, shape((side, 16, share * width // 16), BF16), terms)
    term = swap(term, "batch", near)
    sent, term = lax.optimization_barrier((sent, term))
    back = swap(sent)
    term = call(add_kernel, shape(term.shape[1:], BF16), term)
    far = [[a + side * i for i in range(planes // side)] for a in range(side)]
    term = lax.all_gather(term, "batch", axis=0, axis_index_groups=far)
    grad_rows, weight_share = call(
        final_kernel,
        [shape((node_rows, width), BF16), shape((share, width), F32)],
        back,
        pick,
        coef,
        grad_mixed,
        term,
    )
    return (out_rows[None], grad_rows[None], weight_share)


def solution(mesh):
    return jax.shard_map(
        body,
        mesh=mesh,
        in_specs=(
            P(("batch", "hist"), None, None),
            P("hist", None),
            P(),
            P(("batch", "hist"), None, None),
            P(("batch", "hist"), None),
            P(("batch", "hist"), None, None),
            P(("batch", "hist"), None),
            P(("batch", "hist"), None, None),
        ),
        out_specs=(
            P(("batch", "hist"), None, None),
            P(("batch", "hist"), None, None),
            P("hist", None),
        ),
        check_vma=False,
    )
```

```python
import functools

import jax
import jax.numpy as jnp
from jax import lax
from jax.experimental import pallas as pl
from jax.experimental.pallas import tpu as pltpu
from jax.sharding import PartitionSpec as P

F32 = jnp.float32
BF16 = jnp.bfloat16
LANES = 128
CAP = 16
ROWS_T = (((1,), (1,)), ((), ()))
COLS_T = (((0,), (0,)), ((), ()))


def dot(a, b, dims=(((1,), (0,)), ((), ()))):
    return lax.dot_general(a, b, dims, preferred_element_type=F32)


def sigmoid(values):
    return 1.0 / (1.0 + jnp.exp(-values))


def in_edge_order(first_tile, values):
    half = values.shape[1] // 2
    swapped = jnp.concatenate([values[:, half:], values[:, :half]], axis=1)
    return jnp.where(first_tile == 0, values, swapped)


def earlier_slots(slots):
    earlier = (
        lax.broadcasted_iota(jnp.int32, (slots, slots), 0)
        < lax.broadcasted_iota(jnp.int32, (slots, slots), 1)
    )
    return jnp.where(earlier, 1.0, 0.0).astype(BF16)


def slot_places(owners, peers, earlier):
    slots = owners.shape[1]
    named = lax.broadcasted_iota(jnp.int32, (peers, slots), 0) == owners
    named = jnp.where(named, 1.0, 0.0)
    rank = dot(named.astype(BF16), earlier)
    return named, jnp.sum(named * rank, axis=0, keepdims=True).astype(jnp.int32)


def request_kernel(tile_in, owner_in, row_in, ids_ref, tile_ref, owner_ref, row_ref, sems):
    copies = [
        pltpu.make_async_copy(tile_in, tile_ref, sems.at[0]),
        pltpu.make_async_copy(owner_in, owner_ref, sems.at[1]),
        pltpu.make_async_copy(row_in, row_ref, sems.at[2]),
    ]
    for copy in copies:
        copy.start()
    earlier = earlier_slots(owner_ref.shape[1])
    for copy in copies:
        copy.wait()
    peers = ids_ref.shape[0]
    first = tile_ref[0, 0]
    owners = in_edge_order(first, owner_ref[...])
    rows = in_edge_order(first, row_ref[...])
    named, place = slot_places(owners, peers, earlier)
    spot = lax.broadcasted_iota(jnp.int32, (LANES, rows.shape[1]), 0) == place
    spot = jnp.where(spot, 1.0, 0.0).astype(BF16)
    low = named * (rows % LANES).astype(F32)
    high = named * (rows // LANES).astype(F32)
    ids = dot(jnp.concatenate([low, high], axis=0).astype(BF16), spot, ROWS_T)
    ids = ids[:peers] + LANES * ids[peers:]
    ids_ref[...] = ids.astype(jnp.int32).reshape(ids_ref.shape)


def gather_kernel(ids_ref, table_ref, taken_ref, pick):
    table_rows, width = table_ref.shape
    peers = ids_ref.shape[0]
    ids = ids_ref[...].reshape(peers, LANES).astype(F32)
    ids = jnp.concatenate([ids, jnp.zeros((LANES - peers, LANES), F32)], axis=0)
    by_place = ids.T.astype(jnp.int32)
    columns = lax.broadcasted_iota(jnp.int32, (CAP, table_rows), 1)
    for g in range(peers):
        chosen = columns == by_place[:CAP, g : g + 1]
        pick[g * CAP : (g + 1) * CAP, :] = jnp.where(chosen, 1.0, 0.0).astype(BF16)
    part = peers // 4
    for start in range(0, peers, part):
        emb = dot(pick[start * CAP : (start + part) * CAP, :], table_ref[...])
        taken_ref[start : start + part] = emb.astype(BF16).reshape(part, CAP, width)


def coef_kernel(
    peers, node_rows, tile_in, owner_in, row_in, edge_in, all_ref, inside_ref, tile_ref, owner_ref,
    row_ref, edge_ref, sems
):
    copies = [
        pltpu.make_async_copy(tile_in, tile_ref, sems.at[0]),
        pltpu.make_async_copy(owner_in, owner_ref, sems.at[1]),
        pltpu.make_async_copy(row_in, row_ref, sems.at[2]),
        pltpu.make_async_copy(edge_in, edge_ref, sems.at[3]),
    ]
    for copy in copies:
        copy.start()
    earlier = earlier_slots(owner_ref.shape[1])
    for copy in copies:
        copy.wait()
    first = tile_ref[0, 0]
    owners = in_edge_order(first, owner_ref[...])
    rows = in_edge_order(first, row_ref[...])
    _, place = slot_places(owners, peers, earlier)
    target = owners * CAP + place
    at = lax.broadcasted_iota(jnp.int32, (peers * CAP, target.shape[1]), 0) == target
    moved = jnp.where(at, 1.0, 0.0)
    all_ref[...] = dot(edge_ref[...], moved.astype(BF16), ROWS_T).astype(BF16)
    kept = jnp.where(rows < node_rows, moved, 0.0).astype(BF16)
    inside_ref[...] = dot(edge_ref[...], kept, ROWS_T).astype(BF16)


def forward_kernel(
    pulled_ref,
    all_ref,
    feats_ref,
    weight_ref,
    grad_ref,
    pair_ref,
):
    width = feats_ref.shape[1]
    pulled = pulled_ref[...].reshape(-1, width)
    mixed = (feats_ref[...].astype(F32) + dot(all_ref[...], pulled)).astype(BF16)
    pre = dot(mixed, weight_ref[...])
    gate = sigmoid(pre)
    grad_pre = (grad_ref[...].astype(F32) * gate * (1.0 + pre * (1.0 - gate))).astype(BF16)
    pair_ref[:, :width] = mixed
    pair_ref[:, width:] = grad_pre


def term_kernel(peers, width, pairs_ref, term_out, term_ref, sems):
    half = width // 2
    second_core = lax.axis_index("hist") % 2 == 1
    pairs = pairs_ref[...].reshape(-1, 2 * width)
    left, right = pairs[:, width : width + half], pairs[:, width + half :]
    grad_pre = jnp.where(second_core, right, left)
    share = width // peers
    step = 8
    terms = dot(pairs[:, :width], grad_pre, COLS_T)
    parts = sems.shape[0]
    copies = []
    for part in range(parts):
        group = peers // parts
        first = part * group
        for peer in range(first, first + group):
            blocks = [
                terms[peer * share + i : peer * share + i + step, :] for i in range(0, share, step)
            ]
            term_ref[peer] = jnp.concatenate(blocks, axis=1).astype(BF16)
        copies.append(
            pltpu.make_async_copy(
                term_ref.at[first : first + group],
                term_out.at[first : first + group],
                sems.at[part],
            )
        )
        copies[-1].start()
    for copy in copies:
        copy.wait()


def backward_kernel(
    pair_ref,
    weight_ref,
    inside_ref,
    pick_in,
    history_in,
    send_ref,
    mixed_ref,
    out_ref,
    pick,
    aux,
    sems,
):
    node_rows, width = mixed_ref.shape
    peers = send_ref.shape[0]
    load_pick = pltpu.make_async_copy(pick_in, pick, sems.at[0])
    load_aux = pltpu.make_async_copy(history_in.at[:, width:], aux, sems.at[1])
    load_pick.start()
    load_aux.start()
    grad_mixed = dot(pair_ref[:, width:], weight_ref[...], ROWS_T).astype(BF16)
    mixed_ref[...] = grad_mixed
    slot_grad = dot(inside_ref[...], grad_mixed, COLS_T).astype(BF16)
    send_ref[:, :, :width] = slot_grad.reshape(peers, CAP, width)
    pre = dot(pair_ref[:, :width], weight_ref[...])
    out_ref[...] = (pre * sigmoid(pre)).astype(BF16)
    load_pick.wait()
    load_aux.wait()
    taken = dot(pick[:, node_rows:], aux[...]).astype(BF16)
    send_ref[:, :, width:] = taken.reshape(peers, CAP, width)


def weight_kernel(terms_ref, sum_ref):
    peers, step = terms_ref.shape[:2]
    for core in range(2):
        total = terms_ref[core].astype(F32)
        for peer in range(core + 2, peers, 2):
            total = total + terms_ref[peer].astype(F32)
        sum_ref[core * step : (core + 1) * step, :] = total.astype(BF16)


def add_kernel(near_ref, sum_ref):
    sum_ref[...] = jnp.sum(near_ref[...].astype(F32), axis=0).astype(BF16)


def final_kernel(
    back_ref, pick_ref, all_ref, mixed_ref, far_ref, grad_ref, share_ref
):
    total = jnp.sum(far_ref[...].astype(F32), axis=0)
    share, width = share_ref.shape
    half = width // 2
    step = total.shape[0] // 2
    for i in range(share // step):
        for core in range(2):
            share_ref[i * step : (i + 1) * step, core * half : (core + 1) * half] = total[
                core * step : (core + 1) * step, i * half : (i + 1) * half
            ]
    peers = back_ref.shape[0]
    node_rows = mixed_ref.shape[0]
    slots = back_ref[:, :, :width].reshape(peers * CAP, width)
    aux = back_ref[:, :, width:].reshape(peers * CAP, width)
    returned = dot(pick_ref[:, :node_rows], slots, COLS_T)
    compensation = dot(all_ref[...], aux)
    grad = mixed_ref[...].astype(F32) + returned + compensation
    grad_ref[...] = grad.astype(BF16)


def call(kernel, out_shape, *args, smem=(), hbm=(), hbm_out=(), scratch=(), vmem=32, cost=None):
    spaces = [
        pltpu.SMEM if i in smem else pltpu.HBM if i in hbm else pltpu.VMEM
        for i in range(len(args))
    ]
    single = not isinstance(out_shape, (list, tuple))
    out_shape = [out_shape] if single else out_shape
    out_spaces = [pltpu.HBM if i in hbm_out else pltpu.VMEM for i in range(len(out_shape))]
    result = pl.pallas_call(
        kernel,
        out_shape=out_shape,
        in_specs=[pl.BlockSpec(memory_space=space) for space in spaces],
        out_specs=[pl.BlockSpec(memory_space=space) for space in out_spaces],
        scratch_shapes=list(scratch),
        compiler_params=pltpu.CompilerParams(vmem_limit_bytes=vmem << 20),
        cost_estimate=cost,
    )(*args)
    return result[0] if single else result


def swap(values, axis="hist", groups=None):
    return lax.all_to_all(
        values, axis, split_axis=0, concat_axis=0, tiled=True, axis_index_groups=groups
    )


def body(feats, history, weight, edge_coef, tile_map, nbr_owner, nbr_row, grad_out):
    peers = lax.axis_size("hist")
    planes = lax.axis_size("batch")
    node_rows, width = feats.shape[1:]
    table_rows = history.shape[0]
    slots = nbr_row.shape[1]
    assert 2 * slots // peers == CAP and planes == 16
    share = width // peers
    shape = jax.ShapeDtypeStruct
    owners = nbr_owner.reshape(1, slots)
    ids = call(
        request_kernel,
        shape((peers, 1, LANES), jnp.int32),
        tile_map,
        owners,
        nbr_row,
        hbm=(0, 1, 2),
        vmem=60,
        scratch=(
            pltpu.SMEM(tile_map.shape, jnp.int32),
            pltpu.VMEM(owners.shape, jnp.int32),
            pltpu.VMEM(nbr_row.shape, jnp.int32),
            pltpu.SemaphoreType.DMA((3,)),
        ),
    )
    received = swap(ids)
    coef, coef_inside = call(
        functools.partial(coef_kernel, peers, node_rows),
        [shape((node_rows, peers * CAP), BF16)] * 2,
        tile_map,
        owners,
        nbr_row,
        edge_coef[0],
        hbm=(0, 1, 2, 3),
        vmem=60,
        scratch=(
            pltpu.SMEM(tile_map.shape, jnp.int32),
            pltpu.VMEM(owners.shape, jnp.int32),
            pltpu.VMEM(nbr_row.shape, jnp.int32),
            pltpu.VMEM(edge_coef.shape[1:], BF16),
            pltpu.SemaphoreType.DMA((4,)),
        ),
    )
    table = node_rows + table_rows
    received, coef, coef_inside = lax.optimization_barrier((received, coef, coef_inside))
    taken, pick = call(
        gather_kernel,
        [shape((peers, CAP, width), BF16), shape((peers * CAP, table), BF16)],
        received,
        jnp.concatenate([feats[0], history[:, :width]], axis=0),
    )
    pulled = swap(taken)
    pair = call(
        forward_kernel,
        shape((node_rows, 2 * width), BF16),
        pulled,
        coef,
        feats[0],
        weight,
        grad_out[0],
    )
    chips = [[i, i + 1] for i in range(0, peers, 2)]
    pairs = lax.all_gather(pair, "hist", axis=0, axis_index_groups=chips)
    terms = call(
        functools.partial(term_kernel, peers, width),
        shape((peers, 8, share * width // 16), BF16),
        pairs,
        hbm_out=(0,),
        scratch=(
            pltpu.VMEM((peers, 8, share * width // 16), BF16),
            pltpu.SemaphoreType.DMA((4,)),
        ),
    )
    pair, terms = lax.optimization_barrier((pair, terms))
    terms = swap(terms)
    sent, grad_mixed, out_rows = call(
        backward_kernel,
        [
            shape((peers, CAP, 2 * width), BF16),
            shape((node_rows, width), BF16),
            shape((node_rows, width), BF16),
        ],
        pair,
        weight,
        coef_inside,
        pick,
        history,
        hbm=(3, 4),
        scratch=(
            pltpu.VMEM((peers * CAP, table), BF16),
            pltpu.VMEM((table_rows, width), BF16),
            pltpu.SemaphoreType.DMA((2,)),
        ),
    )
    sent, terms = lax.optimization_barrier((sent, terms))
    back = swap(sent)
    side = 4
    term = call(weight_kernel, shape((16, share * width // 16), BF16), terms)
    for bit in (1, 2):
        twins = [[i, i + bit] for i in range(planes) if not i & bit]
        term = lax.all_gather(term, "batch", axis=0, axis_index_groups=twins)
        term = call(add_kernel, shape(term.shape[1:], BF16), term)
    far = [[a + side * i for i in range(planes // side)] for a in range(side)]
    term = lax.all_gather(term, "batch", axis=0, axis_index_groups=far)
    grad_rows, weight_share = call(
        final_kernel,
        [shape((node_rows, width), BF16), shape((share, width), F32)],
        back,
        pick,
        coef,
        grad_mixed,
        term,
    )
    return (out_rows[None], grad_rows[None], weight_share)


def solution(mesh):
    return jax.shard_map(
        body,
        mesh=mesh,
        in_specs=(
            P(("batch", "hist"), None, None),
            P("hist", None),
            P(),
            P(("batch", "hist"), None, None),
            P(("batch", "hist"), None),
            P(("batch", "hist"), None, None),
            P(("batch", "hist"), None),
            P(("batch", "hist"), None, None),
        ),
        out_specs=(
            P(("batch", "hist"), None, None),
            P(("batch", "hist"), None, None),
            P("hist", None),
        ),
        check_vma=False,
    )
```

```python
import functools

import jax
import jax.numpy as jnp
from jax import lax
from jax.experimental import pallas as pl
from jax.experimental.pallas import tpu as pltpu
from jax.sharding import PartitionSpec as P

F32 = jnp.float32
BF16 = jnp.bfloat16
LANES = 128
CAP = 16
ROWS_T = (((1,), (1,)), ((), ()))
COLS_T = (((0,), (0,)), ((), ()))


def dot(a, b, dims=(((1,), (0,)), ((), ()))):
    return lax.dot_general(a, b, dims, preferred_element_type=F32)


def sigmoid(values):
    return 1.0 / (1.0 + jnp.exp(-values))


def in_edge_order(first_tile, values):
    half = values.shape[1] // 2
    swapped = jnp.concatenate([values[:, half:], values[:, :half]], axis=1)
    return jnp.where(first_tile == 0, values, swapped)


def earlier_slots(slots):
    earlier = (
        lax.broadcasted_iota(jnp.int32, (slots, slots), 0)
        < lax.broadcasted_iota(jnp.int32, (slots, slots), 1)
    )
    return jnp.where(earlier, 1.0, 0.0).astype(BF16)


def slot_places(owners, peers, earlier):
    slots = owners.shape[1]
    named = lax.broadcasted_iota(jnp.int32, (peers, slots), 0) == owners
    named = jnp.where(named, 1.0, 0.0)
    rank = dot(named.astype(BF16), earlier)
    return named, jnp.sum(named * rank, axis=0, keepdims=True).astype(jnp.int32)


def request_kernel(tile_in, owner_in, row_in, ids_ref, tile_ref, owner_ref, row_ref, sems):
    copies = [
        pltpu.make_async_copy(tile_in, tile_ref, sems.at[0]),
        pltpu.make_async_copy(owner_in, owner_ref, sems.at[1]),
        pltpu.make_async_copy(row_in, row_ref, sems.at[2]),
    ]
    for copy in copies:
        copy.start()
    earlier = earlier_slots(owner_ref.shape[1])
    for copy in copies:
        copy.wait()
    peers = ids_ref.shape[0]
    first = tile_ref[:, :1]
    owners = in_edge_order(first, owner_ref[...])
    rows = in_edge_order(first, row_ref[...])
    named, place = slot_places(owners, peers, earlier)
    spot = lax.broadcasted_iota(jnp.int32, (LANES, rows.shape[1]), 0) == place
    spot = jnp.where(spot, 1.0, 0.0).astype(BF16)
    low = named * (rows % LANES).astype(F32)
    high = named * (rows // LANES).astype(F32)
    ids = dot(jnp.concatenate([low, high], axis=0).astype(BF16), spot, ROWS_T)
    ids = ids[:peers] + LANES * ids[peers:]
    ids_ref[...] = ids.astype(jnp.int32).reshape(ids_ref.shape)


def gather_kernel(ids_ref, table_ref, taken_ref, pick):
    table_rows, width = table_ref.shape
    peers = ids_ref.shape[0]
    ids = ids_ref[...].reshape(peers, LANES).astype(F32)
    ids = jnp.concatenate([ids, jnp.zeros((LANES - peers, LANES), F32)], axis=0)
    by_place = ids.T.astype(jnp.int32)
    columns = lax.broadcasted_iota(jnp.int32, (CAP, table_rows), 1)
    for g in range(peers):
        chosen = columns == by_place[:CAP, g : g + 1]
        pick[g * CAP : (g + 1) * CAP, :] = jnp.where(chosen, 1.0, 0.0).astype(BF16)
    part = peers // 4
    for start in range(0, peers, part):
        emb = dot(pick[start * CAP : (start + part) * CAP, :], table_ref[...])
        taken_ref[start : start + part] = emb.astype(BF16).reshape(part, CAP, width)


def coef_kernel(
    peers, node_rows, tile_in, owner_in, row_in, edge_in, all_ref, inside_ref, tile_ref, owner_ref,
    row_ref, edge_ref, sems
):
    copies = [
        pltpu.make_async_copy(tile_in, tile_ref, sems.at[0]),
        pltpu.make_async_copy(owner_in, owner_ref, sems.at[1]),
        pltpu.make_async_copy(row_in, row_ref, sems.at[2]),
        pltpu.make_async_copy(edge_in, edge_ref, sems.at[3]),
    ]
    for copy in copies:
        copy.start()
    earlier = earlier_slots(owner_ref.shape[1])
    for copy in copies:
        copy.wait()
    first = tile_ref[:, :1]
    owners = in_edge_order(first, owner_ref[...])
    rows = in_edge_order(first, row_ref[...])
    _, place = slot_places(owners, peers, earlier)
    target = owners * CAP + place
    at = lax.broadcasted_iota(jnp.int32, (peers * CAP, target.shape[1]), 0) == target
    moved = jnp.where(at, 1.0, 0.0)
    all_ref[...] = dot(edge_ref[...], moved.astype(BF16), ROWS_T).astype(BF16)
    kept = jnp.where(rows < node_rows, moved, 0.0).astype(BF16)
    inside_ref[...] = dot(edge_ref[...], kept, ROWS_T).astype(BF16)


def forward_kernel(
    pulled_ref,
    all_ref,
    feats_ref,
    weight_ref,
    grad_ref,
    pair_ref,
):
    width = feats_ref.shape[1]
    pulled = pulled_ref[...].reshape(-1, width)
    mixed = (feats_ref[...].astype(F32) + dot(all_ref[...], pulled)).astype(BF16)
    pre = dot(mixed, weight_ref[...])
    gate = sigmoid(pre)
    grad_pre = (grad_ref[...].astype(F32) * gate * (1.0 + pre * (1.0 - gate))).astype(BF16)
    pair_ref[:, :width] = mixed
    pair_ref[:, width:] = grad_pre


def term_kernel(peers, width, pairs_ref, term_ref):
    half = width // 2
    second_core = lax.axis_index("hist") % 2 == 1
    pairs = pairs_ref[...].reshape(-1, 2 * width)
    mixed = pairs[:, :width]
    left, right = pairs[:, width : width + half], pairs[:, width + half :]
    grad_pre = jnp.where(second_core, right, left)
    share = width // peers
    step = 8
    term = dot(mixed, grad_pre, COLS_T)
    for peer in range(peers):
        blocks = [
            term[peer * share + i : peer * share + i + step, :] for i in range(0, share, step)
        ]
        term_ref[peer] = jnp.concatenate(blocks, axis=1).astype(BF16)


def backward_kernel(
    pair_ref,
    weight_ref,
    inside_ref,
    pick_in,
    history_in,
    send_ref,
    mixed_ref,
    out_ref,
    pick,
    aux,
    sems,
):
    node_rows, width = mixed_ref.shape
    peers = send_ref.shape[0]
    load_pick = pltpu.make_async_copy(pick_in, pick, sems.at[0])
    load_aux = pltpu.make_async_copy(history_in.at[:, width:], aux, sems.at[1])
    load_pick.start()
    load_aux.start()
    grad_mixed = dot(pair_ref[:, width:], weight_ref[...], ROWS_T).astype(BF16)
    mixed_ref[...] = grad_mixed
    slot_grad = dot(inside_ref[...], grad_mixed, COLS_T).astype(BF16)
    send_ref[:, :, :width] = slot_grad.reshape(peers, CAP, width)
    pre = dot(pair_ref[:, :width], weight_ref[...])
    out_ref[...] = (pre * sigmoid(pre)).astype(BF16)
    load_pick.wait()
    load_aux.wait()
    taken = dot(pick[:, node_rows:], aux[...]).astype(BF16)
    send_ref[:, :, width:] = taken.reshape(peers, CAP, width)


def weight_kernel(terms_ref, sum_ref):
    peers, step = terms_ref.shape[:2]
    for core in range(2):
        total = terms_ref[core].astype(F32)
        for peer in range(core + 2, peers, 2):
            total = total + terms_ref[peer].astype(F32)
        total = total.astype(BF16)
        for plane in range(sum_ref.shape[0]):
            sum_ref[plane, core * step : (core + 1) * step, :] = total


def add_kernel(near_ref, sum_ref):
    sum_ref[...] = jnp.sum(near_ref[...].astype(F32), axis=0).astype(BF16)


def final_kernel(
    back_ref, pick_ref, all_ref, mixed_ref, far_ref, grad_ref, share_ref
):
    total = jnp.sum(far_ref[...].astype(F32), axis=0)
    share, width = share_ref.shape
    half = width // 2
    step = total.shape[0] // 2
    for i in range(share // step):
        for core in range(2):
            share_ref[i * step : (i + 1) * step, core * half : (core + 1) * half] = total[
                core * step : (core + 1) * step, i * half : (i + 1) * half
            ]
    peers = back_ref.shape[0]
    node_rows = mixed_ref.shape[0]
    slots = back_ref[:, :, :width].reshape(peers * CAP, width)
    aux = back_ref[:, :, width:].reshape(peers * CAP, width)
    returned = dot(pick_ref[:, :node_rows], slots, COLS_T)
    compensation = dot(all_ref[...], aux)
    grad = mixed_ref[...].astype(F32) + returned + compensation
    grad_ref[...] = grad.astype(BF16)


def call(kernel, out_shape, *args, smem=(), hbm=(), hbm_out=(), scratch=(), vmem=32, cost=None):
    spaces = [
        pltpu.SMEM if i in smem else pltpu.HBM if i in hbm else pltpu.VMEM
        for i in range(len(args))
    ]
    single = not isinstance(out_shape, (list, tuple))
    out_shape = [out_shape] if single else out_shape
    out_spaces = [pltpu.HBM if i in hbm_out else pltpu.VMEM for i in range(len(out_shape))]
    result = pl.pallas_call(
        kernel,
        out_shape=out_shape,
        in_specs=[pl.BlockSpec(memory_space=space) for space in spaces],
        out_specs=[pl.BlockSpec(memory_space=space) for space in out_spaces],
        scratch_shapes=list(scratch),
        compiler_params=pltpu.CompilerParams(vmem_limit_bytes=vmem << 20),
        cost_estimate=cost,
    )(*args)
    return result[0] if single else result


def swap(values, axis="hist", groups=None):
    return lax.all_to_all(
        values, axis, split_axis=0, concat_axis=0, tiled=True, axis_index_groups=groups
    )


def body(feats, history, weight, edge_coef, tile_map, nbr_owner, nbr_row, grad_out):
    peers = lax.axis_size("hist")
    planes = lax.axis_size("batch")
    node_rows, width = feats.shape[1:]
    table_rows = history.shape[0]
    slots = nbr_row.shape[1]
    assert 2 * slots // peers == CAP and planes == 16
    share = width // peers
    shape = jax.ShapeDtypeStruct
    owners = nbr_owner.reshape(1, slots)
    ids = call(
        request_kernel,
        shape((peers, 1, LANES), jnp.int32),
        tile_map,
        owners,
        nbr_row,
        hbm=(0, 1, 2),
        vmem=60,
        scratch=(
            pltpu.VMEM(tile_map.shape, jnp.int32),
            pltpu.VMEM(owners.shape, jnp.int32),
            pltpu.VMEM(nbr_row.shape, jnp.int32),
            pltpu.SemaphoreType.DMA((3,)),
        ),
    )
    received = swap(ids)
    coef, coef_inside = call(
        functools.partial(coef_kernel, peers, node_rows),
        [shape((node_rows, peers * CAP), BF16)] * 2,
        tile_map,
        owners,
        nbr_row,
        edge_coef[0],
        hbm=(0, 1, 2, 3),
        vmem=60,
        scratch=(
            pltpu.VMEM(tile_map.shape, jnp.int32),
            pltpu.VMEM(owners.shape, jnp.int32),
            pltpu.VMEM(nbr_row.shape, jnp.int32),
            pltpu.VMEM(edge_coef.shape[1:], BF16),
            pltpu.SemaphoreType.DMA((4,)),
        ),
    )
    table = node_rows + table_rows
    received, coef, coef_inside = lax.optimization_barrier((received, coef, coef_inside))
    taken, pick = call(
        gather_kernel,
        [shape((peers, CAP, width), BF16), shape((peers * CAP, table), BF16)],
        received,
        jnp.concatenate([feats[0], history[:, :width]], axis=0),
    )
    pulled = swap(taken)
    pair = call(
        forward_kernel,
        shape((node_rows, 2 * width), BF16),
        pulled,
        coef,
        feats[0],
        weight,
        grad_out[0],
    )
    chips = [[i, i + 1] for i in range(0, peers, 2)]
    pairs = lax.all_gather(pair, "hist", axis=0, axis_index_groups=chips)
    terms = call(
        functools.partial(term_kernel, peers, width),
        shape((peers, 8, share * width // 16), BF16),
        pairs,
    )
    pair, terms = lax.optimization_barrier((pair, terms))
    terms = swap(terms)
    sent, grad_mixed, out_rows = call(
        backward_kernel,
        [
            shape((peers, CAP, 2 * width), BF16),
            shape((node_rows, width), BF16),
            shape((node_rows, width), BF16),
        ],
        pair,
        weight,
        coef_inside,
        pick,
        history,
        hbm=(3, 4),
        scratch=(
            pltpu.VMEM((peers * CAP, table), BF16),
            pltpu.VMEM((table_rows, width), BF16),
            pltpu.SemaphoreType.DMA((2,)),
        ),
    )
    side = 4
    near = [[a * side + i for i in range(side)] for a in range(planes // side)]
    term = call(weight_kernel, shape((side, 16, share * width // 16), BF16), terms)
    term = swap(term, "batch", near)
    sent, term = lax.optimization_barrier((sent, term))
    back = swap(sent)
    term = call(add_kernel, shape(term.shape[1:], BF16), term)
    far = [[a + side * i for i in range(planes // side)] for a in range(side)]
    term = lax.all_gather(term, "batch", axis=0, axis_index_groups=far)
    grad_rows, weight_share = call(
        final_kernel,
        [shape((node_rows, width), BF16), shape((share, width), F32)],
        back,
        pick,
        coef,
        grad_mixed,
        term,
    )
    return (out_rows[None], grad_rows[None], weight_share)


def solution(mesh):
    return jax.shard_map(
        body,
        mesh=mesh,
        in_specs=(
            P(("batch", "hist"), None, None),
            P("hist", None),
            P(),
            P(("batch", "hist"), None, None),
            P(("batch", "hist"), None),
            P(("batch", "hist"), None, None),
            P(("batch", "hist"), None),
            P(("batch", "hist"), None, None),
        ),
        out_specs=(
            P(("batch", "hist"), None, None),
            P(("batch", "hist"), None, None),
            P("hist", None),
        ),
        check_vma=False,
    )
```

```python
import functools

import jax
import jax.numpy as jnp
from jax import lax
from jax.experimental import pallas as pl
from jax.experimental.pallas import tpu as pltpu
from jax.sharding import PartitionSpec as P

F32 = jnp.float32
BF16 = jnp.bfloat16
LANES = 128
CAP = 16
ROWS_T = (((1,), (1,)), ((), ()))
COLS_T = (((0,), (0,)), ((), ()))


def dot(a, b, dims=(((1,), (0,)), ((), ()))):
    return lax.dot_general(a, b, dims, preferred_element_type=F32)


def sigmoid(values):
    return 1.0 / (1.0 + jnp.exp(-values))


def lead_of(peers):
    return 5 * peers // 8


def to_blocks(owners, peers):
    return (owners + peers - lead_of(peers)) % peers


def in_edge_order(first_tile, values):
    half = values.shape[1] // 2
    swapped = jnp.concatenate([values[:, half:], values[:, :half]], axis=1)
    return jnp.where(first_tile == 0, values, swapped)


def earlier_slots(slots):
    earlier = (
        lax.broadcasted_iota(jnp.int32, (slots, slots), 0)
        < lax.broadcasted_iota(jnp.int32, (slots, slots), 1)
    )
    return jnp.where(earlier, 1.0, 0.0).astype(BF16)


def slot_places(owners, peers, earlier):
    slots = owners.shape[1]
    named = lax.broadcasted_iota(jnp.int32, (peers, slots), 0) == owners
    named = jnp.where(named, 1.0, 0.0)
    rank = dot(named.astype(BF16), earlier)
    return named, jnp.sum(named * rank, axis=0, keepdims=True).astype(jnp.int32)


def request_kernel(tile_in, owner_in, row_in, ids_ref, tile_ref, owner_ref, row_ref, sems):
    copies = [
        pltpu.make_async_copy(tile_in, tile_ref, sems.at[0]),
        pltpu.make_async_copy(owner_in, owner_ref, sems.at[1]),
        pltpu.make_async_copy(row_in, row_ref, sems.at[2]),
    ]
    for copy in copies:
        copy.start()
    earlier = earlier_slots(owner_ref.shape[1])
    for copy in copies:
        copy.wait()
    peers = ids_ref.shape[0]
    first = tile_ref[:, :1]
    owners = in_edge_order(first, to_blocks(owner_ref[...], peers))
    rows = in_edge_order(first, row_ref[...])
    named, place = slot_places(owners, peers, earlier)
    spot = lax.broadcasted_iota(jnp.int32, (LANES, rows.shape[1]), 0) == place
    spot = jnp.where(spot, 1.0, 0.0).astype(BF16)
    low = named * (rows % LANES).astype(F32)
    high = named * (rows // LANES).astype(F32)
    ids = dot(jnp.concatenate([low, high], axis=0).astype(BF16), spot, ROWS_T)
    ids = ids[:peers] + LANES * ids[peers:]
    ids_ref[...] = ids.astype(jnp.int32).reshape(ids_ref.shape)


def gather_kernel(ids_ref, table_ref, taken_ref, pick):
    table_rows, width = table_ref.shape
    peers = ids_ref.shape[0]
    ids = ids_ref[...].reshape(peers, LANES).astype(F32)
    ids = jnp.concatenate([ids, jnp.zeros((LANES - peers, LANES), F32)], axis=0)
    by_place = ids.T.astype(jnp.int32)
    columns = lax.broadcasted_iota(jnp.int32, (CAP, table_rows), 1)
    for g in range(peers):
        chosen = columns == by_place[:CAP, g : g + 1]
        pick[g * CAP : (g + 1) * CAP, :] = jnp.where(chosen, 1.0, 0.0).astype(BF16)
    part = peers // 4
    for start in range(0, peers, part):
        emb = dot(pick[start * CAP : (start + part) * CAP, :], table_ref[...])
        taken_ref[start : start + part] = emb.astype(BF16).reshape(part, CAP, width)


def coef_kernel(
    peers, node_rows, tile_in, owner_in, row_in, edge_in, all_ref, inside_ref, tile_ref, owner_ref,
    row_ref, edge_ref, sems
):
    copies = [
        pltpu.make_async_copy(tile_in, tile_ref, sems.at[0]),
        pltpu.make_async_copy(owner_in, owner_ref, sems.at[1]),
        pltpu.make_async_copy(row_in, row_ref, sems.at[2]),
        pltpu.make_async_copy(edge_in, edge_ref, sems.at[3]),
    ]
    for copy in copies:
        copy.start()
    earlier = earlier_slots(owner_ref.shape[1])
    for copy in copies:
        copy.wait()
    first = tile_ref[:, :1]
    owners = in_edge_order(first, to_blocks(owner_ref[...], peers))
    rows = in_edge_order(first, row_ref[...])
    _, place = slot_places(owners, peers, earlier)
    target = owners * CAP + place
    at = lax.broadcasted_iota(jnp.int32, (peers * CAP, target.shape[1]), 0) == target
    moved = jnp.where(at, 1.0, 0.0)
    all_ref[...] = dot(edge_ref[...], moved.astype(BF16), ROWS_T).astype(BF16)
    kept = jnp.where(rows < node_rows, moved, 0.0).astype(BF16)
    inside_ref[...] = dot(edge_ref[...], kept, ROWS_T).astype(BF16)


def forward_kernel(
    pulled_ref,
    all_ref,
    feats_ref,
    weight_ref,
    grad_ref,
    pair_ref,
):
    width = feats_ref.shape[1]
    pulled = pulled_ref[...].reshape(-1, width)
    mixed = (feats_ref[...].astype(F32) + dot(all_ref[...], pulled)).astype(BF16)
    pre = dot(mixed, weight_ref[...])
    gate = sigmoid(pre)
    grad_pre = (grad_ref[...].astype(F32) * gate * (1.0 + pre * (1.0 - gate))).astype(BF16)
    pair_ref[:, :width] = mixed
    pair_ref[:, width:] = grad_pre


def term_kernel(peers, width, pairs_ref, term_ref):
    half = width // 2
    second_core = lax.axis_index("hist") % 2 == 1
    pairs = pairs_ref[...].reshape(-1, 2 * width)
    mixed = pairs[:, :width]
    left, right = pairs[:, width : width + half], pairs[:, width + half :]
    grad_pre = jnp.where(second_core, right, left)
    share = width // peers
    step = 8
    term = dot(mixed, grad_pre, COLS_T)
    for peer in range(peers):
        row = (peer + lead_of(peers)) % peers * share
        blocks = [term[row + i : row + i + step, :] for i in range(0, share, step)]
        term_ref[peer] = jnp.concatenate(blocks, axis=1).astype(BF16)


def backward_kernel(
    pair_ref,
    weight_ref,
    inside_ref,
    pick_in,
    history_in,
    send_ref,
    mixed_ref,
    out_ref,
    pick,
    aux,
    sems,
):
    node_rows, width = mixed_ref.shape
    peers = send_ref.shape[0]
    load_pick = pltpu.make_async_copy(pick_in, pick, sems.at[0])
    load_aux = pltpu.make_async_copy(history_in.at[:, width:], aux, sems.at[1])
    load_pick.start()
    load_aux.start()
    grad_mixed = dot(pair_ref[:, width:], weight_ref[...], ROWS_T).astype(BF16)
    mixed_ref[...] = grad_mixed
    slot_grad = dot(inside_ref[...], grad_mixed, COLS_T).astype(BF16)
    send_ref[:, :, :width] = slot_grad.reshape(peers, CAP, width)
    pre = dot(pair_ref[:, :width], weight_ref[...])
    out_ref[...] = (pre * sigmoid(pre)).astype(BF16)
    load_pick.wait()
    load_aux.wait()
    taken = dot(pick[:, node_rows:], aux[...]).astype(BF16)
    send_ref[:, :, width:] = taken.reshape(peers, CAP, width)


def weight_kernel(terms_ref, sum_ref):
    peers, step = terms_ref.shape[:2]
    for core in range(2):
        total = terms_ref[core].astype(F32)
        for peer in range(core + 2, peers, 2):
            total = total + terms_ref[peer].astype(F32)
        total = total.astype(BF16)
        for plane in range(sum_ref.shape[0]):
            sum_ref[plane, core * step : (core + 1) * step, :] = total


def add_kernel(near_ref, sum_ref):
    sum_ref[...] = jnp.sum(near_ref[...].astype(F32), axis=0).astype(BF16)


def final_kernel(
    back_ref, pick_ref, all_ref, mixed_ref, far_ref, grad_ref, share_ref
):
    total = jnp.sum(far_ref[...].astype(F32), axis=0)
    share, width = share_ref.shape
    half = width // 2
    step = total.shape[0] // 2
    for i in range(share // step):
        for core in range(2):
            share_ref[i * step : (i + 1) * step, core * half : (core + 1) * half] = total[
                core * step : (core + 1) * step, i * half : (i + 1) * half
            ]
    peers = back_ref.shape[0]
    node_rows = mixed_ref.shape[0]
    slots = back_ref[:, :, :width].reshape(peers * CAP, width)
    aux = back_ref[:, :, width:].reshape(peers * CAP, width)
    returned = dot(pick_ref[:, :node_rows], slots, COLS_T)
    compensation = dot(all_ref[...], aux)
    grad = mixed_ref[...].astype(F32) + returned + compensation
    grad_ref[...] = grad.astype(BF16)


def call(kernel, out_shape, *args, smem=(), hbm=(), hbm_out=(), scratch=(), vmem=32, cost=None):
    spaces = [
        pltpu.SMEM if i in smem else pltpu.HBM if i in hbm else pltpu.VMEM
        for i in range(len(args))
    ]
    single = not isinstance(out_shape, (list, tuple))
    out_shape = [out_shape] if single else out_shape
    out_spaces = [pltpu.HBM if i in hbm_out else pltpu.VMEM for i in range(len(out_shape))]
    result = pl.pallas_call(
        kernel,
        out_shape=out_shape,
        in_specs=[pl.BlockSpec(memory_space=space) for space in spaces],
        out_specs=[pl.BlockSpec(memory_space=space) for space in out_spaces],
        scratch_shapes=list(scratch),
        compiler_params=pltpu.CompilerParams(vmem_limit_bytes=vmem << 20),
        cost_estimate=cost,
    )(*args)
    return result[0] if single else result


def swap(values, axis="hist", groups=None):
    if groups is None:
        peers = lax.axis_size(axis)
        groups = [[(i + lead_of(peers)) % peers for i in range(peers)]]
    return lax.all_to_all(
        values, axis, split_axis=0, concat_axis=0, tiled=True, axis_index_groups=groups
    )


def body(feats, history, weight, edge_coef, tile_map, nbr_owner, nbr_row, grad_out):
    peers = lax.axis_size("hist")
    planes = lax.axis_size("batch")
    node_rows, width = feats.shape[1:]
    table_rows = history.shape[0]
    slots = nbr_row.shape[1]
    assert 2 * slots // peers == CAP and planes == 16
    share = width // peers
    shape = jax.ShapeDtypeStruct
    owners = nbr_owner.reshape(1, slots)
    ids = call(
        request_kernel,
        shape((peers, 1, LANES), jnp.int32),
        tile_map,
        owners,
        nbr_row,
        hbm=(0, 1, 2),
        vmem=60,
        scratch=(
            pltpu.VMEM(tile_map.shape, jnp.int32),
            pltpu.VMEM(owners.shape, jnp.int32),
            pltpu.VMEM(nbr_row.shape, jnp.int32),
            pltpu.SemaphoreType.DMA((3,)),
        ),
    )
    received = swap(ids)
    coef, coef_inside = call(
        functools.partial(coef_kernel, peers, node_rows),
        [shape((node_rows, peers * CAP), BF16)] * 2,
        tile_map,
        owners,
        nbr_row,
        edge_coef[0],
        hbm=(0, 1, 2, 3),
        vmem=60,
        scratch=(
            pltpu.VMEM(tile_map.shape, jnp.int32),
            pltpu.VMEM(owners.shape, jnp.int32),
            pltpu.VMEM(nbr_row.shape, jnp.int32),
            pltpu.VMEM(edge_coef.shape[1:], BF16),
            pltpu.SemaphoreType.DMA((4,)),
        ),
    )
    table = node_rows + table_rows
    received, coef, coef_inside = lax.optimization_barrier((received, coef, coef_inside))
    taken, pick = call(
        gather_kernel,
        [shape((peers, CAP, width), BF16), shape((peers * CAP, table), BF16)],
        received,
        jnp.concatenate([feats[0], history[:, :width]], axis=0),
    )
    pulled = swap(taken)
    pair = call(
        forward_kernel,
        shape((node_rows, 2 * width), BF16),
        pulled,
        coef,
        feats[0],
        weight,
        grad_out[0],
    )
    chips = [[i, i + 1] for i in range(0, peers, 2)]
    pairs = lax.all_gather(pair, "hist", axis=0, axis_index_groups=chips)
    terms = call(
        functools.partial(term_kernel, peers, width),
        shape((peers, 8, share * width // 16), BF16),
        pairs,
    )
    pair, terms = lax.optimization_barrier((pair, terms))
    terms = swap(terms)
    sent, grad_mixed, out_rows = call(
        backward_kernel,
        [
            shape((peers, CAP, 2 * width), BF16),
            shape((node_rows, width), BF16),
            shape((node_rows, width), BF16),
        ],
        pair,
        weight,
        coef_inside,
        pick,
        history,
        hbm=(3, 4),
        scratch=(
            pltpu.VMEM((peers * CAP, table), BF16),
            pltpu.VMEM((table_rows, width), BF16),
            pltpu.SemaphoreType.DMA((2,)),
        ),
    )
    side = 4
    near = [[a * side + i for i in (2, 1, 3, 0)] for a in range(planes // side)]
    term = call(weight_kernel, shape((side, 16, share * width // 16), BF16), terms)
    term = swap(term, "batch", near)
    sent, term = lax.optimization_barrier((sent, term))
    back = swap(sent)
    term = call(add_kernel, shape(term.shape[1:], BF16), term)
    far = [[a + side * i for i in range(planes // side)] for a in range(side)]
    term = lax.all_gather(term, "batch", axis=0, axis_index_groups=far)
    grad_rows, weight_share = call(
        final_kernel,
        [shape((node_rows, width), BF16), shape((share, width), F32)],
        back,
        pick,
        coef,
        grad_mixed,
        term,
    )
    return (out_rows[None], grad_rows[None], weight_share)


def solution(mesh):
    return jax.shard_map(
        body,
        mesh=mesh,
        in_specs=(
            P(("batch", "hist"), None, None),
            P("hist", None),
            P(),
            P(("batch", "hist"), None, None),
            P(("batch", "hist"), None),
            P(("batch", "hist"), None, None),
            P(("batch", "hist"), None),
            P(("batch", "hist"), None, None),
        ),
        out_specs=(
            P(("batch", "hist"), None, None),
            P(("batch", "hist"), None, None),
            P("hist", None),
        ),
        check_vma=False,
    )
```

```python
import functools

import jax
import jax.numpy as jnp
from jax import lax
from jax.experimental import pallas as pl
from jax.experimental.pallas import tpu as pltpu
from jax.sharding import PartitionSpec as P

F32 = jnp.float32
BF16 = jnp.bfloat16
LANES = 128
CAP = 16
ROWS_T = (((1,), (1,)), ((), ()))
COLS_T = (((0,), (0,)), ((), ()))


def dot(a, b, dims=(((1,), (0,)), ((), ()))):
    return lax.dot_general(a, b, dims, preferred_element_type=F32)


def sigmoid(values):
    return 1.0 / (1.0 + jnp.exp(-values))


def lead_of(peers):
    return 5 * peers // 8


def to_blocks(owners, peers):
    return (owners + peers - lead_of(peers)) % peers


def in_edge_order(first_tile, values):
    half = values.shape[1] // 2
    swapped = jnp.concatenate([values[:, half:], values[:, :half]], axis=1)
    return jnp.where(first_tile == 0, values, swapped)


def earlier_slots(slots):
    earlier = (
        lax.broadcasted_iota(jnp.int32, (slots, slots), 0)
        < lax.broadcasted_iota(jnp.int32, (slots, slots), 1)
    )
    return jnp.where(earlier, 1.0, 0.0).astype(BF16)


def slot_places(owners, peers, earlier):
    slots = owners.shape[1]
    named = lax.broadcasted_iota(jnp.int32, (peers, slots), 0) == owners
    named = jnp.where(named, 1.0, 0.0)
    rank = dot(named.astype(BF16), earlier)
    return named, jnp.sum(named * rank, axis=0, keepdims=True).astype(jnp.int32)


def request_kernel(
    tile_in, owner_in, row_in, ids_ref, slots_ref, tile_ref, owner_ref, row_ref, sems
):
    copies = [
        pltpu.make_async_copy(tile_in, tile_ref, sems.at[0]),
        pltpu.make_async_copy(owner_in, owner_ref, sems.at[1]),
        pltpu.make_async_copy(row_in, row_ref, sems.at[2]),
    ]
    for copy in copies:
        copy.start()
    earlier = earlier_slots(owner_ref.shape[1])
    for copy in copies:
        copy.wait()
    peers = ids_ref.shape[0]
    first = tile_ref[:, :1]
    owners = in_edge_order(first, to_blocks(owner_ref[...], peers))
    rows = in_edge_order(first, row_ref[...])
    named, place = slot_places(owners, peers, earlier)
    spot = lax.broadcasted_iota(jnp.int32, (LANES, rows.shape[1]), 0) == place
    spot = jnp.where(spot, 1.0, 0.0).astype(BF16)
    low = named * (rows % LANES).astype(F32)
    high = named * (rows // LANES).astype(F32)
    ids = dot(jnp.concatenate([low, high], axis=0).astype(BF16), spot, ROWS_T)
    ids = ids[:peers] + LANES * ids[peers:]
    ids_ref[...] = ids.astype(jnp.int32).reshape(ids_ref.shape)
    slots_ref[:1, :] = owners * CAP + place
    slots_ref[1:, :] = rows


def gather_kernel(ids_ref, table_ref, taken_ref, pick):
    table_rows, width = table_ref.shape
    peers = ids_ref.shape[0]
    ids = ids_ref[...].reshape(peers, LANES).astype(F32)
    ids = jnp.concatenate([ids, jnp.zeros((LANES - peers, LANES), F32)], axis=0)
    by_place = ids.T.astype(jnp.int32)
    columns = lax.broadcasted_iota(jnp.int32, (CAP, table_rows), 1)
    for g in range(peers):
        chosen = columns == by_place[:CAP, g : g + 1]
        pick[g * CAP : (g + 1) * CAP, :] = jnp.where(chosen, 1.0, 0.0).astype(BF16)
    part = peers // 4
    for start in range(0, peers, part):
        emb = dot(pick[start * CAP : (start + part) * CAP, :], table_ref[...])
        taken_ref[start : start + part] = emb.astype(BF16).reshape(part, CAP, width)


def coef_kernel(node_rows, slots_in, edge_in, all_ref, inside_ref, slots_ref, edge_ref, sems):
    copies = [
        pltpu.make_async_copy(slots_in, slots_ref, sems.at[0]),
        pltpu.make_async_copy(edge_in, edge_ref, sems.at[1]),
    ]
    for copy in copies:
        copy.start()
    places, slots = all_ref.shape[1], slots_ref.shape[1]
    columns = lax.broadcasted_iota(jnp.int32, (places, slots), 0)
    for copy in copies:
        copy.wait()
    moved = jnp.where(columns == slots_ref[:1, :], 1.0, 0.0).astype(BF16)
    kept = jnp.where(slots_ref[1:, :] < node_rows, 1.0, 0.0)
    kept = jnp.broadcast_to(kept, (16, slots)).astype(BF16)
    edge = edge_ref[...]
    rows = edge.shape[0]
    both = dot(jnp.concatenate([edge, kept], axis=0), moved, ROWS_T)
    coef = both[:rows]
    all_ref[...] = coef.astype(BF16)
    inside_ref[...] = (coef * both[rows : rows + 1]).astype(BF16)


def forward_kernel(
    pulled_ref,
    all_ref,
    feats_ref,
    weight_ref,
    grad_ref,
    pair_ref,
):
    width = feats_ref.shape[1]
    pulled = pulled_ref[...].reshape(-1, width)
    mixed = (feats_ref[...].astype(F32) + dot(all_ref[...], pulled)).astype(BF16)
    pre = dot(mixed, weight_ref[...])
    gate = sigmoid(pre)
    grad_pre = (grad_ref[...].astype(F32) * gate * (1.0 + pre * (1.0 - gate))).astype(BF16)
    pair_ref[:, :width] = mixed
    pair_ref[:, width:] = grad_pre


def term_kernel(peers, width, pairs_ref, term_ref):
    half = width // 2
    second_core = lax.axis_index("hist") % 2 == 1
    pairs = pairs_ref[...].reshape(-1, 2 * width)
    mixed = pairs[:, :width]
    left, right = pairs[:, width : width + half], pairs[:, width + half :]
    grad_pre = jnp.where(second_core, right, left)
    share = width // peers
    step = 8
    term = dot(mixed, grad_pre, COLS_T)
    for peer in range(peers):
        row = (peer + lead_of(peers)) % peers * share
        blocks = [term[row + i : row + i + step, :] for i in range(0, share, step)]
        term_ref[peer] = jnp.concatenate(blocks, axis=1).astype(BF16)


def backward_kernel(
    pair_ref,
    weight_ref,
    inside_ref,
    pick_in,
    history_in,
    send_ref,
    mixed_ref,
    out_ref,
    pick,
    aux,
    sems,
):
    node_rows, width = mixed_ref.shape
    peers = send_ref.shape[0]
    load_pick = pltpu.make_async_copy(pick_in, pick, sems.at[0])
    load_aux = pltpu.make_async_copy(history_in.at[:, width:], aux, sems.at[1])
    load_pick.start()
    load_aux.start()
    grad_mixed = dot(pair_ref[:, width:], weight_ref[...], ROWS_T).astype(BF16)
    mixed_ref[...] = grad_mixed
    slot_grad = dot(inside_ref[...], grad_mixed, COLS_T).astype(BF16)
    send_ref[:, :, :width] = slot_grad.reshape(peers, CAP, width)
    pre = dot(pair_ref[:, :width], weight_ref[...])
    out_ref[...] = (pre * sigmoid(pre)).astype(BF16)
    load_pick.wait()
    load_aux.wait()
    taken = dot(pick[:, node_rows:], aux[...]).astype(BF16)
    send_ref[:, :, width:] = taken.reshape(peers, CAP, width)


def weight_kernel(terms_ref, sum_ref):
    peers, step = terms_ref.shape[:2]
    for core in range(2):
        total = terms_ref[core].astype(F32)
        for peer in range(core + 2, peers, 2):
            total = total + terms_ref[peer].astype(F32)
        total = total.astype(BF16)
        for plane in range(sum_ref.shape[0]):
            sum_ref[plane, core * step : (core + 1) * step, :] = total


def add_kernel(near_ref, sum_ref):
    sum_ref[...] = jnp.sum(near_ref[...].astype(F32), axis=0).astype(BF16)


def final_kernel(
    back_ref, pick_ref, all_ref, mixed_ref, far_ref, grad_ref, share_ref
):
    total = jnp.sum(far_ref[...].astype(F32), axis=0)
    share, width = share_ref.shape
    half = width // 2
    step = total.shape[0] // 2
    for i in range(share // step):
        for core in range(2):
            share_ref[i * step : (i + 1) * step, core * half : (core + 1) * half] = total[
                core * step : (core + 1) * step, i * half : (i + 1) * half
            ]
    peers = back_ref.shape[0]
    node_rows = mixed_ref.shape[0]
    slots = back_ref[:, :, :width].reshape(peers * CAP, width)
    aux = back_ref[:, :, width:].reshape(peers * CAP, width)
    returned = dot(pick_ref[:, :node_rows], slots, COLS_T)
    compensation = dot(all_ref[...], aux)
    grad = mixed_ref[...].astype(F32) + returned + compensation
    grad_ref[...] = grad.astype(BF16)


def call(kernel, out_shape, *args, smem=(), hbm=(), hbm_out=(), scratch=(), vmem=32, cost=None):
    spaces = [
        pltpu.SMEM if i in smem else pltpu.HBM if i in hbm else pltpu.VMEM
        for i in range(len(args))
    ]
    single = not isinstance(out_shape, (list, tuple))
    out_shape = [out_shape] if single else out_shape
    out_spaces = [pltpu.HBM if i in hbm_out else pltpu.VMEM for i in range(len(out_shape))]
    result = pl.pallas_call(
        kernel,
        out_shape=out_shape,
        in_specs=[pl.BlockSpec(memory_space=space) for space in spaces],
        out_specs=[pl.BlockSpec(memory_space=space) for space in out_spaces],
        scratch_shapes=list(scratch),
        compiler_params=pltpu.CompilerParams(vmem_limit_bytes=vmem << 20),
        cost_estimate=cost,
    )(*args)
    return result[0] if single else result


def swap(values, axis="hist", groups=None):
    if groups is None:
        peers = lax.axis_size(axis)
        groups = [[(i + lead_of(peers)) % peers for i in range(peers)]]
    return lax.all_to_all(
        values, axis, split_axis=0, concat_axis=0, tiled=True, axis_index_groups=groups
    )


def body(feats, history, weight, edge_coef, tile_map, nbr_owner, nbr_row, grad_out):
    peers = lax.axis_size("hist")
    planes = lax.axis_size("batch")
    node_rows, width = feats.shape[1:]
    table_rows = history.shape[0]
    slots = nbr_row.shape[1]
    assert 2 * slots // peers == CAP and planes == 16
    share = width // peers
    shape = jax.ShapeDtypeStruct
    owners = nbr_owner.reshape(1, slots)
    ids, placed = call(
        request_kernel,
        [shape((peers, 1, LANES), jnp.int32), shape((2, slots), jnp.int32)],
        tile_map,
        owners,
        nbr_row,
        hbm=(0, 1, 2),
        vmem=60,
        scratch=(
            pltpu.VMEM(tile_map.shape, jnp.int32),
            pltpu.VMEM(owners.shape, jnp.int32),
            pltpu.VMEM(nbr_row.shape, jnp.int32),
            pltpu.SemaphoreType.DMA((3,)),
        ),
    )
    received = swap(ids)
    coef, coef_inside = call(
        functools.partial(coef_kernel, node_rows),
        [shape((node_rows, peers * CAP), BF16)] * 2,
        placed,
        edge_coef[0],
        hbm=(0, 1),
        vmem=60,
        scratch=(
            pltpu.VMEM((2, slots), jnp.int32),
            pltpu.VMEM(edge_coef.shape[1:], BF16),
            pltpu.SemaphoreType.DMA((2,)),
        ),
    )
    table = node_rows + table_rows
    received, coef, coef_inside = lax.optimization_barrier((received, coef, coef_inside))
    taken, pick = call(
        gather_kernel,
        [shape((peers, CAP, width), BF16), shape((peers * CAP, table), BF16)],
        received,
        jnp.concatenate([feats[0], history[:, :width]], axis=0),
    )
    pulled = swap(taken)
    pair = call(
        forward_kernel,
        shape((node_rows, 2 * width), BF16),
        pulled,
        coef,
        feats[0],
        weight,
        grad_out[0],
    )
    chips = [[i, i + 1] for i in range(0, peers, 2)]
    pairs = lax.all_gather(pair, "hist", axis=0, axis_index_groups=chips)
    terms = call(
        functools.partial(term_kernel, peers, width),
        shape((peers, 8, share * width // 16), BF16),
        pairs,
    )
    pair, terms = lax.optimization_barrier((pair, terms))
    terms = swap(terms)
    sent, grad_mixed, out_rows = call(
        backward_kernel,
        [
            shape((peers, CAP, 2 * width), BF16),
            shape((node_rows, width), BF16),
            shape((node_rows, width), BF16),
        ],
        pair,
        weight,
        coef_inside,
        pick,
        history,
        hbm=(3, 4),
        scratch=(
            pltpu.VMEM((peers * CAP, table), BF16),
            pltpu.VMEM((table_rows, width), BF16),
            pltpu.SemaphoreType.DMA((2,)),
        ),
    )
    side = 4
    near = [[a * side + i for i in (2, 1, 3, 0)] for a in range(planes // side)]
    term = call(weight_kernel, shape((side, 16, share * width // 16), BF16), terms)
    term = swap(term, "batch", near)
    sent, term = lax.optimization_barrier((sent, term))
    back = swap(sent)
    term = call(add_kernel, shape(term.shape[1:], BF16), term)
    far = [[a + side * i for i in range(planes // side)] for a in range(side)]
    term = lax.all_gather(term, "batch", axis=0, axis_index_groups=far)
    grad_rows, weight_share = call(
        final_kernel,
        [shape((node_rows, width), BF16), shape((share, width), F32)],
        back,
        pick,
        coef,
        grad_mixed,
        term,
    )
    return (out_rows[None], grad_rows[None], weight_share)


def solution(mesh):
    return jax.shard_map(
        body,
        mesh=mesh,
        in_specs=(
            P(("batch", "hist"), None, None),
            P("hist", None),
            P(),
            P(("batch", "hist"), None, None),
            P(("batch", "hist"), None),
            P(("batch", "hist"), None, None),
            P(("batch", "hist"), None),
            P(("batch", "hist"), None, None),
        ),
        out_specs=(
            P(("batch", "hist"), None, None),
            P(("batch", "hist"), None, None),
            P("hist", None),
        ),
        check_vma=False,
    )
```

```python
import functools

import jax
import jax.numpy as jnp
from jax import lax
from jax.experimental import pallas as pl
from jax.experimental.pallas import tpu as pltpu
from jax.sharding import PartitionSpec as P

F32 = jnp.float32
BF16 = jnp.bfloat16
LANES = 128
CAP = 16
ROWS_T = (((1,), (1,)), ((), ()))
COLS_T = (((0,), (0,)), ((), ()))


def dot(a, b, dims=(((1,), (0,)), ((), ()))):
    return lax.dot_general(a, b, dims, preferred_element_type=F32)


def sigmoid(values):
    return 1.0 / (1.0 + jnp.exp(-values))


def lead_of(peers):
    return 5 * peers // 8 + 1


def to_blocks(owners, peers):
    return (owners + peers - lead_of(peers)) % peers


def in_edge_order(first_tile, values):
    half = values.shape[1] // 2
    swapped = jnp.concatenate([values[:, half:], values[:, :half]], axis=1)
    return jnp.where(first_tile == 0, values, swapped)


def earlier_slots(slots):
    earlier = (
        lax.broadcasted_iota(jnp.int32, (slots, slots), 0)
        < lax.broadcasted_iota(jnp.int32, (slots, slots), 1)
    )
    return jnp.where(earlier, 1.0, 0.0).astype(BF16)


def slot_places(owners, peers, earlier):
    slots = owners.shape[1]
    named = lax.broadcasted_iota(jnp.int32, (peers, slots), 0) == owners
    named = jnp.where(named, 1.0, 0.0)
    rank = dot(named.astype(BF16), earlier)
    return named, jnp.sum(named * rank, axis=0, keepdims=True).astype(jnp.int32)


def request_kernel(
    tile_in, owner_in, row_in, ids_ref, slots_ref, tile_ref, owner_ref, row_ref, sems
):
    copies = [
        pltpu.make_async_copy(tile_in, tile_ref, sems.at[0]),
        pltpu.make_async_copy(owner_in, owner_ref, sems.at[1]),
        pltpu.make_async_copy(row_in, row_ref, sems.at[2]),
    ]
    for copy in copies:
        copy.start()
    earlier = earlier_slots(owner_ref.shape[1])
    for copy in copies:
        copy.wait()
    peers = ids_ref.shape[0]
    first = tile_ref[:, :1]
    owners = in_edge_order(first, to_blocks(owner_ref[...], peers))
    rows = in_edge_order(first, row_ref[...])
    named, place = slot_places(owners, peers, earlier)
    spot = lax.broadcasted_iota(jnp.int32, (LANES, rows.shape[1]), 0) == place
    spot = jnp.where(spot, 1.0, 0.0).astype(BF16)
    low = named * (rows % LANES).astype(F32)
    high = named * (rows // LANES).astype(F32)
    ids = dot(jnp.concatenate([low, high], axis=0).astype(BF16), spot, ROWS_T)
    ids = ids[:peers] + LANES * ids[peers:]
    ids_ref[...] = ids.astype(jnp.int32).reshape(ids_ref.shape)
    slots_ref[:1, :] = owners * CAP + place
    slots_ref[1:, :] = rows


def gather_kernel(ids_ref, table_ref, taken_ref, pick):
    table_rows, width = table_ref.shape
    peers = ids_ref.shape[0]
    ids = ids_ref[...].reshape(peers, LANES).astype(F32)
    ids = jnp.concatenate([ids, jnp.zeros((LANES - peers, LANES), F32)], axis=0)
    by_place = ids.T.astype(jnp.int32)
    columns = lax.broadcasted_iota(jnp.int32, (CAP, table_rows), 1)
    for g in range(peers):
        chosen = columns == by_place[:CAP, g : g + 1]
        pick[g * CAP : (g + 1) * CAP, :] = jnp.where(chosen, 1.0, 0.0).astype(BF16)
    part = peers // 4
    for start in range(0, peers, part):
        emb = dot(pick[start * CAP : (start + part) * CAP, :], table_ref[...])
        taken_ref[start : start + part] = emb.astype(BF16).reshape(part, CAP, width)


def coef_kernel(node_rows, slots_in, edge_in, all_ref, inside_ref, slots_ref, edge_ref, sems):
    copies = [
        pltpu.make_async_copy(slots_in, slots_ref, sems.at[0]),
        pltpu.make_async_copy(edge_in, edge_ref, sems.at[1]),
    ]
    for copy in copies:
        copy.start()
    places, slots = all_ref.shape[1], slots_ref.shape[1]
    columns = lax.broadcasted_iota(jnp.int32, (places, slots), 0)
    for copy in copies:
        copy.wait()
    moved = jnp.where(columns == slots_ref[:1, :], 1.0, 0.0).astype(BF16)
    kept = jnp.where(slots_ref[1:, :] < node_rows, 1.0, 0.0)
    kept = jnp.broadcast_to(kept, (16, slots)).astype(BF16)
    edge = edge_ref[...]
    rows = edge.shape[0]
    both = dot(jnp.concatenate([edge, kept], axis=0), moved, ROWS_T)
    coef = both[:rows]
    all_ref[...] = coef.astype(BF16)
    inside_ref[...] = (coef * both[rows : rows + 1]).astype(BF16)


def forward_kernel(
    pulled_ref,
    all_ref,
    feats_ref,
    weight_ref,
    grad_ref,
    pair_ref,
):
    width = feats_ref.shape[1]
    pulled = pulled_ref[...].reshape(-1, width)
    mixed = (feats_ref[...].astype(F32) + dot(all_ref[...], pulled)).astype(BF16)
    pre = dot(mixed, weight_ref[...])
    gate = sigmoid(pre)
    grad_pre = (grad_ref[...].astype(F32) * gate * (1.0 + pre * (1.0 - gate))).astype(BF16)
    pair_ref[:, :width] = mixed
    pair_ref[:, width:] = grad_pre


def term_kernel(peers, width, pairs_ref, term_ref):
    half = width // 2
    second_core = lax.axis_index("hist") % 2 == 1
    pairs = pairs_ref[...].reshape(-1, 2 * width)
    mixed = pairs[:, :width]
    left, right = pairs[:, width : width + half], pairs[:, width + half :]
    grad_pre = jnp.where(second_core, right, left)
    share = width // peers
    step = 8
    term = dot(mixed, grad_pre, COLS_T)
    for peer in range(peers):
        row = (peer + lead_of(peers)) % peers * share
        blocks = [term[row + i : row + i + step, :] for i in range(0, share, step)]
        term_ref[peer] = jnp.concatenate(blocks, axis=1).astype(BF16)


def backward_kernel(
    pair_ref,
    weight_ref,
    inside_ref,
    pick_in,
    history_in,
    send_ref,
    mixed_ref,
    out_ref,
    pick,
    aux,
    sems,
):
    node_rows, width = mixed_ref.shape
    peers = send_ref.shape[0]
    load_pick = pltpu.make_async_copy(pick_in, pick, sems.at[0])
    load_aux = pltpu.make_async_copy(history_in.at[:, width:], aux, sems.at[1])
    load_pick.start()
    load_aux.start()
    grad_mixed = dot(pair_ref[:, width:], weight_ref[...], ROWS_T).astype(BF16)
    mixed_ref[...] = grad_mixed
    slot_grad = dot(inside_ref[...], grad_mixed, COLS_T).astype(BF16)
    send_ref[:, :, :width] = slot_grad.reshape(peers, CAP, width)
    pre = dot(pair_ref[:, :width], weight_ref[...])
    out_ref[...] = (pre * sigmoid(pre)).astype(BF16)
    load_pick.wait()
    load_aux.wait()
    taken = dot(pick[:, node_rows:], aux[...]).astype(BF16)
    send_ref[:, :, width:] = taken.reshape(peers, CAP, width)


def weight_kernel(terms_ref, sum_ref):
    peers, step = terms_ref.shape[:2]
    for core in range(2):
        first = (core + lead_of(peers)) % 2
        total = terms_ref[first].astype(F32)
        for peer in range(first + 2, peers, 2):
            total = total + terms_ref[peer].astype(F32)
        total = total.astype(BF16)
        for plane in range(sum_ref.shape[0]):
            sum_ref[plane, core * step : (core + 1) * step, :] = total


def add_kernel(near_ref, sum_ref):
    sum_ref[...] = jnp.sum(near_ref[...].astype(F32), axis=0).astype(BF16)


def final_kernel(
    back_ref, pick_ref, all_ref, mixed_ref, far_ref, grad_ref, share_ref
):
    total = jnp.sum(far_ref[...].astype(F32), axis=0)
    share, width = share_ref.shape
    half = width // 2
    step = total.shape[0] // 2
    for i in range(share // step):
        for core in range(2):
            share_ref[i * step : (i + 1) * step, core * half : (core + 1) * half] = total[
                core * step : (core + 1) * step, i * half : (i + 1) * half
            ]
    peers = back_ref.shape[0]
    node_rows = mixed_ref.shape[0]
    slots = back_ref[:, :, :width].reshape(peers * CAP, width)
    aux = back_ref[:, :, width:].reshape(peers * CAP, width)
    returned = dot(pick_ref[:, :node_rows], slots, COLS_T)
    compensation = dot(all_ref[...], aux)
    grad = mixed_ref[...].astype(F32) + returned + compensation
    grad_ref[...] = grad.astype(BF16)


def call(kernel, out_shape, *args, smem=(), hbm=(), hbm_out=(), scratch=(), vmem=32, cost=None):
    spaces = [
        pltpu.SMEM if i in smem else pltpu.HBM if i in hbm else pltpu.VMEM
        for i in range(len(args))
    ]
    single = not isinstance(out_shape, (list, tuple))
    out_shape = [out_shape] if single else out_shape
    out_spaces = [pltpu.HBM if i in hbm_out else pltpu.VMEM for i in range(len(out_shape))]
    result = pl.pallas_call(
        kernel,
        out_shape=out_shape,
        in_specs=[pl.BlockSpec(memory_space=space) for space in spaces],
        out_specs=[pl.BlockSpec(memory_space=space) for space in out_spaces],
        scratch_shapes=list(scratch),
        compiler_params=pltpu.CompilerParams(vmem_limit_bytes=vmem << 20),
        cost_estimate=cost,
    )(*args)
    return result[0] if single else result


def swap(values, axis="hist", groups=None):
    if groups is None:
        peers = lax.axis_size(axis)
        groups = [[(i + lead_of(peers)) % peers for i in range(peers)]]
    return lax.all_to_all(
        values, axis, split_axis=0, concat_axis=0, tiled=True, axis_index_groups=groups
    )


def body(feats, history, weight, edge_coef, tile_map, nbr_owner, nbr_row, grad_out):
    peers = lax.axis_size("hist")
    planes = lax.axis_size("batch")
    node_rows, width = feats.shape[1:]
    table_rows = history.shape[0]
    slots = nbr_row.shape[1]
    assert 2 * slots // peers == CAP and planes == 16
    share = width // peers
    shape = jax.ShapeDtypeStruct
    owners = nbr_owner.reshape(1, slots)
    ids, placed = call(
        request_kernel,
        [shape((peers, 1, LANES), jnp.int32), shape((2, slots), jnp.int32)],
        tile_map,
        owners,
        nbr_row,
        hbm=(0, 1, 2),
        vmem=60,
        scratch=(
            pltpu.VMEM(tile_map.shape, jnp.int32),
            pltpu.VMEM(owners.shape, jnp.int32),
            pltpu.VMEM(nbr_row.shape, jnp.int32),
            pltpu.SemaphoreType.DMA((3,)),
        ),
    )
    received = swap(ids)
    coef, coef_inside = call(
        functools.partial(coef_kernel, node_rows),
        [shape((node_rows, peers * CAP), BF16)] * 2,
        placed,
        edge_coef[0],
        hbm=(0, 1),
        vmem=60,
        scratch=(
            pltpu.VMEM((2, slots), jnp.int32),
            pltpu.VMEM(edge_coef.shape[1:], BF16),
            pltpu.SemaphoreType.DMA((2,)),
        ),
    )
    table = node_rows + table_rows
    received, coef, coef_inside = lax.optimization_barrier((received, coef, coef_inside))
    taken, pick = call(
        gather_kernel,
        [shape((peers, CAP, width), BF16), shape((peers * CAP, table), BF16)],
        received,
        jnp.concatenate([feats[0], history[:, :width]], axis=0),
    )
    pulled = swap(taken)
    pair = call(
        forward_kernel,
        shape((node_rows, 2 * width), BF16),
        pulled,
        coef,
        feats[0],
        weight,
        grad_out[0],
    )
    chips = [[i, i + 1] for i in range(0, peers, 2)]
    pairs = lax.all_gather(pair, "hist", axis=0, axis_index_groups=chips)
    terms = call(
        functools.partial(term_kernel, peers, width),
        shape((peers, 8, share * width // 16), BF16),
        pairs,
    )
    pair, terms = lax.optimization_barrier((pair, terms))
    terms = swap(terms)
    sent, grad_mixed, out_rows = call(
        backward_kernel,
        [
            shape((peers, CAP, 2 * width), BF16),
            shape((node_rows, width), BF16),
            shape((node_rows, width), BF16),
        ],
        pair,
        weight,
        coef_inside,
        pick,
        history,
        hbm=(3, 4),
        scratch=(
            pltpu.VMEM((peers * CAP, table), BF16),
            pltpu.VMEM((table_rows, width), BF16),
            pltpu.SemaphoreType.DMA((2,)),
        ),
    )
    side = 4
    near = [[a * side + i for i in (2, 1, 3, 0)] for a in range(planes // side)]
    term = call(weight_kernel, shape((side, 16, share * width // 16), BF16), terms)
    term = swap(term, "batch", near)
    sent, term = lax.optimization_barrier((sent, term))
    back = swap(sent)
    term = call(add_kernel, shape(term.shape[1:], BF16), term)
    far = [[a + side * i for i in range(planes // side)] for a in range(side)]
    term = lax.all_gather(term, "batch", axis=0, axis_index_groups=far)
    grad_rows, weight_share = call(
        final_kernel,
        [shape((node_rows, width), BF16), shape((share, width), F32)],
        back,
        pick,
        coef,
        grad_mixed,
        term,
    )
    return (out_rows[None], grad_rows[None], weight_share)


def solution(mesh):
    return jax.shard_map(
        body,
        mesh=mesh,
        in_specs=(
            P(("batch", "hist"), None, None),
            P("hist", None),
            P(),
            P(("batch", "hist"), None, None),
            P(("batch", "hist"), None),
            P(("batch", "hist"), None, None),
            P(("batch", "hist"), None),
            P(("batch", "hist"), None, None),
        ),
        out_specs=(
            P(("batch", "hist"), None, None),
            P(("batch", "hist"), None, None),
            P("hist", None),
        ),
        check_vma=False,
    )
```

```python
import functools

import jax
import jax.numpy as jnp
from jax import lax
from jax.experimental import pallas as pl
from jax.experimental.pallas import tpu as pltpu
from jax.sharding import PartitionSpec as P

F32 = jnp.float32
BF16 = jnp.bfloat16
LANES = 128
CAP = 16
ROWS_T = (((1,), (1,)), ((), ()))
COLS_T = (((0,), (0,)), ((), ()))


def dot(a, b, dims=(((1,), (0,)), ((), ()))):
    return lax.dot_general(a, b, dims, preferred_element_type=F32)


def sigmoid(values):
    return 1.0 / (1.0 + jnp.exp(-values))


def lead_of(peers):
    return 5 * peers // 8 + 1


def to_blocks(owners, peers):
    return (owners + peers - lead_of(peers)) % peers


def in_edge_order(first_tile, values):
    half = values.shape[1] // 2
    swapped = jnp.concatenate([values[:, half:], values[:, :half]], axis=1)
    return jnp.where(first_tile == 0, values, swapped)


def earlier_slots(slots):
    earlier = (
        lax.broadcasted_iota(jnp.int32, (slots, slots), 0)
        < lax.broadcasted_iota(jnp.int32, (slots, slots), 1)
    )
    return jnp.where(earlier, 1.0, 0.0).astype(BF16)


def slot_places(owners, peers, earlier):
    slots = owners.shape[1]
    named = lax.broadcasted_iota(jnp.int32, (peers, slots), 0) == owners
    named = jnp.where(named, 1.0, 0.0)
    rank = dot(named.astype(BF16), earlier)
    return named, jnp.sum(named * rank, axis=0, keepdims=True).astype(jnp.int32)


def request_kernel(
    tile_in, owner_in, row_in, ids_ref, slots_ref, tile_ref, owner_ref, row_ref, sems
):
    copies = [
        pltpu.make_async_copy(tile_in, tile_ref, sems.at[0]),
        pltpu.make_async_copy(owner_in, owner_ref, sems.at[1]),
        pltpu.make_async_copy(row_in, row_ref, sems.at[2]),
    ]
    for copy in copies:
        copy.start()
    earlier = earlier_slots(owner_ref.shape[1])
    for copy in copies:
        copy.wait()
    peers = ids_ref.shape[0]
    first = tile_ref[:, :1]
    owners = in_edge_order(first, to_blocks(owner_ref[...], peers))
    rows = in_edge_order(first, row_ref[...])
    named, place = slot_places(owners, peers, earlier)
    spot = lax.broadcasted_iota(jnp.int32, (LANES, rows.shape[1]), 0) == place
    spot = jnp.where(spot, 1.0, 0.0).astype(BF16)
    low = named * (rows % LANES).astype(F32)
    high = named * (rows // LANES).astype(F32)
    ids = dot(jnp.concatenate([low, high], axis=0).astype(BF16), spot, ROWS_T)
    ids = ids[:peers] + LANES * ids[peers:]
    ids_ref[...] = ids.astype(jnp.int32).reshape(ids_ref.shape)
    slots_ref[:1, :] = owners * CAP + place
    slots_ref[1:, :] = rows


def gather_kernel(ids_ref, table_ref, taken_ref, pick):
    table_rows, width = table_ref.shape
    peers = ids_ref.shape[0]
    ids = ids_ref[...].reshape(peers, LANES).astype(F32)
    ids = jnp.concatenate([ids, jnp.zeros((LANES - peers, LANES), F32)], axis=0)
    by_place = ids.T.astype(jnp.int32)
    columns = lax.broadcasted_iota(jnp.int32, (CAP, table_rows), 1)
    for g in range(peers):
        chosen = columns == by_place[:CAP, g : g + 1]
        pick[g * CAP : (g + 1) * CAP, :] = jnp.where(chosen, 1.0, 0.0).astype(BF16)
    part = peers // 4
    for start in range(0, peers, part):
        emb = dot(pick[start * CAP : (start + part) * CAP, :], table_ref[...])
        taken_ref[start : start + part] = emb.astype(BF16).reshape(part, CAP, width)


def coef_kernel(node_rows, slots_in, edge_in, all_ref, inside_ref, slots_ref, edge_ref, sems):
    copies = [
        pltpu.make_async_copy(slots_in, slots_ref, sems.at[0]),
        pltpu.make_async_copy(edge_in, edge_ref, sems.at[1]),
    ]
    for copy in copies:
        copy.start()
    places, slots = all_ref.shape[1], slots_ref.shape[1]
    columns = lax.broadcasted_iota(jnp.int32, (places, slots), 0)
    for copy in copies:
        copy.wait()
    moved = jnp.where(columns == slots_ref[:1, :], 1.0, 0.0).astype(BF16)
    kept = jnp.where(slots_ref[1:, :] < node_rows, 1.0, 0.0)
    kept = jnp.broadcast_to(kept, (16, slots)).astype(BF16)
    edge = edge_ref[...]
    rows = edge.shape[0]
    both = dot(jnp.concatenate([edge, kept], axis=0), moved, ROWS_T)
    coef = both[:rows]
    all_ref[...] = coef.astype(BF16)
    inside_ref[...] = (coef * both[rows : rows + 1]).astype(BF16)


def forward_kernel(
    pulled_ref,
    all_ref,
    feats_ref,
    weight_ref,
    grad_ref,
    pair_ref,
):
    width = feats_ref.shape[1]
    pulled = pulled_ref[...].reshape(-1, width)
    mixed = (feats_ref[...].astype(F32) + dot(all_ref[...], pulled)).astype(BF16)
    pre = dot(mixed, weight_ref[...])
    gate = sigmoid(pre)
    grad_pre = (grad_ref[...].astype(F32) * gate * (1.0 + pre * (1.0 - gate))).astype(BF16)
    pair_ref[:, :width] = mixed
    pair_ref[:, width:] = grad_pre


def term_kernel(peers, width, pairs_ref, term_ref):
    half = width // 2
    second_core = lax.axis_index("hist") % 2 == 1
    pairs = pairs_ref[...].reshape(-1, 2 * width)
    mixed = pairs[:, :width]
    left, right = pairs[:, width : width + half], pairs[:, width + half :]
    grad_pre = jnp.where(second_core, right, left)
    share = width // peers
    step = 8
    term = dot(mixed, grad_pre, COLS_T)
    for peer in range(peers):
        row = (peer + lead_of(peers)) % peers * share
        blocks = [term[row + i : row + i + step, :] for i in range(0, share, step)]
        term_ref[peer] = jnp.concatenate(blocks, axis=1).astype(BF16)


def backward_kernel(
    pair_ref,
    weight_ref,
    inside_ref,
    pick_in,
    history_in,
    send_ref,
    mixed_ref,
    out_ref,
    pick,
    aux,
    sems,
):
    node_rows, width = mixed_ref.shape
    peers = send_ref.shape[0]
    load_pick = pltpu.make_async_copy(pick_in, pick, sems.at[0])
    load_aux = pltpu.make_async_copy(history_in.at[:, width:], aux, sems.at[1])
    load_pick.start()
    load_aux.start()
    grad_mixed = dot(pair_ref[:, width:], weight_ref[...], ROWS_T).astype(BF16)
    mixed_ref[...] = grad_mixed
    slot_grad = dot(inside_ref[...], grad_mixed, COLS_T).astype(BF16)
    send_ref[:, :, :width] = slot_grad.reshape(peers, CAP, width)
    pre = dot(pair_ref[:, :width], weight_ref[...])
    out_ref[...] = (pre * sigmoid(pre)).astype(BF16)
    load_pick.wait()
    load_aux.wait()
    taken = dot(pick[:, node_rows:], aux[...]).astype(BF16)
    send_ref[:, :, width:] = taken.reshape(peers, CAP, width)


def weight_kernel(terms_ref, sum_ref):
    peers, step = terms_ref.shape[:2]
    for core in range(2):
        first = (core + lead_of(peers)) % 2
        total = terms_ref[first].astype(F32)
        for peer in range(first + 2, peers, 2):
            total = total + terms_ref[peer].astype(F32)
        total = total.astype(BF16)
        for plane in range(sum_ref.shape[0]):
            sum_ref[plane, core * step : (core + 1) * step, :] = total


def add_kernel(near_ref, sum_ref):
    sum_ref[...] = jnp.sum(near_ref[...].astype(F32), axis=0).astype(BF16)


def final_kernel(
    back_ref, pick_ref, all_ref, mixed_ref, far_ref, grad_ref, share_ref
):
    total = jnp.sum(far_ref[...].astype(F32), axis=0)
    share, width = share_ref.shape
    half = width // 2
    step = total.shape[0] // 2
    for i in range(share // step):
        for core in range(2):
            share_ref[i * step : (i + 1) * step, core * half : (core + 1) * half] = total[
                core * step : (core + 1) * step, i * half : (i + 1) * half
            ]
    peers = back_ref.shape[0]
    node_rows = mixed_ref.shape[0]
    slots = back_ref[:, :, :width].reshape(peers * CAP, width)
    aux = back_ref[:, :, width:].reshape(peers * CAP, width)
    returned = dot(pick_ref[:, :node_rows], slots, COLS_T)
    compensation = dot(all_ref[...], aux)
    grad = mixed_ref[...].astype(F32) + returned + compensation
    grad_ref[...] = grad.astype(BF16)


def call(kernel, out_shape, *args, smem=(), hbm=(), hbm_out=(), scratch=(), vmem=32, cost=None):
    spaces = [
        pltpu.SMEM if i in smem else pltpu.HBM if i in hbm else pltpu.VMEM
        for i in range(len(args))
    ]
    single = not isinstance(out_shape, (list, tuple))
    out_shape = [out_shape] if single else out_shape
    out_spaces = [pltpu.HBM if i in hbm_out else pltpu.VMEM for i in range(len(out_shape))]
    result = pl.pallas_call(
        kernel,
        out_shape=out_shape,
        in_specs=[pl.BlockSpec(memory_space=space) for space in spaces],
        out_specs=[pl.BlockSpec(memory_space=space) for space in out_spaces],
        scratch_shapes=list(scratch),
        compiler_params=pltpu.CompilerParams(vmem_limit_bytes=vmem << 20),
        cost_estimate=cost,
    )(*args)
    return result[0] if single else result


def swap(values, axis="hist", groups=None):
    if groups is None:
        peers = lax.axis_size(axis)
        groups = [[(i + lead_of(peers)) % peers for i in range(peers)]]
    return lax.all_to_all(
        values, axis, split_axis=0, concat_axis=0, tiled=True, axis_index_groups=groups
    )


def body(feats, history, weight, edge_coef, tile_map, nbr_owner, nbr_row, grad_out):
    peers = lax.axis_size("hist")
    planes = lax.axis_size("batch")
    node_rows, width = feats.shape[1:]
    table_rows = history.shape[0]
    slots = nbr_row.shape[1]
    assert 2 * slots // peers == CAP and planes == 16
    share = width // peers
    shape = jax.ShapeDtypeStruct
    owners = nbr_owner.reshape(1, slots)
    ids, placed = call(
        request_kernel,
        [shape((peers, 1, LANES), jnp.int32), shape((2, slots), jnp.int32)],
        tile_map,
        owners,
        nbr_row,
        hbm=(0, 1, 2),
        vmem=60,
        scratch=(
            pltpu.VMEM(tile_map.shape, jnp.int32),
            pltpu.VMEM(owners.shape, jnp.int32),
            pltpu.VMEM(nbr_row.shape, jnp.int32),
            pltpu.SemaphoreType.DMA((3,)),
        ),
    )
    received = swap(ids)
    coef, coef_inside = call(
        functools.partial(coef_kernel, node_rows),
        [shape((node_rows, peers * CAP), BF16)] * 2,
        placed,
        edge_coef[0],
        hbm=(0, 1),
        vmem=60,
        scratch=(
            pltpu.VMEM((2, slots), jnp.int32),
            pltpu.VMEM(edge_coef.shape[1:], BF16),
            pltpu.SemaphoreType.DMA((2,)),
        ),
    )
    table = node_rows + table_rows
    received, coef, coef_inside = lax.optimization_barrier((received, coef, coef_inside))
    taken, pick = call(
        gather_kernel,
        [shape((peers, CAP, width), BF16), shape((peers * CAP, table), BF16)],
        received,
        jnp.concatenate([feats[0], history[:, :width]], axis=0),
    )
    pulled = swap(taken)
    pair = call(
        forward_kernel,
        shape((node_rows, 2 * width), BF16),
        pulled,
        coef,
        feats[0],
        weight,
        grad_out[0],
    )
    chips = [[i + 1, i] for i in range(0, peers, 2)]
    pairs = lax.all_gather(pair, "hist", axis=0, axis_index_groups=chips)
    terms = call(
        functools.partial(term_kernel, peers, width),
        shape((peers, 8, share * width // 16), BF16),
        pairs,
    )
    pair, terms = lax.optimization_barrier((pair, terms))
    terms = swap(terms)
    sent, grad_mixed, out_rows = call(
        backward_kernel,
        [
            shape((peers, CAP, 2 * width), BF16),
            shape((node_rows, width), BF16),
            shape((node_rows, width), BF16),
        ],
        pair,
        weight,
        coef_inside,
        pick,
        history,
        hbm=(3, 4),
        scratch=(
            pltpu.VMEM((peers * CAP, table), BF16),
            pltpu.VMEM((table_rows, width), BF16),
            pltpu.SemaphoreType.DMA((2,)),
        ),
    )
    side = 4
    near = [[a * side + i for i in (2, 1, 3, 0)] for a in range(planes // side)]
    term = call(weight_kernel, shape((side, 16, share * width // 16), BF16), terms)
    term = swap(term, "batch", near)
    sent, term = lax.optimization_barrier((sent, term))
    back = swap(sent)
    term = call(add_kernel, shape(term.shape[1:], BF16), term)
    far = [[a + side * i for i in range(planes // side)] for a in range(side)]
    term = lax.all_gather(term, "batch", axis=0, axis_index_groups=far)
    grad_rows, weight_share = call(
        final_kernel,
        [shape((node_rows, width), BF16), shape((share, width), F32)],
        back,
        pick,
        coef,
        grad_mixed,
        term,
    )
    return (out_rows[None], grad_rows[None], weight_share)


def solution(mesh):
    return jax.shard_map(
        body,
        mesh=mesh,
        in_specs=(
            P(("batch", "hist"), None, None),
            P("hist", None),
            P(),
            P(("batch", "hist"), None, None),
            P(("batch", "hist"), None),
            P(("batch", "hist"), None, None),
            P(("batch", "hist"), None),
            P(("batch", "hist"), None, None),
        ),
        out_specs=(
            P(("batch", "hist"), None, None),
            P(("batch", "hist"), None, None),
            P("hist", None),
        ),
        check_vma=False,
    )
```
